256 devices in a mesh: ens: 2 (over z_hi), tile: 128 (over x, y, z_lo, core).
Axes of the slice: x: 4, y: 4, z: 8 (z_hi: 2, z_lo: 4; z = z_hi * 4 + z_lo), core: 2. Of those that a mesh axis runs over, the one named last changes fastest.
Arguments:
- fields: bfloat16 [2, 128, 64, 16, 128], P('ens', 'tile'), may hold values from -6 to 6
- cotangent: bfloat16 [2, 128, 64, 16, 128], P('ens', 'tile'), may hold values from -6 to 6
- kernel_first: bfloat16 [9, 64, 64], replicated, may hold values from -0.25 to 0.25
- kernel_second: bfloat16 [9, 128, 64], replicated, may hold values from -0.25 to 0.25
- kernel_third: bfloat16 [9, 128, 128], replicated, may hold values from -0.1875 to 0.1875
- closing_filter_weights: bfloat16 [9, 64, 192], replicated, may hold values from -0.15625 to 0.15625
- offset_first: float32 [64], replicated, may hold values from -3 to 3
- offset_second: float32 [128], replicated, may hold values from -3 to 3
- offset_third: float32 [128], replicated, may hold values from -3 to 3
- closing_shift_values: float32 [64], replicated, may hold values from -3 to 3
- codes: int32 [128, 4], P('tile'), may hold values from 0 to 3
- filter_stride_spread: int32 [4], replicated, may hold values from 1 to 4, as said below
Outputs:
- network_predicted_state: bfloat16 [2, 128, 64, 16, 128], P('ens', 'tile')
- state_input_derivative: float32 [2, 128, 64, 16, 128], P('ens', 'tile')
- initial_filter_derivative: float32 [9, 64, 64], replicated
- latter_filter_derivative: float32 [9, 128, 64], replicated
- penultimate_filter_derivative: float32 [9, 128, 128], replicated
- closing_filter_derivative: float32 [9, 64, 192], replicated
- initial_shift_derivative: float32 [64], replicated
- latter_shift_derivative: float32 [128], replicated
- penultimate_shift_derivative: float32 [128], replicated
- closing_shift_derivative: float32 [64], replicated
The draws below stay inside these ranges and needn't reach their ends.
Inputs may be any that keep to these rules, and one draw needn't show every extreme that they name: `codes`: bit 0 picks which of the two parallel edges of the sending tile is sent, bit 1 reverses it. `filter_stride_spread`: at least one layer has dilation 4 and one has dilation 1.
All inputs are finite; a program needn't handle non-finite values.
Results may differ from the reference program's by a relative error of at most 0.009.
Values may be sent and summed in bfloat16 or wider, within the bound.
A program may use at most 128 MiB of HBM per device.

```python
import math
import jax
import jax.numpy as jnp
from jax import lax

C0 = 64
C1 = 128
H = 16
W = 128
LAYERS = 4
DMAX = 4
TILE_ROW = 8
MEMBERS = 2
TILES = 128


def draw_filter_stride_spread(key, part):
    key = jax.random.fold_in(key, 7)
    first_key, second_key = jax.random.split(key)
    values = jax.random.randint(first_key, (LAYERS,), 1, DMAX + 1)
    order = jax.random.permutation(second_key, LAYERS)
    positions = jnp.arange(LAYERS)
    values = jnp.where(positions == order[0], DMAX, values)
    values = jnp.where(positions == order[1], 1, values)
    return values.astype(jnp.int32)


def touch_ends(drawn, stream_key, smallest, top_value):
    shape = drawn.shape
    index_at = [jax.random.randint(jax.random.fold_in(stream_key, axis), (), 0, shape[axis]) for axis in range(len(shape))]
    drawn = drawn.at[tuple(index_at)].set(smallest)
    longest = shape.index(max(shape))
    index_at[longest] = (index_at[longest] + 1) % shape[longest]
    return drawn.at[tuple(index_at)].set(top_value)


def block_scale(rng, shape, pieces, smallest, top_value):
    level = 1.0
    for dim, parts in pieces:
        steps = jax.random.uniform(jax.random.fold_in(jax.random.fold_in(rng, 6), dim), (parts,), jnp.float32, smallest / len(pieces), top_value / len(pieces))
        level = level * jnp.repeat(jnp.exp(steps), shape[dim] // parts).reshape((-1,) + (1,) * (len(shape) - 1 - dim))
    return level


def normal_values(own_key, shape, spread, reach, pieces=(), kind=jnp.bfloat16):
    result = jax.random.normal(own_key, shape, jnp.float32) * spread
    if len(pieces) > 0:
        result = block_scale(own_key, shape, pieces, -0.22, 0.18) * result
    return jnp.clip(result, min=-reach, max=reach).astype(kind)


def setup_inputs(seed: int = 0) -> dict:
    key_list = jax.random.split(jax.random.key(seed), 13)
    return {
        "fields": normal_values(key_list[0], (MEMBERS, TILES, C0, H, W), 1.0, 6.0, ((0, 2), (1, 128))),
        "cotangent": normal_values(key_list[1], (MEMBERS, TILES, C0, H, W), 1.0, 6.0, ((0, 2), (1, 128))),
        "kernel_first": normal_values(key_list[2], (9, C0, C0), (9 * C0) ** -0.5, 0.25),
        "kernel_second": normal_values(key_list[3], (9, C1, C0), (9 * C0) ** -0.5, 0.25),
        "kernel_third": normal_values(key_list[4], (9, C1, C1), (9 * C1) ** -0.5, 0.1875),
        "closing_filter_weights": normal_values(key_list[5], (9, C0, C0 + C1), (9 * (C0 + C1)) ** -0.5, 0.15625),
        "offset_first": normal_values(key_list[6], (C0,), 0.5, 3.0, (), jnp.float32),
        "offset_second": normal_values(key_list[7], (C1,), 0.5, 3.0, (), jnp.float32),
        "offset_third": normal_values(key_list[8], (C1,), 0.5, 3.0, (), jnp.float32),
        "closing_shift_values": normal_values(key_list[9], (C0,), 0.5, 3.0, (), jnp.float32),
        "codes": touch_ends(jax.random.randint(key_list[10], (TILES, 4), 0, 4), jax.random.fold_in(key_list[10], 1), 0, 3).astype(jnp.int32),
        "filter_stride_spread": draw_filter_stride_spread(jax.random.fold_in(key_list[12], 71), 0),
    }


def exact_gelu(values):
    return jax.nn.gelu(values, approximate=False)

def gelu_slope(values):
    return jax.vjp(exact_gelu, values)[1](jnp.ones_like(values))[0]

def edge_columns(values, flag, margin):
    extent = values.shape[-1]
    picked = jnp.where(flag % 2 == 1, values[..., extent - margin:], values[..., :margin])
    return jnp.where(flag // 2 == 1, jnp.flip(picked, -2), picked)

def edge_rows(values, flag, margin):
    extent = values.shape[-2]
    picked = jnp.where(flag % 2 == 1, values[..., extent - margin:, :], values[..., :margin, :])
    return jnp.where(flag // 2 == 1, jnp.flip(picked, -1), picked)

def return_columns(summed, incoming, flag, margin):
    extent = summed.shape[-1]
    unflipped = jnp.where(flag // 2 == 1, jnp.flip(incoming, -2), incoming)
    nothing = jnp.zeros_like(unflipped)
    summed = summed.at[..., :margin].add(jnp.where(flag % 2 == 0, unflipped, nothing))
    return summed.at[..., extent - margin:].add(jnp.where(flag % 2 == 1, unflipped, nothing))

def return_rows(summed, incoming, flag, margin):
    extent = summed.shape[-2]
    unflipped = jnp.where(flag // 2 == 1, jnp.flip(incoming, -1), incoming)
    nothing = jnp.zeros_like(unflipped)
    summed = summed.at[..., :margin, :].add(jnp.where(flag % 2 == 0, unflipped, nothing))
    return summed.at[..., extent - margin:, :].add(jnp.where(flag % 2 == 1, unflipped, nothing))

def surround(values, codes, margin):
    column_fn = jax.vmap(edge_columns, in_axes=(0, 0, None))
    row_fn = jax.vmap(edge_rows, in_axes=(0, 0, None))
    toward_right = column_fn(values, codes[:, 3], margin)
    toward_left = column_fn(values, codes[:, 2], margin)
    leftward = jnp.roll(toward_right, 1, axis=0)
    rightward = jnp.roll(toward_left, -1, axis=0)
    widened = jnp.concatenate([leftward, values, rightward], axis=-1)
    toward_lower = row_fn(widened, codes[:, 1], margin)
    toward_upper = row_fn(widened, codes[:, 0], margin)
    upper_rim = jnp.roll(toward_lower, TILE_ROW, axis=0)
    lower_rim = jnp.roll(toward_upper, -TILE_ROW, axis=0)
    return jnp.concatenate([upper_rim, widened, lower_rim], axis=-2)

def fold_rims(padded, codes, margin):
    rows_all = padded.shape[-2]
    upper = padded[..., :margin, :]
    lower = padded[..., rows_all - margin:, :]
    inner = padded[..., margin:rows_all - margin, :]
    from_upper = jnp.roll(upper, -TILE_ROW, axis=0)
    from_lower = jnp.roll(lower, TILE_ROW, axis=0)
    rows_back = jax.vmap(return_rows, in_axes=(0, 0, 0, None))
    cols_back = jax.vmap(return_columns, in_axes=(0, 0, 0, None))
    inner = rows_back(inner, from_lower, codes[:, 0], margin)
    inner = rows_back(inner, from_upper, codes[:, 1], margin)
    cols_all = inner.shape[-1]
    left_part = inner[..., :margin]
    right_part = inner[..., cols_all - margin:]
    core = inner[..., margin:cols_all - margin]
    back_left = jnp.roll(left_part, -1, axis=0)
    back_right = jnp.roll(right_part, 1, axis=0)
    core = cols_back(core, back_right, codes[:, 2], margin)
    return cols_back(core, back_left, codes[:, 3], margin)

def product(first, second, form):
    return jnp.einsum(form, first.astype(jnp.float32), second.astype(jnp.float32), precision=lax.Precision.HIGHEST)

def start_of(row_tap, col_tap, spacing, border):
    zero = jnp.int32(0)
    return (zero, zero, border + (row_tap - 1) * spacing, border + (col_tap - 1) * spacing)

def convolve(padded, kernel, spacing, border):
    members, channels, rows_pad, cols_pad = padded.shape
    rows, cols = (rows_pad - 2 * border, cols_pad - 2 * border)
    summed = jnp.zeros((members, kernel.shape[1], rows, cols), jnp.float32)
    for row_tap in range(3):
        for col_tap in range(3):
            section = lax.dynamic_slice(padded, start_of(row_tap, col_tap, spacing, border), (members, channels, rows, cols))
            summed = summed + product(kernel[3 * row_tap + col_tap], section, 'oc,mchw->mohw')
    return summed

def kernel_terms(padded, grad, spacing, border):
    members, channels, rows_pad, cols_pad = padded.shape
    rows, cols = (rows_pad - 2 * border, cols_pad - 2 * border)
    listed = []
    for row_tap in range(3):
        for col_tap in range(3):
            section = lax.dynamic_slice(padded, start_of(row_tap, col_tap, spacing, border), (members, channels, rows, cols))
            listed.append(product(grad, section, 'mohw,mchw->oc'))
    return jnp.stack(listed)

def spread_back(grad, kernel, spacing, border):
    members, outs_count, rows, cols = grad.shape
    channels = kernel.shape[2]
    summed = jnp.zeros((members, channels, rows + 2 * border, cols + 2 * border), jnp.float32)
    for row_tap in range(3):
        for col_tap in range(3):
            begin = start_of(row_tap, col_tap, spacing, border)
            current = lax.dynamic_slice(summed, begin, (members, channels, rows, cols))
            summed = lax.dynamic_update_slice(summed, current + product(kernel[3 * row_tap + col_tap], grad, 'oc,mohw->mchw'), begin)
    return summed

def coarsen(values):
    lead = values.shape[:-2]
    rows, cols = (values.shape[-2], values.shape[-1])
    blocks = values.astype(jnp.float32).reshape(lead + (rows // 2, 2, cols // 2, 2))
    return lax.optimization_barrier(jnp.mean(blocks, axis=(-3, -1))).astype(jnp.bfloat16)

def refine(values):
    return jnp.repeat(jnp.repeat(values, 2, axis=-2), 2, axis=-1)

def collapse(values):
    lead = values.shape[:-2]
    rows, cols = (values.shape[-2], values.shape[-1])
    return lax.optimization_barrier(jnp.sum(values.reshape(lead + (rows // 2, 2, cols // 2, 2)), axis=(-3, -1)))

def reference(fields, cotangent, kernel_first, kernel_second, kernel_third, closing_filter_weights, offset_first, offset_second, offset_third, closing_shift_values, codes, filter_stride_spread):
    border = DMAX

    def apply_filters_throughout(padded, kernel, spacing):
        return lax.map(lambda single: convolve(single, kernel, spacing, border), padded)

    def terms_all(padded, grad, spacing):
        return lax.optimization_barrier(jnp.sum(lax.map(lambda pair: kernel_terms(pair[0], pair[1], spacing, border), (padded, grad)), axis=0))

    def back_all(grad, kernel, spacing):
        return fold_rims(lax.map(lambda single: spread_back(single, kernel, spacing, border), grad), codes, border)
    start_fields = jnp.swapaxes(fields, 0, 1)
    upstream = jnp.swapaxes(cotangent, 0, 1)
    first_pad = surround(start_fields, codes, border)
    first_pre = apply_filters_throughout(first_pad, kernel_first, filter_stride_spread[0]) + offset_first[:, None, None]
    first_act = exact_gelu(first_pre).astype(jnp.bfloat16)
    pooled = coarsen(first_act)
    second_pad = surround(pooled, codes, border)
    second_pre = apply_filters_throughout(second_pad, kernel_second, filter_stride_spread[1]) + offset_second[:, None, None]
    second_act = exact_gelu(second_pre).astype(jnp.bfloat16)
    third_pad = surround(second_act, codes, border)
    third_pre = apply_filters_throughout(third_pad, kernel_third, filter_stride_spread[2]) + offset_third[:, None, None]
    third_act = exact_gelu(third_pre).astype(jnp.bfloat16)
    joined = jnp.concatenate([refine(third_act), first_act], axis=-3)
    merged_halo_margin = surround(joined, codes, border)
    network_predicted_state = (apply_filters_throughout(merged_halo_margin, closing_filter_weights, filter_stride_spread[3]) + closing_shift_values[:, None, None]).astype(jnp.bfloat16)
    coarse_count = kernel_third.shape[1]
    joined_grad = back_all(upstream, closing_filter_weights, filter_stride_spread[3])
    third_delta = (collapse(joined_grad[..., :coarse_count, :, :]) * gelu_slope(third_pre)).astype(jnp.bfloat16)
    second_delta = (back_all(third_delta, kernel_third, filter_stride_spread[2]) * gelu_slope(second_pre)).astype(jnp.bfloat16)
    pooled_grad = back_all(second_delta, kernel_second, filter_stride_spread[1])
    first_grad = joined_grad[..., coarse_count:, :, :] + 0.25 * refine(pooled_grad)
    first_delta = (first_grad * gelu_slope(first_pre)).astype(jnp.bfloat16)
    state_input_derivative = back_all(first_delta, kernel_first, filter_stride_spread[0])
    scale = jnp.float32(1.0 / math.sqrt(MEMBERS * TILES * H * W))
    closing_filter_derivative = terms_all(merged_halo_margin, upstream, filter_stride_spread[3]) * scale
    penultimate_filter_derivative = terms_all(third_pad, third_delta, filter_stride_spread[2]) * scale
    latter_filter_derivative = terms_all(second_pad, second_delta, filter_stride_spread[1]) * scale
    initial_filter_derivative = terms_all(first_pad, first_delta, filter_stride_spread[0]) * scale
    axes_sum = (0, 1, 3, 4)
    initial_shift_derivative = lax.optimization_barrier(jnp.sum(first_delta.astype(jnp.float32), axis=axes_sum)) * scale
    latter_shift_derivative = lax.optimization_barrier(jnp.sum(second_delta.astype(jnp.float32), axis=axes_sum)) * scale
    penultimate_shift_derivative = lax.optimization_barrier(jnp.sum(third_delta.astype(jnp.float32), axis=axes_sum)) * scale
    closing_shift_derivative = lax.optimization_barrier(jnp.sum(upstream.astype(jnp.float32), axis=axes_sum)) * scale
    return (jnp.swapaxes(network_predicted_state, 0, 1), jnp.swapaxes(state_input_derivative, 0, 1), initial_filter_derivative, latter_filter_derivative, penultimate_filter_derivative, closing_filter_derivative, initial_shift_derivative, latter_shift_derivative, penultimate_shift_derivative, closing_shift_derivative)
```

```python
import functools
import math

import jax
import jax.numpy as jnp
from jax import lax
from jax.experimental import pallas as pl
from jax.experimental.pallas import tpu as pltpu
from jax.sharding import PartitionSpec as P

MESH = pl.DeviceIdType.MESH
BF = jnp.bfloat16
F32 = jnp.float32

RIM = 4
TILE_ROW = 8
LANES = 128
ONES = 16

EXCHANGES = (
    ("fields", 64, 4, 1),
    ("pooled", 64, 4, 1),
    ("first", 64, 4, 1),
    ("second", 128, 4, 1),
    ("third", 128, 2, 1),
    ("b4c", 128, 2, 3),
    ("b4f", 64, 4, 3),
    ("b3", 128, 4, 3),
    ("b2", 64, 4, 3),
    ("b1", 64, 4, 3),
)
OFFSETS = (1, -1, 9, 7, -7, -9, 8, -8)
LAYERS = ((64, 64, 16, 128), (64, 128, 8, 64), (128, 128, 8, 64), (192, 64, 16, 128))


def iota(shape, dim):
    return lax.broadcasted_iota(jnp.int32, shape, dim)


def onehot(cond):
    return jnp.where(cond, 1.0, 0.0).astype(BF)


def mm(a, b):
    return jnp.dot(a, b, preferred_element_type=F32)


def mm_nt(a, b):
    return lax.dot_general(a, b, (((1,), (1,)), ((), ())), preferred_element_type=F32)


def split(values):
    high = values.astype(BF)
    low = (values - high.astype(F32)).astype(BF)
    return jnp.concatenate([high, low], axis=-1)


def cat(parts, axis):
    return parts[0] if len(parts) == 1 else jnp.concatenate(parts, axis=axis)


def log2(m):
    return m.bit_length() - 1


def column_pick(H, W, m, code_right, code_left, shape=(LANES, LANES)):
    lane = iota(shape, 1)
    code = jnp.where(lane < 64, code_right, code_left)
    idx = lane & 63
    row, col = idx >> log2(m), idx & (m - 1)
    col = jnp.where((code & 1) == 1, W - m + col, col)
    row = jnp.where((code >> 1) == 1, H - 1 - row, row)
    valid = idx < H * m
    return jnp.where(valid, row, -1), jnp.where(valid, col, -1)


def halo_target(H, m, code, row):
    w = iota((LANES, LANES), 1)
    picked = jnp.where((code & 1) == 1, H - m + row, row)
    flip = (code >> 1) == 1
    k = w - (LANES - m)
    left = jnp.where(flip, 64 + m * picked + (m - 1 - k), m * picked + k)
    right = jnp.where(flip, m * picked + (m - 1 - w), 64 + m * picked + w)
    return jnp.where(w >= LANES - m, left, jnp.where(w < m, right, -1))


def shift_matrix(W, d):
    source = iota((2 * LANES, 2 * LANES), 0)
    out = iota((2 * LANES, 2 * LANES), 1)
    j = out & (LANES - 1)
    minus = jnp.where(j >= d, j - d, 2 * LANES + j - d)
    plus = jnp.where(j + d < W, j + d, LANES + j + d - W)
    return onehot((source == jnp.where(out < LANES, minus, plus)) & (j < W))


def reversal(W, code, shape=(LANES, LANES)):
    u, w = iota(shape, 0), iota(shape, 1)
    flip = (code >> 1) == 1
    return (u == jnp.where(flip, W - 1 - w, w)) & (w < W)


def pick_rows_matrix(W, code):
    u = iota((2 * LANES, LANES), 0)
    w = iota((2 * LANES, LANES), 1)
    flip = (code >> 1) == 1
    hit = (u & (LANES - 1)) == jnp.where(flip, W - 1 - w, w)
    return onehot(hit & ((u >> 7) == (code & 1)) & (w < W))


def return_rows_matrix(W, code_upper, code_lower, last):
    u = iota((2 * LANES, LANES), 0)
    w = iota((2 * LANES, LANES), 1)
    code = jnp.where(u < LANES, code_upper, code_lower)
    flip = (code >> 1) == 1
    hit = (u & (LANES - 1)) == jnp.where(flip, W - 1 - w, w)
    return onehot(hit & ((code & 1) == last) & (w < W))


def rim_matrix(H, m, code_above, code_below, collapse):
    shape = (2 * LANES, LANES)
    u, lane = iota(shape, 0), iota(shape, 1)
    src = u & (LANES - 1)
    if collapse:
        src = ((src >> 3) << 1) + ((src & 3) >> 1)
    src = src + (u >> 7) * 1024
    idx = lane & 63
    row, k = idx >> log2(m), idx & (m - 1)
    leftward = lane < 64
    valid = idx < H * m
    parts = [onehot((src == (row + m) * m + k + jnp.where(leftward, 1024, 0)) & valid)]
    for code, base in ((code_above, 0), (code_below, H + m)):
        picked = jnp.where((code & 1) == 1, row - (H - m), row)
        flip = jnp.where((code >> 1) == 1, 1, 0)
        kk = jnp.where(flip == 1, m - 1 - k, k)
        left_side = jnp.where(leftward, 1 - flip, flip)
        hit = src == (picked + base) * m + kk + left_side * 1024
        parts.append(onehot(hit & valid & (picked >= 0) & (picked < m)))
    return jnp.concatenate(parts, axis=1)


def edge_matrix(H, d):
    u, v = iota((LANES, LANES), 0), iota((LANES, LANES), 1)
    row, k = v >> 2, v & 3
    parts = []
    for a in range(3):
        h = row - RIM - (a - 1) * d
        inside = (h >= 0) & (h < H)
        parts.append(onehot((u == 4 * h + (4 - d + k)) & inside & (k < d)))
        parts.append(onehot((u == 64 + 4 * h + (k - 4 + d)) & inside & (k >= 4 - d)))
    return jnp.concatenate(parts, axis=1)


def gelu_and_slope(x):
    cdf = 0.5 + 0.5 * lax.erf(x * math.sqrt(0.5))
    pdf = jnp.exp(-0.5 * x * x) * (1.0 / math.sqrt(2.0 * math.pi))
    return x * cdf, cdf + x * pdf


def stacked(values):
    return values.reshape(values.shape[0] * values.shape[1], values.shape[2])


def net_kernel(tiles, names, *refs):
    R = dict(zip(names, refs))
    tile = lax.axis_index("tile")
    ens = lax.axis_index("ens")

    def device(offset):
        return (ens, lax.rem(tile + (offset + tiles), tiles))

    copies = {}
    for x, (name, C, m, sent) in enumerate(EXCHANGES):
        listed = []
        for slot, offset in enumerate(OFFSETS):
            if slot < 6:
                which = 0 if sent == 1 else (0, 0, 2, 2, 1, 1)[slot]
                src = R["cs_" + name].at[which]
                dst = R["cr_" + name].at[slot]
            else:
                src = R["rs_" + name].at[slot - 6]
                dst = R["rr_" + name].at[slot - 6]
            listed.append(
                pltpu.make_async_remote_copy(
                    src_ref=src,
                    dst_ref=dst,
                    send_sem=R["send"].at[x, slot],
                    recv_sem=R["recv"].at[x, slot],
                    device_id=device(offset),
                    device_id_type=MESH,
                )
            )
        copies[name] = listed
    copies["codes"] = [
        pltpu.make_async_remote_copy(
            src_ref=R["code_rows"],
            dst_ref=R["code_near"].at[k],
            send_sem=R["send_code"].at[k],
            recv_sem=R["recv_code"].at[k],
            device_id=device(offset),
            device_id_type=MESH,
        )
        for k, offset in enumerate((8, -8))
    ]

    def start(name):
        for copy in copies[name]:
            copy.start()

    def arrive(name):
        for copy in copies[name]:
            copy.wait_recv()

    barrier = pltpu.get_barrier_semaphore()
    for offset in OFFSETS:
        pl.semaphore_signal(barrier, inc=1, device_id=device(offset), device_id_type=MESH)

    codes = [R["codes"][s] for s in range(4)]
    dil = [R["dil"][i] for i in range(4)]

    shifts = R["shifts"]
    for i, (_, _, _, W) in enumerate(LAYERS):
        shifts[i] = shift_matrix(W, dil[i])
    picks = R["picks"]
    PICK = {(16, 4): 0, (8, 4): 1, (8, 2): 2}
    for (H, m), where in PICK.items():
        _, col = column_pick(H, 128 if H == 16 else 64, m, codes[3], codes[2])
        picks[where] = onehot(iota((LANES, LANES), 0) == col)

    def pick_rows(H, m):
        row, _ = column_pick(H, 128 if H == 16 else 64, m, codes[3], codes[2], (1, LANES))
        return row

    for name, O, H in (("d4", 64, 16), ("d1", 64, 16), ("d3", 128, 8), ("d2", 128, 8)):
        R[name][0 : 2 * RIM] = jnp.zeros((2 * RIM, 3 * O, LANES), BF)
        R[name][2 * RIM + H : 4 * RIM + H] = jnp.zeros((2 * RIM, 3 * O, LANES), BF)
    for name, C, H in (("x4", 192, 16), ("x1", 64, 16), ("x3", 128, 8), ("x2", 64, 8)):
        R[name][:, 3 * C : 3 * C + ONES, :] = jnp.ones((H + 2 * RIM, ONES, LANES), BF)

    def columns_of(x_ref, H, m, C):
        row = pick_rows(H, m)
        total = jnp.zeros((C, LANES), F32)
        for g in range(H // 4):
            y = mm(stacked(x_ref[4 * g : 4 * g + 4]), picks[PICK[(H, m)]])
            for q in range(4):
                total = total + jnp.where(row == 4 * g + q, y[q * C : (q + 1) * C], 0.0)
        return total

    def send_forward(name, x_ref, H, W, m, C):
        R["cs_" + name][0] = columns_of(x_ref, H, m, C).astype(BF)
        both = jnp.concatenate([stacked(x_ref[0:m]), stacked(x_ref[H - m : H])], axis=1)
        for k, side in enumerate((1, 0)):
            rows = mm(both, pick_rows_matrix(W, codes[side])).astype(BF)
            R["rs_" + name][k] = rows.reshape(m, C, LANES)

    def halo_arrays(name):
        near = R["cr_" + name]
        low = iota((1, LANES), 1) < 64
        return [jnp.where(low, near[2 * i], near[2 * i + 1]) for i in range(3)]

    def halo_rows(Z, H, m, code, rows):
        lane = iota((LANES, LANES), 0)
        mats = cat([onehot(lane == halo_target(H, m, code, r)) for r in rows], 1)
        y = mm(Z, mats).astype(BF)
        return cat([y[:, LANES * q : LANES * (q + 1)] for q in range(len(rows))], 0)

    def fill(X3, r0, core, halo, C, S, offs, repeat):
        y = mm(jnp.concatenate([core, halo], axis=1), S).astype(BF)
        for q in range(core.shape[0] // C):
            part = slice(q * C, (q + 1) * C)
            for z in range(repeat):
                r = r0 + q * repeat + z
                X3[r, offs[0] : offs[0] + C, :] = y[part, :LANES]
                X3[r, offs[1] : offs[1] + C, :] = core[part]
                X3[r, offs[2] : offs[2] + C, :] = y[part, LANES:]

    def pad_and_shift(name, x_ref, H, m, C, layer, X3, offs, refine):
        Z, Zu, Zl = halo_arrays(name)
        S = shifts[layer]
        rr = R["rr_" + name]
        code_u = R["code_near"][0, 1:2, :]
        code_l = R["code_near"][1, 0:1, :]
        rep = 2 if refine else 1

        def prepare(core, halo):
            if not refine:
                return core, halo
            u, w = iota((LANES, LANES), 0), iota((LANES, LANES), 1)
            core = mm(core, onehot(u == (w >> 1))).astype(BF)
            near = jnp.where(w < 4, w >> 1, jnp.where(w >= LANES - 4, 64 + (w >> 1), -1))
            return core, mm(halo, onehot(u == near)).astype(BF)

        def body(g, carry):
            rows = [m * g + q for q in range(m)]
            core, halo = prepare(stacked(x_ref[pl.ds(m * g, m)]), halo_rows(Z, H, m, 0, rows))
            fill(X3, RIM + m * rep * g, core, halo, C, S, offs, rep)
            return carry

        lax.fori_loop(0, H // m, body, 0)
        core, halo = prepare(stacked(rr[0]), halo_rows(Zu, H, m, code_u, range(m)))
        fill(X3, 0, core, halo, C, S, offs, rep)
        core, halo = prepare(stacked(rr[1]), halo_rows(Zl, H, m, code_l, range(m)))
        fill(X3, RIM + H * rep, core, halo, C, S, offs, rep)

    def conv(Z3, width, K, d, rows, write):
        def body(i, carry):
            r = 2 * i
            taps = []
            for b in range(3):
                base = r + RIM + (b - 1) * d
                taps.append(
                    jnp.concatenate(
                        [Z3[base, 0:width, :], Z3[base + 1, 0:width, :]], axis=1
                    )
                )
            y = mm(K[...], jnp.concatenate(taps, axis=0))
            write(r, y[:, :LANES])
            write(r + 1, y[:, LANES:])
            return carry

        lax.fori_loop(0, rows // 2, body, 0)

    def weight_terms(X3, C, D3, O, d, rows, acc):
        n = 3 * C + ONES

        def body(i, carry):
            r = 4 * i
            lhs = jnp.concatenate([X3[r + q] for q in range(4)], axis=1)
            taps = []
            for a in range(3):
                base = r + RIM - (a - 1) * d
                taps.append(
                    jnp.concatenate([D3[base + q, O : 2 * O, :] for q in range(4)], axis=1)
                )
            if O == 64:
                taps.append(jnp.zeros((O, 4 * LANES), BF))
            y = mm_nt(lhs, jnp.concatenate(taps, axis=0))
            acc[0:n] = acc[0:n] + y
            return carry

        acc[0:n] = jnp.zeros((n, acc.shape[1]), F32)
        lax.fori_loop(0, rows // 4, body, 0)

    def spread_delta(x_ref, H, O, layer, D3):
        def body(g, carry):
            core = stacked(x_ref[pl.ds(4 * g, 4)])
            y = mm(core, shifts[layer, 0:LANES, :]).astype(BF)
            for q in range(4):
                part = slice(q * O, (q + 1) * O)
                D3[2 * RIM + 4 * g + q, 0:O, :] = y[part, :LANES]
                D3[2 * RIM + 4 * g + q, O : 2 * O, :] = core[part]
                D3[2 * RIM + 4 * g + q, 2 * O : 3 * O, :] = y[part, LANES:]
            return carry

        lax.fori_loop(0, H // 4, body, 0)

    def rims_of(x_ref, H, W, O, layer, K):
        row, col = column_pick(H, W, RIM, 1, 0, (1, LANES))
        _, col_full = column_pick(H, W, RIM, 1, 0)
        pick = onehot(iota((LANES, LANES), 0) == col_full)
        edges = jnp.zeros((O, LANES), F32)
        for g in range(H // 4):
            y = mm(stacked(x_ref[4 * g : 4 * g + 4]), pick)
            for q in range(4):
                edges = edges + jnp.where(row == 4 * g + q, y[q * O : (q + 1) * O], 0.0)
        e = mm(edges.astype(BF), edge_matrix(H, dil[layer])).astype(BF)
        none = jnp.zeros((O, LANES), BF)
        blocks = []
        for b in range(3):
            a = 2 - b
            right = e[:, 2 * a * LANES : (2 * a + 1) * LANES]
            left = e[:, (2 * a + 1) * LANES : (2 * a + 2) * LANES]
            blocks.append(jnp.concatenate([right, none], axis=1))
            blocks.append(jnp.zeros((O, 2 * LANES), BF))
            blocks.append(jnp.concatenate([none, left], axis=1))
        return mm(K[...], jnp.concatenate(blocks, axis=0)).astype(BF)

    def send_backward(name, rims, G, c0, C, H, m, collapse=False):
        code_u = R["code_near"][0, 1:2, :]
        code_l = R["code_near"][1, 0:1, :]
        y = mm(rims, rim_matrix(H, m, code_u, code_l, collapse)).astype(BF)
        for k in range(3):
            R["cs_" + name][k] = y[:, k * LANES : (k + 1) * LANES]
        R["rs_" + name][0] = G[H + m : H + 2 * m, c0 : c0 + C, :].astype(BF)
        R["rs_" + name][1] = G[0:m, c0 : c0 + C, :].astype(BF)

    def fold(name, G, c0, C, H, W, m, write):
        near = R["cr_" + name]
        rr = R["rr_" + name]
        low = iota((1, LANES), 1) < 64
        back = jnp.where(
            low,
            near[1].astype(F32) + near[3].astype(F32) + near[5].astype(F32),
            near[0].astype(F32) + near[2].astype(F32) + near[4].astype(F32),
        )
        row = pick_rows(H, m)
        both = jnp.concatenate([stacked(rr[0]), stacked(rr[1])], axis=1)
        first = mm(both, return_rows_matrix(W, codes[0], codes[1], 0))
        last = mm(both, return_rows_matrix(W, codes[0], codes[1], 1))
        pick = picks[PICK[(H, m)]]
        for g in range(H // m):
            masked = [jnp.where(row == m * g + q, back, 0.0).astype(BF) for q in range(m)]
            y = mm_nt(cat(masked, 0), pick)
            if g == 0:
                y = y + first
            if g == H // m - 1:
                y = y + last
            for q in range(m):
                h = m * g + q
                write(h, G[h + m, c0 : c0 + C, :] + y[q * C : (q + 1) * C])

    send_forward("fields", R["fields"], 16, 128, 4, 64)
    pl.semaphore_wait(barrier, len(OFFSETS))
    start("codes")
    start("fields")

    cot = R["cot"]
    spread_delta(cot, 16, 64, 3, R["d4"])
    G4 = R["g4"]

    def write_g4(r, v):
        G4[r] = v

    conv(R["d4"], 192, R["kt4"], dil[3], 24, write_g4)
    rims4 = rims_of(cot, 16, 128, 64, 3, R["kt4"])
    arrive("codes")
    G4c = R["g4c"]
    u, w = iota((2 * LANES, LANES), 0), iota((2 * LANES, LANES), 1)
    pool = onehot(((u & (LANES - 1)) >> 1) == w)
    for g in range(3):
        pairs = [G4[8 * g + 2 * q, 0:128, :] + G4[8 * g + 2 * q + 1, 0:128, :] for q in range(4)]
        y = mm(split(cat(pairs, 0)), pool)
        G4c[4 * g : 4 * g + 4] = y.reshape(4, 128, LANES)
    send_backward("b4c", rims4[0:128], G4c, 0, 128, 8, 2, True)
    start("b4c")
    send_backward("b4f", rims4[128:192], G4, 128, 64, 16, 4)
    start("b4f")

    arrive("fields")
    pad_and_shift("fields", R["fields"], 16, 4, 64, 0, R["x1"], (0, 64, 128), False)
    first_act, slope1 = R["first_act"], R["slope1"]

    def write_first(r, v):
        act, slope = gelu_and_slope(v + R["off1"][...])
        first_act[r] = act.astype(BF)
        slope1[r] = slope

    conv(R["x1"], 192, R["kf1"], dil[0], 16, write_first)
    pooled = R["pooled"]
    quarter = jnp.where(((u & (LANES - 1)) >> 1) == w, 0.25, 0.0).astype(BF)
    for g in range(2):
        lhs = cat(
            [
                jnp.concatenate([first_act[8 * g + 2 * q], first_act[8 * g + 2 * q + 1]], axis=1)
                for q in range(4)
            ],
            0,
        )
        pooled[4 * g : 4 * g + 4] = mm(lhs, quarter).astype(BF).reshape(4, 64, LANES)
    send_forward("pooled", pooled, 8, 64, 4, 64)
    start("pooled")
    send_forward("first", first_act, 16, 128, 4, 64)
    start("first")

    arrive("b4c")
    arrive("b4f")
    coarse, skip = R["coarse"], R["skip"]

    def write_coarse(r, v):
        coarse[r] = v

    def write_skip(r, v):
        skip[r] = v

    fold("b4c", G4c, 0, 128, 8, 64, 2, write_coarse)
    fold("b4f", G4, 128, 64, 16, 128, 4, write_skip)

    arrive("pooled")
    pad_and_shift("pooled", pooled, 8, 4, 64, 1, R["x2"], (0, 64, 128), False)
    second_act, slope2 = R["second_act"], R["slope2"]
    inside = iota((1, LANES), 1) < 64

    def write_second(r, v):
        act, slope = gelu_and_slope(v + R["off2"][...])
        second_act[r] = jnp.where(inside, act, 0.0).astype(BF)
        slope2[r] = jnp.where(inside, slope, 0.0)

    conv(R["x2"], 192, R["kf2"], dil[1], 8, write_second)
    send_forward("second", second_act, 8, 64, 4, 128)
    start("second")

    arrive("first")
    pad_and_shift("first", first_act, 16, 4, 64, 3, R["x4"], (128, 320, 512), False)

    arrive("second")
    pad_and_shift("second", second_act, 8, 4, 128, 2, R["x3"], (0, 128, 256), False)
    third_act, delta3 = R["third_act"], R["delta3"]

    def write_third(r, v):
        act, slope = gelu_and_slope(v + R["off3"][...])
        third_act[r] = jnp.where(inside, act, 0.0).astype(BF)
        delta3[r] = jnp.where(inside, coarse[r] * slope, 0.0).astype(BF)

    conv(R["x3"], 384, R["kf3"], dil[2], 8, write_third)
    send_forward("third", third_act, 8, 64, 2, 128)
    start("third")
    spread_delta(delta3, 8, 128, 2, R["d3"])
    G3 = R["g3"]

    def write_g3(r, v):
        G3[r] = v

    conv(R["d3"], 384, R["kt3"], dil[2], 16, write_g3)
    send_backward("b3", rims_of(delta3, 8, 64, 128, 2, R["kt3"]), G3, 0, 128, 8, 4)
    start("b3")

    weight_terms(R["x3"], 128, R["d3"], 128, dil[2], 16, R["w3"])
    arrive("third")
    pad_and_shift("third", third_act, 8, 2, 128, 3, R["x4"], (0, 192, 384), True)

    arrive("b3")
    delta2 = R["delta2"]

    def write_delta2(r, v):
        delta2[r] = (v * slope2[r]).astype(BF)

    fold("b3", G3, 0, 128, 8, 64, 4, write_delta2)
    spread_delta(delta2, 8, 128, 1, R["d2"])
    G2 = R["g2"]

    def write_g2(r, v):
        G2[r] = v

    conv(R["d2"], 384, R["kt2"], dil[1], 16, write_g2)
    send_backward("b2", rims_of(delta2, 8, 64, 128, 1, R["kt2"]), G2, 0, 64, 8, 4)
    start("b2")

    state = R["state"]

    def write_state(r, v):
        state[r] = (v + R["off4"][...]).astype(BF)

    conv(R["x4"], 576, R["kf4"], dil[3], 16, write_state)
    weight_terms(R["x2"], 64, R["d2"], 128, dil[1], 16, R["w2"])

    arrive("b2")
    delta1 = R["delta1"]
    repeat = jnp.where((u & (LANES - 1)) == (w >> 1), 0.25, 0.0).astype(BF)

    def write_delta1(r, v):
        wide = mm(split(v), repeat)
        for z in range(2):
            delta1[2 * r + z] = ((skip[2 * r + z] + wide) * slope1[2 * r + z]).astype(BF)

    fold("b2", G2, 0, 64, 8, 64, 4, write_delta1)
    spread_delta(delta1, 16, 64, 0, R["d1"])
    G1 = R["g1"]

    def write_g1(r, v):
        G1[r] = v

    conv(R["d1"], 192, R["kt1"], dil[0], 24, write_g1)
    send_backward("b1", rims_of(delta1, 16, 128, 64, 0, R["kt1"]), G1, 0, 64, 16, 4)
    start("b1")

    weight_terms(R["x4"], 192, R["d4"], 64, dil[3], 24, R["w4"])
    weight_terms(R["x1"], 64, R["d1"], 64, dil[0], 24, R["w1"])
    pay = R["pay"]
    at = 0
    for name, C, chunks in PAYLOAD:
        n = 3 * C + ONES
        for k in range(chunks):
            pay[at : at + n, :] = R[name][0:n, k * LANES : (k + 1) * LANES].astype(BF)
            at += n
    pay[at:, :] = jnp.zeros((pay.shape[0] - at, LANES), BF)

    arrive("b1")
    out = R["grad"]

    def write_out(r, v):
        out[r] = v

    fold("b1", G1, 0, 64, 16, 128, 4, write_out)

    for listed in copies.values():
        for copy in listed:
            copy.wait_send()


PAYLOAD = (("w4", 192, 2), ("w3", 128, 3), ("w2", 64, 3), ("w1", 64, 2))
PAY_ROWS = sum((3 * C + ONES) * chunks for _, C, chunks in PAYLOAD)


def run_net(tiles, pay_rows, operands):
    V = pltpu.VMEM
    scratch = [
        ("shifts", V((4, 256, 256), BF)),
        ("picks", V((3, LANES, LANES), BF)),
        ("x1", V((24, 192 + ONES, LANES), BF)),
        ("x2", V((16, 192 + ONES, LANES), BF)),
        ("x3", V((16, 384 + ONES, LANES), BF)),
        ("x4", V((24, 576 + ONES, LANES), BF)),
        ("d1", V((32, 192, LANES), BF)),
        ("d2", V((24, 384, LANES), BF)),
        ("d3", V((24, 384, LANES), BF)),
        ("d4", V((32, 192, LANES), BF)),
        ("g1", V((24, 64, LANES), F32)),
        ("g2", V((16, 64, LANES), F32)),
        ("g3", V((16, 128, LANES), F32)),
        ("g4", V((24, 192, LANES), F32)),
        ("g4c", V((12, 128, LANES), F32)),
        ("first_act", V((16, 64, LANES), BF)),
        ("slope1", V((16, 64, LANES), F32)),
        ("pooled", V((8, 64, LANES), BF)),
        ("second_act", V((8, 128, LANES), BF)),
        ("slope2", V((8, 128, LANES), F32)),
        ("third_act", V((8, 128, LANES), BF)),
        ("coarse", V((8, 128, LANES), F32)),
        ("skip", V((16, 64, LANES), F32)),
        ("delta1", V((16, 64, LANES), BF)),
        ("delta2", V((8, 128, LANES), BF)),
        ("delta3", V((8, 128, LANES), BF)),
        ("w1", V((208, 256), F32)),
        ("w2", V((208, 384), F32)),
        ("w3", V((400, 384), F32)),
        ("w4", V((592, 256), F32)),
        ("code_near", V((2, 8, LANES), jnp.int32)),
        ("send", pltpu.SemaphoreType.DMA((len(EXCHANGES), 8))),
        ("recv", pltpu.SemaphoreType.DMA((len(EXCHANGES), 8))),
        ("send_code", pltpu.SemaphoreType.DMA((2,))),
        ("recv_code", pltpu.SemaphoreType.DMA((2,))),
    ]
    for name, C, m, sent in EXCHANGES:
        scratch += [
            ("cs_" + name, V((sent, C, LANES), BF)),
            ("rs_" + name, V((2, m, C, LANES), BF)),
            ("cr_" + name, V((6, C, LANES), BF)),
            ("rr_" + name, V((2, m, C, LANES), BF)),
        ]
    names = [n for n, _ in operands] + ["state", "grad", "pay"] + [n for n, _ in scratch]
    smem = pl.BlockSpec(memory_space=pltpu.SMEM)
    vmem = pl.BlockSpec(memory_space=pltpu.VMEM)
    return pl.pallas_call(
        functools.partial(net_kernel, tiles, names),
        out_shape=(
            jax.ShapeDtypeStruct((16, 64, LANES), BF),
            jax.ShapeDtypeStruct((16, 64, LANES), F32),
            jax.ShapeDtypeStruct((pay_rows, LANES), BF),
        ),
        in_specs=[smem if n in ("codes", "dil") else vmem for n, _ in operands],
        out_specs=(vmem, vmem, vmem),
        scratch_shapes=[s for _, s in scratch],
        compiler_params=pltpu.CompilerParams(
            collective_id=0, has_side_effects=True, vmem_limit_bytes=56 * 2**20
        ),
        name="net",
    )(*[v for _, v in operands])


def sum_kernel(sizes, scale, pay, out, from_core, half, buf_xy, buf_z, res, s1, r1, s2, r2, s3, r3, s4, r4, s5, r5):
    n_ens, n_xy, n_low = sizes
    n_z = n_ens * n_low
    ens, tile = lax.axis_index("ens"), lax.axis_index("tile")
    xy = lax.div(tile, 2 * n_low)
    low = lax.div(lax.rem(tile, 2 * n_low), 2)
    core = lax.rem(tile, 2)
    z = ens * n_low + low

    def at(z_, xy_, core_):
        return (lax.div(z_, n_low), (xy_ * n_low + lax.rem(z_, n_low)) * 2 + core_)

    def xy_peer(k):
        return lax.rem(xy + k, n_xy)

    def z_peer(k):
        return lax.rem(z + k, n_z)

    barrier = pltpu.get_barrier_semaphore()

    def greet(device):
        pl.semaphore_signal(barrier, inc=1, device_id=device, device_id_type=MESH)

    greet(at(z, xy, 1 - core))
    for k in range(1, n_xy):
        greet(at(z, xy_peer(k), core))
    for k in range(1, n_z):
        greet(at(z_peer(k), xy, core))
    pl.semaphore_wait(barrier, 1 + (n_xy - 1) + (n_z - 1))

    def remote(src, dst, send, recv, device):
        return pltpu.make_async_remote_copy(
            src_ref=src, dst_ref=dst, send_sem=send, recv_sem=recv, device_id=device, device_id_type=MESH
        )

    pair = remote(pay.at[1 - core], from_core, s1, r1, at(z, xy, 1 - core))
    pair.start()
    pair.wait()

    def add(p, carry):
        half[p] = (pay[core, p].astype(F32) + from_core[p].astype(F32)).astype(BF)
        return carry

    lax.fori_loop(0, n_xy, add, 0)

    def xy_copy(k):
        p = xy_peer(k)
        return remote(half.at[p], buf_xy.at[xy], s2.at[k], r2.at[xy], at(z, p, core))

    def xy_arrival(k):
        p = xy_peer(k)
        return remote(half.at[p], buf_xy.at[p], s2.at[k], r2.at[p], at(z, p, core))

    for k in range(1, n_xy):
        xy_copy(k).start()
    buf_xy[xy] = half[xy]
    for k in range(1, n_xy):
        xy_arrival(k).wait_recv()
    total = buf_xy[0].astype(F32)
    for p in range(1, n_xy):
        total = total + buf_xy[p].astype(F32)
    buf_z[z] = total.astype(BF)

    def z_copy(k):
        return remote(buf_z.at[z], buf_z.at[z], s3.at[k], r3.at[z], at(z_peer(k), xy, core))

    def z_arrival(k):
        p = z_peer(k)
        return remote(buf_z.at[p], buf_z.at[p], s3.at[k], r3.at[p], at(p, xy, core))

    for k in range(1, n_z):
        z_copy(k).start()
    for k in range(1, n_z):
        z_arrival(k).wait_recv()
    total = buf_z[0].astype(F32)
    for p in range(1, n_z):
        total = total + buf_z[p].astype(F32)
    res[core, xy] = (total * scale).astype(BF)

    def back_copy(k):
        return remote(res.at[core, xy], res.at[core, xy], s4.at[k], r4.at[xy], at(z, xy_peer(k), core))

    def back_arrival(k):
        p = xy_peer(k)
        return remote(res.at[core, p], res.at[core, p], s4.at[k], r4.at[p], at(z, p, core))

    for k in range(1, n_xy):
        back_copy(k).start()
    for k in range(1, n_xy):
        back_arrival(k).wait_recv()
    other = remote(res.at[core], res.at[core], s5, r5, at(z, xy, 1 - core))
    other.start()
    theirs = remote(res.at[1 - core], res.at[1 - core], s5, r5, at(z, xy, 1 - core))
    theirs.wait_recv()
    out[...] = res[...].astype(F32)
    other.wait_send()
    for k in range(1, n_xy):
        xy_copy(k).wait_send()
        back_copy(k).wait_send()
    for k in range(1, n_z):
        z_copy(k).wait_send()


def run_sum(sizes, scale, pay):
    n_ens, n_xy, n_low = sizes
    n_z = n_ens * n_low
    _, _, q, _ = pay.shape
    V, D = pltpu.VMEM, pltpu.SemaphoreType.DMA
    vmem = pl.BlockSpec(memory_space=pltpu.VMEM)
    return pl.pallas_call(
        functools.partial(sum_kernel, sizes, scale),
        out_shape=jax.ShapeDtypeStruct(pay.shape, F32),
        in_specs=[vmem],
        out_specs=vmem,
        scratch_shapes=[
            V((n_xy, q, LANES), BF),
            V((n_xy, q, LANES), BF),
            V((n_xy, q, LANES), BF),
            V((n_z, q, LANES), BF),
            V((2, n_xy, q, LANES), BF),
            D, D, D((n_xy,)), D((n_xy,)), D((n_z,)), D((n_z,)), D((n_xy,)), D((n_xy,)), D, D,
        ],
        compiler_params=pltpu.CompilerParams(
            collective_id=1, has_side_effects=True, vmem_limit_bytes=48 * 2**20
        ),
        name="total",
    )(pay)


def shards(
    tiles,
    members,
    fields,
    cotangent,
    kernel_first,
    kernel_second,
    kernel_third,
    closing_filter_weights,
    offset_first,
    offset_second,
    offset_third,
    closing_shift_values,
    codes,
    filter_stride_spread,
):
    def forward_weights(k):
        return jnp.transpose(k, (1, 0, 2)).reshape(k.shape[1], 9 * k.shape[2])

    def backward_weights(k):
        return jnp.transpose(k[::-1], (2, 0, 1)).reshape(k.shape[2], 9 * k.shape[1])

    kernels = (kernel_first, kernel_second, kernel_third, closing_filter_weights)
    offsets = (offset_first, offset_second, offset_third, closing_shift_values)
    code_rows = jnp.broadcast_to(jnp.concatenate([codes[0], codes[0]])[:, None], (8, LANES))
    operands = [
        ("codes", codes[0]),
        ("dil", filter_stride_spread),
        ("code_rows", code_rows),
        ("fields", jnp.swapaxes(fields[0, 0], 0, 1)),
        ("cot", jnp.swapaxes(cotangent[0, 0], 0, 1)),
    ]
    for i in range(4):
        operands.append((f"kf{i + 1}", forward_weights(kernels[i])))
        operands.append((f"kt{i + 1}", backward_weights(kernels[i])))
        operands.append((f"off{i + 1}", offsets[i][:, None]))
    n_low = 4
    n_xy = tiles // (2 * n_low)
    pieces = 2 * n_xy
    q = -(-PAY_ROWS // (pieces * 16)) * 16
    state, grad, pay = run_net(tiles, q * pieces, operands)
    H, W = fields.shape[3], fields.shape[4]
    scale = 1.0 / math.sqrt(members * tiles * H * W)
    res = run_sum((members, n_xy, n_low), scale, pay.reshape(2, n_xy, q, LANES))
    res = res.reshape(q * pieces, LANES)
    weights, biases = {}, {}
    at = 0
    for name, C, chunks in PAYLOAD:
        n = 3 * C + ONES
        O = 64 if chunks == 2 else 128
        block = jnp.concatenate([res[at + k * n : at + (k + 1) * n] for k in range(chunks)], axis=1)
        at += n * chunks
        body = block[: 3 * C, : 3 * O].reshape(3, C, 3, O)
        weights[name] = jnp.transpose(body, (2, 0, 3, 1)).reshape(9, O, C)
        biases[name] = block[3 * C, O : 2 * O]
    return (
        jnp.swapaxes(state, 0, 1)[None, None],
        jnp.swapaxes(grad, 0, 1)[None, None],
        weights["w1"],
        weights["w2"],
        weights["w3"],
        weights["w4"],
        biases["w1"],
        biases["w2"],
        biases["w3"],
        biases["w4"],
    )


def solution(mesh):
    big = P("ens", "tile", None, None, None)
    in_specs = (big, big) + (P(),) * 8 + (P("tile", None), P())
    out_specs = (big, big) + (P(),) * 8
    body = functools.partial(shards, mesh.shape["tile"], mesh.shape["ens"])
    return jax.shard_map(body, mesh=mesh, in_specs=in_specs, out_specs=out_specs, check_vma=False)
```

```python
import functools
import math

import jax
import jax.numpy as jnp
from jax import lax
from jax.experimental import pallas as pl
from jax.experimental.pallas import tpu as pltpu
from jax.sharding import PartitionSpec as P

MESH = pl.DeviceIdType.MESH
BF = jnp.bfloat16
F32 = jnp.float32

RIM = 4
TILE_ROW = 8
LANES = 128
ONES = 16

FIELDS, POOLED, FIRST, SECOND, THIRD, BACK4C, BACK4F, BACK3, BACK2, BACK1 = range(10)
EXCHANGES = (
    (64, 4, 1),
    (64, 4, 1),
    (64, 4, 1),
    (128, 4, 1),
    (128, 2, 1),
    (128, 2, 3),
    (64, 4, 3),
    (128, 4, 3),
    (64, 4, 3),
    (64, 4, 3),
)
OFFSETS = (1, -1, 9, 7, -7, -9, 8, -8)
LAYERS = ((64, 64, 16, 128), (64, 128, 8, 64), (128, 128, 8, 64), (192, 64, 16, 128))


def iota(shape, dim):
    return lax.broadcasted_iota(jnp.int32, shape, dim)


def onehot(cond):
    return jnp.where(cond, 1.0, 0.0).astype(BF)


def mm(a, b):
    return jnp.dot(a, b, preferred_element_type=F32)


def mm_nt(a, b):
    return lax.dot_general(a, b, (((1,), (1,)), ((), ())), preferred_element_type=F32)


def split(values):
    high = values.astype(BF)
    low = (values - high.astype(F32)).astype(BF)
    return jnp.concatenate([high, low], axis=-1)


def cat(parts, axis):
    return parts[0] if len(parts) == 1 else jnp.concatenate(parts, axis=axis)


def log2(m):
    return m.bit_length() - 1


def column_pick(H, W, m, code_right, code_left, shape=(LANES, LANES)):
    lane = iota(shape, 1)
    code = jnp.where(lane < 64, code_right, code_left)
    idx = lane & 63
    row, col = idx >> log2(m), idx & (m - 1)
    col = jnp.where((code & 1) == 1, W - m + col, col)
    row = jnp.where((code >> 1) == 1, H - 1 - row, row)
    valid = idx < H * m
    return jnp.where(valid, row, -1), jnp.where(valid, col, -1)


def halo_target(H, m, code, row):
    w = iota((LANES, LANES), 1)
    picked = jnp.where((code & 1) == 1, H - m + row, row)
    flip = (code >> 1) == 1
    k = w - (LANES - m)
    left = jnp.where(flip, 64 + m * picked + (m - 1 - k), m * picked + k)
    right = jnp.where(flip, m * picked + (m - 1 - w), 64 + m * picked + w)
    return jnp.where(w >= LANES - m, left, jnp.where(w < m, right, -1))


def shift_matrix(W, d):
    source = iota((2 * LANES, 2 * LANES), 0)
    out = iota((2 * LANES, 2 * LANES), 1)
    j = out & (LANES - 1)
    minus = jnp.where(j >= d, j - d, 2 * LANES + j - d)
    plus = jnp.where(j + d < W, j + d, LANES + j + d - W)
    return onehot((source == jnp.where(out < LANES, minus, plus)) & (j < W))


def reversal(W, code, shape=(LANES, LANES)):
    u, w = iota(shape, 0), iota(shape, 1)
    flip = (code >> 1) == 1
    return (u == jnp.where(flip, W - 1 - w, w)) & (w < W)


def pick_rows_matrix(W, code):
    u = iota((2 * LANES, LANES), 0)
    w = iota((2 * LANES, LANES), 1)
    flip = (code >> 1) == 1
    hit = (u & (LANES - 1)) == jnp.where(flip, W - 1 - w, w)
    return onehot(hit & ((u >> 7) == (code & 1)) & (w < W))


def return_rows_matrix(W, code_upper, code_lower, last):
    u = iota((2 * LANES, LANES), 0)
    w = iota((2 * LANES, LANES), 1)
    code = jnp.where(u < LANES, code_upper, code_lower)
    flip = (code >> 1) == 1
    hit = (u & (LANES - 1)) == jnp.where(flip, W - 1 - w, w)
    return onehot(hit & ((code & 1) == last) & (w < W))


def rim_matrix(H, m, code_above, code_below, collapse):
    shape = (2 * LANES, LANES)
    u, lane = iota(shape, 0), iota(shape, 1)
    src = u & (LANES - 1)
    if collapse:
        src = ((src >> 3) << 1) + ((src & 3) >> 1)
    src = src + (u >> 7) * 1024
    idx = lane & 63
    row, k = idx >> log2(m), idx & (m - 1)
    leftward = lane < 64
    valid = idx < H * m
    parts = [onehot((src == (row + m) * m + k + jnp.where(leftward, 1024, 0)) & valid)]
    for code, base in ((code_above, 0), (code_below, H + m)):
        picked = jnp.where((code & 1) == 1, row - (H - m), row)
        flip = jnp.where((code >> 1) == 1, 1, 0)
        kk = jnp.where(flip == 1, m - 1 - k, k)
        left_side = jnp.where(leftward, 1 - flip, flip)
        hit = src == (picked + base) * m + kk + left_side * 1024
        parts.append(onehot(hit & valid & (picked >= 0) & (picked < m)))
    return jnp.concatenate(parts, axis=1)


def edge_matrix(H, d):
    u, v = iota((LANES, LANES), 0), iota((LANES, LANES), 1)
    row, k = v >> 2, v & 3
    parts = []
    for a in range(3):
        h = row - RIM - (a - 1) * d
        inside = (h >= 0) & (h < H)
        parts.append(onehot((u == 4 * h + (4 - d + k)) & inside & (k < d)))
        parts.append(onehot((u == 64 + 4 * h + (k - 4 + d)) & inside & (k >= 4 - d)))
    return jnp.concatenate(parts, axis=1)


def gelu_and_slope(x):
    cdf = 0.5 + 0.5 * lax.erf(x * math.sqrt(0.5))
    pdf = jnp.exp(-0.5 * x * x) * (1.0 / math.sqrt(2.0 * math.pi))
    return x * cdf, cdf + x * pdf


def stacked(values):
    return values.reshape(values.shape[0] * values.shape[1], values.shape[2])


class Refs:
    def __init__(self, **parts):
        self.__dict__.update(parts)


def flatten(part):
    for value in part.__dict__.values():
        yield from value if type(value) is list else [value]


def fill_in(parts, refs):
    named = {}
    for part in parts:
        for key, value in part.__dict__.items():
            named[key] = [next(refs) for _ in value] if type(value) is list else next(refs)
    return named


def net_kernel(tiles, members, scale, tree, *refs):
    R = Refs(**fill_in(tree, iter(refs)))
    tile = lax.axis_index("tile")
    ens = lax.axis_index("ens")

    def device(offset):
        return (ens, lax.rem(tile + (offset + tiles), tiles))

    copies = []
    for x, (C, m, sent) in enumerate(EXCHANGES):
        listed = []
        for slot, offset in enumerate(OFFSETS):
            if slot < 6:
                which = 0 if sent == 1 else (0, 0, 2, 2, 1, 1)[slot]
                src = R.cs[x].at[which]
                dst = R.cr[x].at[slot]
            else:
                src = R.rs[x].at[slot - 6]
                dst = R.rr[x].at[slot - 6]
            listed.append(
                pltpu.make_async_remote_copy(
                    src_ref=src,
                    dst_ref=dst,
                    send_sem=R.send.at[x, slot],
                    recv_sem=R.recv.at[x, slot],
                    device_id=device(offset),
                    device_id_type=MESH,
                )
            )
        copies.append(listed)
    code_copies = [
        pltpu.make_async_remote_copy(
            src_ref=R.code_rows,
            dst_ref=R.code_near.at[k],
            send_sem=R.send_code.at[k],
            recv_sem=R.recv_code.at[k],
            device_id=device(offset),
            device_id_type=MESH,
        )
        for k, offset in enumerate((8, -8))
    ]

    def start(name):
        for copy in copies[name]:
            copy.start()

    def arrive(name):
        for copy in copies[name]:
            copy.wait_recv()

    n_ens, n_low = members, 4
    n_xy, n_z = tiles // (2 * n_low), n_ens * n_low
    xy = lax.div(tile, 2 * n_low)
    low = lax.div(lax.rem(tile, 2 * n_low), 2)
    core = lax.rem(tile, 2)
    z = ens * n_low + low

    def at(z_, xy_, core_):
        return (lax.div(z_, n_low), (xy_ * n_low + lax.rem(z_, n_low)) * 2 + core_)

    def xy_peer(k):
        return lax.rem(xy + k, n_xy)

    def z_peer(k):
        return lax.rem(z + k, n_z)

    def remote(src, dst, send, recv, device_id):
        return pltpu.make_async_remote_copy(
            src_ref=src, dst_ref=dst, send_sem=send, recv_sem=recv, device_id=device_id, device_id_type=MESH
        )

    def each(n, act):
        def body(k, carry):
            act(k)
            return carry

        lax.fori_loop(1, n, body, 0)

    class Sum:
        def __init__(self, tag):
            self.pay, self.from_core = R.pay[tag], R.others[tag]
            self.half, self.buf_xy, self.buf_z = R.half[tag], R.bxy[tag], R.bz[tag]
            self.res = R.res[tag]
            self.pair_sem, self.xy_sem = R.psem[tag], R.xysem[tag]
            self.z_sem = R.zsem[tag]
            partner = at(z, xy, 1 - core)
            self.pair = remote(
                self.pay.at[1 - core], self.from_core, self.pair_sem.at[0], self.pair_sem.at[1], partner
            )
            self.other = remote(
                self.res.at[core], self.res.at[core], self.pair_sem.at[2], self.pair_sem.at[3], partner
            )
            self.theirs = remote(
                self.res.at[1 - core], self.res.at[1 - core], self.pair_sem.at[2], self.pair_sem.at[3], partner
            )

        def xy_copy(self, k):
            p = xy_peer(k)
            return remote(
                self.half.at[p], self.buf_xy.at[xy], self.xy_sem.at[0, k], self.xy_sem.at[1, xy], at(z, p, core)
            )

        def xy_arrival(self, k):
            p = xy_peer(k)
            return remote(
                self.half.at[p], self.buf_xy.at[p], self.xy_sem.at[0, k], self.xy_sem.at[1, p], at(z, p, core)
            )

        def z_copy(self, k):
            here = self.buf_z.at[z]
            return remote(here, here, self.z_sem.at[0, k], self.z_sem.at[1, z], at(z_peer(k), xy, core))

        def z_arrival(self, k):
            p = z_peer(k)
            there = self.buf_z.at[p]
            return remote(there, there, self.z_sem.at[0, k], self.z_sem.at[1, p], at(p, xy, core))

        def back_copy(self, k):
            here = self.res.at[core, xy]
            return remote(here, here, self.xy_sem.at[2, k], self.xy_sem.at[3, xy], at(z, xy_peer(k), core))

        def back_arrival(self, k):
            p = xy_peer(k)
            there = self.res.at[core, p]
            return remote(there, there, self.xy_sem.at[2, k], self.xy_sem.at[3, p], at(z, p, core))

        def first(self):
            self.pair.start()

        def second(self):
            self.pair.wait()

            def add(p, carry):
                mine = self.pay[core, p].astype(F32)
                self.half[p] = (mine + self.from_core[p].astype(F32)).astype(BF)
                return carry

            lax.fori_loop(0, n_xy, add, 0)
            each(n_xy, lambda k: self.xy_copy(k).start())
            self.buf_xy[xy] = self.half[xy]

        def third(self):
            each(n_xy, lambda k: self.xy_arrival(k).wait_recv())
            total = self.buf_xy[0].astype(F32)
            for p in range(1, n_xy):
                total = total + self.buf_xy[p].astype(F32)
            self.buf_z[z] = total.astype(BF)
            each(n_z, lambda k: self.z_copy(k).start())

        def fourth(self):
            each(n_z, lambda k: self.z_arrival(k).wait_recv())
            total = self.buf_z[0].astype(F32)
            for p in range(1, n_z):
                total = total + self.buf_z[p].astype(F32)
            self.res[core, xy] = (total * scale).astype(BF)
            each(n_xy, lambda k: self.back_copy(k).start())

        def fifth(self):
            each(n_xy, lambda k: self.back_arrival(k).wait_recv())
            self.other.start()

        def sixth(self):
            self.theirs.wait_recv()

        def finish(self):
            self.other.wait_send()
            each(n_xy, lambda k: self.xy_copy(k).wait_send())
            each(n_xy, lambda k: self.back_copy(k).wait_send())
            each(n_z, lambda k: self.z_copy(k).wait_send())

    sum_a, sum_b = Sum(0), Sum(1)

    barrier = pltpu.get_barrier_semaphore()

    def greet(device_id):
        pl.semaphore_signal(barrier, inc=1, device_id=device_id, device_id_type=MESH)

    for offset in OFFSETS[:6]:
        greet(device(offset))
    each(n_xy, lambda k: greet(at(z, xy_peer(k), core)))
    each(n_z, lambda k: greet(at(z_peer(k), xy, core)))

    codes = [R.codes[0, s] for s in range(4)]
    tile_rows = iota((8, LANES), 0) & 3
    R.code_rows[...] = jnp.where(
        tile_rows == 0, codes[0], jnp.where(tile_rows == 1, codes[1], jnp.where(tile_rows == 2, codes[2], codes[3]))
    )
    dil = [R.dil[i] for i in range(4)]

    shifts = R.shifts
    for i, (_, _, _, W) in enumerate(LAYERS):
        shifts[i] = shift_matrix(W, dil[i])
    picks = R.picks
    PICK = {(16, 4): 0, (8, 4): 1, (8, 2): 2}
    for (H, m), where in PICK.items():
        _, col = column_pick(H, 128 if H == 16 else 64, m, codes[3], codes[2])
        picks[where] = onehot(iota((LANES, LANES), 0) == col)

    def pick_rows(H, m):
        row, _ = column_pick(H, 128 if H == 16 else 64, m, codes[3], codes[2], (1, LANES))
        return row

    for X3, D3, (C, O, H, _) in zip(R.x, R.d, LAYERS):
        D3[0 : 2 * RIM] = jnp.zeros((2 * RIM, 3 * O, LANES), BF)
        D3[2 * RIM + H : 4 * RIM + H] = jnp.zeros((2 * RIM, 3 * O, LANES), BF)
        X3[:, 3 * C : 3 * C + ONES, :] = jnp.ones((H + 2 * RIM, ONES, LANES), BF)

    def columns_of(x_ref, H, m, C):
        row = pick_rows(H, m)
        total = jnp.zeros((C, LANES), F32)
        for g in range(H // 4):
            y = mm(stacked(x_ref[4 * g : 4 * g + 4]), picks[PICK[(H, m)]])
            for q in range(4):
                total = total + jnp.where(row == 4 * g + q, y[q * C : (q + 1) * C], 0.0)
        return total

    def send_forward(name, x_ref, H, W, m, C):
        R.cs[name][0] = columns_of(x_ref, H, m, C).astype(BF)
        both = jnp.concatenate([stacked(x_ref[0:m]), stacked(x_ref[H - m : H])], axis=1)
        for k, side in enumerate((1, 0)):
            rows = mm(both, pick_rows_matrix(W, codes[side])).astype(BF)
            R.rs[name][k] = rows.reshape(m, C, LANES)

    def halo_arrays(name):
        near = R.cr[name]
        low = iota((1, LANES), 1) < 64
        return [jnp.where(low, near[2 * i], near[2 * i + 1]) for i in range(3)]

    def halo_rows(Z, H, m, code, rows):
        lane = iota((LANES, LANES), 0)
        mats = cat([onehot(lane == halo_target(H, m, code, r)) for r in rows], 1)
        y = mm(Z, mats).astype(BF)
        return cat([y[:, LANES * q : LANES * (q + 1)] for q in range(len(rows))], 0)

    def fill(X3, r0, core, halo, C, S, offs, repeat):
        y = mm(jnp.concatenate([core, halo], axis=1), S).astype(BF)
        for q in range(core.shape[0] // C):
            part = slice(q * C, (q + 1) * C)
            for z in range(repeat):
                r = r0 + q * repeat + z
                X3[r, offs[0] : offs[0] + C, :] = y[part, :LANES]
                X3[r, offs[1] : offs[1] + C, :] = core[part]
                X3[r, offs[2] : offs[2] + C, :] = y[part, LANES:]

    def pad_and_shift(name, x_ref, H, m, C, layer, X3, offs, refine):
        Z, Zu, Zl = halo_arrays(name)
        S = shifts[layer]
        rr = R.rr[name]
        code_u = R.code_near[0, 1:2, :]
        code_l = R.code_near[1, 0:1, :]
        rep = 2 if refine else 1

        def prepare(core, halo):
            if not refine:
                return core, halo
            u, w = iota((LANES, LANES), 0), iota((LANES, LANES), 1)
            core = mm(core, onehot(u == (w >> 1))).astype(BF)
            near = jnp.where(w < 4, w >> 1, jnp.where(w >= LANES - 4, 64 + (w >> 1), -1))
            return core, mm(halo, onehot(u == near)).astype(BF)

        def body(g, carry):
            rows = [m * g + q for q in range(m)]
            core, halo = prepare(stacked(x_ref[pl.ds(m * g, m)]), halo_rows(Z, H, m, 0, rows))
            fill(X3, RIM + m * rep * g, core, halo, C, S, offs, rep)
            return carry

        lax.fori_loop(0, H // m, body, 0, unroll=True)
        core, halo = prepare(stacked(rr[0]), halo_rows(Zu, H, m, code_u, range(m)))
        fill(X3, 0, core, halo, C, S, offs, rep)
        core, halo = prepare(stacked(rr[1]), halo_rows(Zl, H, m, code_l, range(m)))
        fill(X3, RIM + H * rep, core, halo, C, S, offs, rep)

    def conv(Z3, width, K, d, rows, write, from_row=0):
        def body(i, carry):
            r = from_row + 2 * i
            taps = []
            for b in range(3):
                base = r + RIM + (b - 1) * d
                taps.append(
                    jnp.concatenate(
                        [Z3[base, 0:width, :], Z3[base + 1, 0:width, :]], axis=1
                    )
                )
            y = mm(K[...], jnp.concatenate(taps, axis=0))
            write(r, y[:, :LANES])
            write(r + 1, y[:, LANES:])
            return carry

        lax.fori_loop(0, rows // 2, body, 0, unroll=True)

    def weight_terms(X3, C, D3, O, d, rows, acc):
        n = 3 * C + ONES

        def body(i, carry):
            r = 4 * i
            lhs = jnp.concatenate([X3[r + q] for q in range(4)], axis=1)
            taps = []
            for a in range(3):
                base = r + RIM - (a - 1) * d
                taps.append(
                    jnp.concatenate([D3[base + q, O : 2 * O, :] for q in range(4)], axis=1)
                )
            if O == 64:
                taps.append(jnp.zeros((O, 4 * LANES), BF))
            y = mm_nt(lhs, jnp.concatenate(taps, axis=0))
            acc[0:n] = acc[0:n] + y
            return carry

        acc[0:n] = jnp.zeros((n, acc.shape[1]), F32)
        lax.fori_loop(0, rows // 4, body, 0, unroll=True)

    def spread_delta(x_ref, H, O, layer, D3):
        def body(g, carry):
            core = stacked(x_ref[pl.ds(4 * g, 4)])
            y = mm(core, shifts[layer, 0:LANES, :]).astype(BF)
            for q in range(4):
                part = slice(q * O, (q + 1) * O)
                D3[2 * RIM + 4 * g + q, 0:O, :] = y[part, :LANES]
                D3[2 * RIM + 4 * g + q, O : 2 * O, :] = core[part]
                D3[2 * RIM + 4 * g + q, 2 * O : 3 * O, :] = y[part, LANES:]
            return carry

        lax.fori_loop(0, H // 4, body, 0, unroll=True)

    def rims_of(x_ref, H, W, O, layer, K):
        row, col = column_pick(H, W, RIM, 1, 0, (1, LANES))
        _, col_full = column_pick(H, W, RIM, 1, 0)
        pick = onehot(iota((LANES, LANES), 0) == col_full)
        edges = jnp.zeros((O, LANES), F32)
        for g in range(H // 4):
            y = mm(stacked(x_ref[4 * g : 4 * g + 4]), pick)
            for q in range(4):
                edges = edges + jnp.where(row == 4 * g + q, y[q * O : (q + 1) * O], 0.0)
        e = mm(edges.astype(BF), edge_matrix(H, dil[layer])).astype(BF)
        none = jnp.zeros((O, LANES), BF)
        blocks = []
        for b in range(3):
            a = 2 - b
            right = e[:, 2 * a * LANES : (2 * a + 1) * LANES]
            left = e[:, (2 * a + 1) * LANES : (2 * a + 2) * LANES]
            blocks.append(jnp.concatenate([right, none], axis=1))
            blocks.append(jnp.zeros((O, 2 * LANES), BF))
            blocks.append(jnp.concatenate([none, left], axis=1))
        return mm(K[...], jnp.concatenate(blocks, axis=0)).astype(BF)

    def send_backward(name, rims, G, c0, C, H, m, collapse=False):
        code_u = R.code_near[0, 1:2, :]
        code_l = R.code_near[1, 0:1, :]
        y = mm(rims, rim_matrix(H, m, code_u, code_l, collapse)).astype(BF)
        for k in range(3):
            R.cs[name][k] = y[:, k * LANES : (k + 1) * LANES]
        R.rs[name][0] = G[H + m : H + 2 * m, c0 : c0 + C, :].astype(BF)
        R.rs[name][1] = G[0:m, c0 : c0 + C, :].astype(BF)

    def fold(name, G, c0, C, H, W, m, write):
        near = R.cr[name]
        rr = R.rr[name]
        low = iota((1, LANES), 1) < 64
        back = jnp.where(
            low,
            near[1].astype(F32) + near[3].astype(F32) + near[5].astype(F32),
            near[0].astype(F32) + near[2].astype(F32) + near[4].astype(F32),
        )
        row = pick_rows(H, m)
        both = jnp.concatenate([stacked(rr[0]), stacked(rr[1])], axis=1)
        first = mm(both, return_rows_matrix(W, codes[0], codes[1], 0))
        last = mm(both, return_rows_matrix(W, codes[0], codes[1], 1))
        pick = picks[PICK[(H, m)]]
        for g in range(H // m):
            masked = [jnp.where(row == m * g + q, back, 0.0).astype(BF) for q in range(m)]
            y = mm_nt(cat(masked, 0), pick)
            if g == 0:
                y = y + first
            if g == H // m - 1:
                y = y + last
            for q in range(m):
                h = m * g + q
                write(h, G[h + m, c0 : c0 + C, :] + y[q * C : (q + 1) * C])

    def eye(n):
        return onehot(iota((n, n), 0) == iota((n, n), 1))

    def forward_weights(i):
        k, kf = R.k[i], R.kf[i]
        if i == 1:
            for t in range(0, 9, 2):
                block = k[8] if t == 8 else jnp.concatenate([k[t], k[t + 1]], axis=0)
                kf[:, t * 64 : t * 64 + block.shape[0]] = mm_nt(eye(LANES), block).astype(BF)
            return
        C = k.shape[2]
        for t in range(0, 9, 2):
            block = k[t] if t == 8 else jnp.concatenate([k[t], k[t + 1]], axis=1)
            kf[:, t * C : t * C + block.shape[1]] = block

    def backward_weights(i):
        k, kt = R.k[i], R.kt[i]
        if i == 1:
            for t in range(9):
                kt[:, t * LANES : (t + 1) * LANES] = k[8 - t]
            return
        O, C = k.shape[1], k.shape[2]
        for t in range(0, 9, 2):
            block = k[0] if t == 8 else jnp.concatenate([k[8 - t], k[7 - t]], axis=0)
            kt[:, t * O : t * O + block.shape[0]] = mm_nt(eye(C), block).astype(BF)

    def column(i):
        row = R.off[i][...]
        n = row.shape[1]
        return jnp.sum(jnp.where(iota((n, n), 0) == iota((n, n), 1), row, 0.0), axis=1, keepdims=True)

    pu, pw = iota((256, 256), 0), iota((256, 256), 1)
    to_rows = onehot(pw == ((pu & 15) << 4) + (pu >> 4))

    def rows_first(x_ref, out):
        for g in range(4):
            y = mm(to_rows, stacked(x_ref[16 * g : 16 * g + 16])).astype(BF)
            for h in range(16):
                out[h, 16 * g : 16 * g + 16, :] = y[16 * h : 16 * h + 16]

    def channels_first(x_ref, out, parts):
        for g in range(4):
            block = cat([x_ref[h, 16 * g : 16 * g + 16, :] for h in range(16)], 0)
            y = mm(to_rows, block) if parts == 1 else mm(to_rows, split(block))
            if parts == 2:
                y = y[:, :LANES] + y[:, LANES:]
            out[16 * g : 16 * g + 16] = y.astype(out.dtype).reshape(16, 16, LANES)

    def put(ref, start_row, value):
        q = ref.shape[2]
        done = 0
        while done < value.shape[0]:
            piece, inner = divmod(start_row + done, q)
            n = min(q - inner, value.shape[0] - done)
            ref[piece // n_xy, piece % n_xy, inner : inner + n, :] = value[done : done + n].astype(BF)
            done += n

    def get(ref, start_row, count):
        q = ref.shape[2]
        parts, done = [], 0
        while done < count:
            piece, inner = divmod(start_row + done, q)
            n = min(q - inner, count - done)
            parts.append(ref[piece // n_xy, piece % n_xy, inner : inner + n, :])
            done += n
        return cat(parts, 0)

    def put_terms(ref, listed):
        where = 0
        for acc, C, O in listed:
            chunks = 2 if O == 64 else 3
            for k in range(chunks):
                put(ref, where, acc[0 : 3 * C, k * LANES : (k + 1) * LANES])
                where += 3 * C
        for acc, C, O in listed:
            k = 0 if O == 64 else 1
            put(ref, where, acc[3 * C : 3 * C + ONES, k * LANES : (k + 1) * LANES])
            where += ONES
        pieces = ref.shape[0] * ref.shape[1] * ref.shape[2]
        put(ref, where, jnp.zeros((pieces - where, LANES), BF))

    def take_terms(ref, listed):
        sel = [onehot(iota((64, LANES), 1) == iota((64, LANES), 0) + 64 * k) for k in range(2)]
        where = 0
        for w_out, b_out, C, O in listed:
            for a in range(3):
                chunk, side = (a // 2, sel[a % 2]) if O == 64 else (a, eye(LANES))
                for e in range(3):
                    block = get(ref, where + chunk * 3 * C + e * C, C)
                    w_out[3 * a + e] = block.astype(F32) if O > C else mm_nt(side, block)
            where += (2 if O == 64 else 3) * 3 * C
        for w_out, b_out, C, O in listed:
            block = get(ref, where, ONES)
            b_out[...] = mm_nt(block, sel[1])[0:1] if O == 64 else block.astype(F32)[0:1]
            where += ONES

    rows_first(R.fields_in, R.fields)
    send_forward(FIELDS, R.fields, 16, 128, 4, 64)
    pl.semaphore_wait(barrier, 6 + (n_xy - 1) + (n_z - 1))
    for copy in code_copies:
        copy.start()
    start(FIELDS)

    forward_weights(0)
    cot = R.cot
    rows_first(R.cot_in, cot)
    backward_weights(3)
    spread_delta(cot, 16, 64, 3, R.d[3])
    G4 = R.g[3]

    def write_g4(r, v):
        G4[r] = v

    conv(R.d[3], 192, R.kt[3], dil[3], 24, write_g4)
    for i in (1, 2, 3):
        forward_weights(i)
    for i in (2, 1, 0):
        backward_weights(i)
    columns = [column(i) for i in range(4)]

    for copy in code_copies:
        copy.wait_recv()
    arrive(FIELDS)
    pad_and_shift(FIELDS, R.fields, 16, 4, 64, 0, R.x[0], (0, 64, 128), False)
    first_act, slope1 = R.first_act, R.slope1

    def write_first(r, v):
        act, slope = gelu_and_slope(v + columns[0])
        first_act[r] = act.astype(BF)
        slope1[r] = slope

    conv(R.x[0], 192, R.kf[0], dil[0], 16, write_first)
    pooled = R.pooled
    u, w = iota((2 * LANES, LANES), 0), iota((2 * LANES, LANES), 1)
    quarter = jnp.where(((u & (LANES - 1)) >> 1) == w, 0.25, 0.0).astype(BF)
    for g in range(2):
        lhs = cat(
            [
                jnp.concatenate([first_act[8 * g + 2 * q], first_act[8 * g + 2 * q + 1]], axis=1)
                for q in range(4)
            ],
            0,
        )
        pooled[4 * g : 4 * g + 4] = mm(lhs, quarter).astype(BF).reshape(4, 64, LANES)
    send_forward(POOLED, pooled, 8, 64, 4, 64)
    start(POOLED)
    send_forward(FIRST, first_act, 16, 128, 4, 64)
    start(FIRST)
    rims4 = rims_of(cot, 16, 128, 64, 3, R.kt[3])
    G4c = R.g4c
    pool = onehot(((u & (LANES - 1)) >> 1) == w)
    for g in range(3):
        pairs = [G4[8 * g + 2 * q, 0:128, :] + G4[8 * g + 2 * q + 1, 0:128, :] for q in range(4)]
        y = mm(split(cat(pairs, 0)), pool)
        G4c[4 * g : 4 * g + 4] = y.reshape(4, 128, LANES)
    send_backward(BACK4C, rims4[0:128], G4c, 0, 128, 8, 2, True)
    start(BACK4C)
    send_backward(BACK4F, rims4[128:192], G4, 128, 64, 16, 4)
    start(BACK4F)


    arrive(POOLED)
    pad_and_shift(POOLED, pooled, 8, 4, 64, 1, R.x[1], (0, 64, 128), False)
    second_act, slope2 = R.second_act, R.slope2
    inside = iota((1, LANES), 1) < 64

    def write_second(r, v):
        act, slope = gelu_and_slope(v + columns[1])
        second_act[r] = jnp.where(inside, act, 0.0).astype(BF)
        slope2[r] = jnp.where(inside, slope, 0.0)

    conv(R.x[1], 192, R.kf[1], dil[1], 8, write_second)
    send_forward(SECOND, second_act, 8, 64, 4, 128)
    start(SECOND)

    arrive(BACK4C)
    arrive(BACK4F)
    coarse, skip = R.coarse, R.skip

    def write_coarse(r, v):
        coarse[r] = v

    def write_skip(r, v):
        skip[r] = v

    fold(BACK4C, G4c, 0, 128, 8, 64, 2, write_coarse)
    fold(BACK4F, G4, 128, 64, 16, 128, 4, write_skip)

    arrive(FIRST)
    pad_and_shift(FIRST, first_act, 16, 4, 64, 3, R.x[3], (128, 320, 512), False)

    arrive(SECOND)
    pad_and_shift(SECOND, second_act, 8, 4, 128, 2, R.x[2], (0, 128, 256), False)
    third_act, delta3 = R.third_act, R.delta3

    def write_third(r, v):
        act, slope = gelu_and_slope(v + columns[2])
        third_act[r] = jnp.where(inside, act, 0.0).astype(BF)
        delta3[r] = jnp.where(inside, coarse[r] * slope, 0.0).astype(BF)

    conv(R.x[2], 384, R.kf[2], dil[2], 8, write_third)
    send_forward(THIRD, third_act, 8, 64, 2, 128)
    start(THIRD)
    spread_delta(delta3, 8, 128, 2, R.d[2])
    G3 = R.g[2]

    def write_g3(r, v):
        G3[r] = v

    conv(R.d[2], 384, R.kt[2], dil[2], 16, write_g3)
    send_backward(BACK3, rims_of(delta3, 8, 64, 128, 2, R.kt[2]), G3, 0, 128, 8, 4)
    start(BACK3)

    weight_terms(R.x[2], 128, R.d[2], 128, dil[2], 16, R.w[2])
    arrive(THIRD)
    pad_and_shift(THIRD, third_act, 8, 2, 128, 3, R.x[3], (0, 192, 384), True)

    arrive(BACK3)
    delta2 = R.delta2

    def write_delta2(r, v):
        delta2[r] = (v * slope2[r]).astype(BF)

    fold(BACK3, G3, 0, 128, 8, 64, 4, write_delta2)
    spread_delta(delta2, 8, 128, 1, R.d[1])
    G2 = R.g[1]

    def write_g2(r, v):
        G2[r] = v

    conv(R.d[1], 384, R.kt[1], dil[1], 16, write_g2)
    send_backward(BACK2, rims_of(delta2, 8, 64, 128, 1, R.kt[1]), G2, 0, 64, 8, 4)
    start(BACK2)

    weight_terms(R.x[1], 64, R.d[1], 128, dil[1], 16, R.w[1])
    weight_terms(R.x[3], 192, R.d[3], 64, dil[3], 24, R.w[3])
    put_terms(R.pay[0], ((R.w[3], 192, 64), (R.w[2], 128, 128), (R.w[1], 64, 128)))
    sum_a.first()
    state = R.state

    def write_state(r, v):
        state[r] = (v + columns[3]).astype(BF)


    arrive(BACK2)
    delta1 = R.delta1
    repeat = jnp.where((u & (LANES - 1)) == (w >> 1), 0.25, 0.0).astype(BF)

    def write_delta1(r, v):
        wide = mm(split(v), repeat)
        for z in range(2):
            delta1[2 * r + z] = ((skip[2 * r + z] + wide) * slope1[2 * r + z]).astype(BF)

    fold(BACK2, G2, 0, 64, 8, 64, 4, write_delta1)
    spread_delta(delta1, 16, 64, 0, R.d[0])
    weight_terms(R.x[0], 64, R.d[0], 64, dil[0], 24, R.w[0])
    put_terms(R.pay[1], ((R.w[0], 64, 64),))
    sum_b.first()
    G1 = R.g[0]

    def write_g1(r, v):
        G1[r] = v

    conv(R.d[0], 192, R.kt[0], dil[0], 24, write_g1)
    sum_b.second()
    send_backward(BACK1, rims_of(delta1, 16, 128, 64, 0, R.kt[0]), G1, 0, 64, 16, 4)
    start(BACK1)

    sum_a.second()
    conv(R.x[3], 576, R.kf[3], dil[3], 8, write_state)
    sum_b.third()
    arrive(BACK1)
    grad = R.grad

    def write_grad(r, v):
        grad[r] = v

    fold(BACK1, G1, 0, 64, 16, 128, 4, write_grad)
    sum_a.third()
    sum_b.fourth()
    conv(R.x[3], 576, R.kf[3], dil[3], 8, write_state, 8)
    sum_a.fourth()
    sum_b.fifth()
    channels_first(state, R.state_out, 1)
    channels_first(grad, R.grad_out, 2)
    sum_a.fifth()
    sum_b.sixth()
    take_terms(R.res[1], ((R.wo[0], R.bo[0], 64, 64),))
    sum_a.sixth()
    take_terms(R.res[0], ((R.wo[3], R.bo[3], 192, 64), (R.wo[2], R.bo[2], 128, 128), (R.wo[1], R.bo[1], 64, 128)))

    sum_a.finish()
    sum_b.finish()
    for listed in (*copies, code_copies):
        for copy in listed:
            copy.wait_send()


PIECE = (96, 16)


def run_net(tiles, members, scale, operands):
    V, D = pltpu.VMEM, pltpu.SemaphoreType.DMA
    n_xy, n_z = tiles // 8, members * 4
    sizes = [(C, O, H + 2 * RIM) for C, O, H, _ in LAYERS]
    scratch = Refs(
        shifts=V((4, 256, 256), BF),
        picks=V((3, LANES, LANES), BF),
        x=[V((P_, 3 * C + ONES, LANES), BF) for C, O, P_ in sizes],
        d=[V((P_ + 2 * RIM, 3 * O, LANES), BF) for C, O, P_ in sizes],
        g=[V((P_, C, LANES), F32) for C, O, P_ in sizes],
        g4c=V((12, 128, LANES), F32),
        kf=[V((O, 9 * C), BF) for C, O, _ in sizes],
        kt=[V((C, 9 * O), BF) for C, O, _ in sizes],
        w=[V((3 * C + ONES, 256 if O == 64 else 384), F32) for C, O, _ in sizes],
        fields=V((16, 64, LANES), BF),
        cot=V((16, 64, LANES), BF),
        state=V((16, 64, LANES), BF),
        grad=V((16, 64, LANES), F32),
        first_act=V((16, 64, LANES), BF),
        slope1=V((16, 64, LANES), F32),
        pooled=V((8, 64, LANES), BF),
        second_act=V((8, 128, LANES), BF),
        slope2=V((8, 128, LANES), F32),
        third_act=V((8, 128, LANES), BF),
        coarse=V((8, 128, LANES), F32),
        skip=V((16, 64, LANES), F32),
        delta1=V((16, 64, LANES), BF),
        delta2=V((8, 128, LANES), BF),
        delta3=V((8, 128, LANES), BF),
        code_rows=V((8, LANES), jnp.int32),
        code_near=V((2, 8, LANES), jnp.int32),
        send=D((len(EXCHANGES), 8)),
        recv=D((len(EXCHANGES), 8)),
        send_code=D((2,)),
        recv_code=D((2,)),
        pay=[V((2, n_xy, q, LANES), BF) for q in PIECE],
        others=[V((n_xy, q, LANES), BF) for q in PIECE],
        half=[V((n_xy, q, LANES), BF) for q in PIECE],
        bxy=[V((n_xy, q, LANES), BF) for q in PIECE],
        bz=[V((n_z, q, LANES), BF) for q in PIECE],
        res=[V((2, n_xy, q, LANES), BF) for q in PIECE],
        psem=[D((4,)) for q in PIECE],
        xysem=[D((4, n_xy)) for q in PIECE],
        zsem=[D((2, n_z)) for q in PIECE],
        cs=[V((sent, C, LANES), BF) for C, m, sent in EXCHANGES],
        rs=[V((2, m, C, LANES), BF) for C, m, sent in EXCHANGES],
        cr=[V((6, C, LANES), BF) for C, m, sent in EXCHANGES],
        rr=[V((2, m, C, LANES), BF) for C, m, sent in EXCHANGES],
    )
    smem = pl.BlockSpec(memory_space=pltpu.SMEM)
    vmem = pl.BlockSpec(memory_space=pltpu.VMEM)
    shape = jax.ShapeDtypeStruct
    outputs = Refs(
        state_out=shape((64, 16, LANES), BF),
        grad_out=shape((64, 16, LANES), F32),
        wo=[shape((9, C, O) if O > C else (9, O, C), F32) for C, O, _, _ in LAYERS],
        bo=[shape((1, O), F32) for C, O, _, _ in LAYERS],
    )
    inputs = Refs(**operands)
    flat_in, flat_out, flat_scratch = (list(flatten(part)) for part in (inputs, outputs, scratch))
    return pl.pallas_call(
        functools.partial(net_kernel, tiles, members, scale, (inputs, outputs, scratch)),
        out_shape=tuple(flat_out),
        in_specs=[smem if v.dtype == jnp.int32 else vmem for v in flat_in],
        out_specs=(vmem,) * len(flat_out),
        scratch_shapes=flat_scratch,
        compiler_params=pltpu.CompilerParams(
            collective_id=0, has_side_effects=True, vmem_limit_bytes=56 * 2**20
        ),
    )(*flat_in)


def shards(tiles, members, fields, cotangent, k1, k2, k3, k4, off1, off2, off3, off4, codes, dilations):
    operands = dict(
        codes=codes,
        dil=dilations,
        fields_in=fields[0, 0],
        cot_in=cotangent[0, 0],
        k=[k1, jnp.swapaxes(k2, 1, 2), k3, k4],
        off=[off1[None, :], off2[None, :], off3[None, :], off4[None, :]],
    )
    scale = 1.0 / math.sqrt(members * tiles * fields.shape[3] * fields.shape[4])
    state, grad, *rest = run_net(tiles, members, scale, operands)
    rest[1] = jnp.swapaxes(rest[1], 1, 2)
    return (state[None, None], grad[None, None], *rest[:4], *[b[0] for b in rest[4:]])


def solution(mesh):
    big = P("ens", "tile", None, None, None)
    in_specs = (big, big) + (P(),) * 8 + (P("tile", None), P())
    out_specs = (big, big) + (P(),) * 8
    body = functools.partial(shards, mesh.shape["tile"], mesh.shape["ens"])
    return jax.shard_map(body, mesh=mesh, in_specs=in_specs, out_specs=out_specs, check_vma=False)
```

```python
import functools
import math

import jax
import jax.numpy as jnp
from jax import lax
from jax.experimental import pallas as pl
from jax.experimental.pallas import tpu as pltpu
from jax.sharding import PartitionSpec as P

MESH = pl.DeviceIdType.MESH
BF = jnp.bfloat16
F32 = jnp.float32

RIM = 4
TILE_ROW = 8
LANES = 128
ONES = 16

FIELDS, POOLED, FIRST, SECOND, THIRD, BACK4C, BACK4F, BACK3, BACK2, BACK1 = range(10)
EXCHANGES = (
    (64, 4, 16, 2),
    (64, 4, 8, 2),
    (64, 4, 16, 2),
    (128, 4, 8, 2),
    (128, 2, 8, 2),
    (128, 2, 8, 6),
    (64, 4, 16, 6),
    (128, 4, 8, 6),
    (64, 4, 8, 6),
    (64, 4, 16, 6),
)
OFFSETS = (1, -1, 9, 7, -7, -9, 8, -8)
LAYERS = ((64, 64, 16, 128), (64, 128, 8, 64), (128, 128, 8, 64), (192, 64, 16, 128))


def iota(shape, dim):
    return lax.broadcasted_iota(jnp.int32, shape, dim)


def onehot(cond):
    return jnp.where(cond, 1.0, 0.0).astype(BF)


def mm(a, b):
    return jnp.dot(a, b, preferred_element_type=F32)


def mm_nt(a, b):
    return lax.dot_general(a, b, (((1,), (1,)), ((), ())), preferred_element_type=F32)


def split(values):
    high = values.astype(BF)
    low = (values - high.astype(F32)).astype(BF)
    return jnp.concatenate([high, low], axis=-1)


def cat(parts, axis):
    return parts[0] if len(parts) == 1 else jnp.concatenate(parts, axis=axis)


def log2(m):
    return m.bit_length() - 1


def column_pick(H, W, m, code_right, code_left, shape=(LANES, LANES)):
    lane = iota(shape, 1)
    code = jnp.where(lane < 64, code_right, code_left)
    idx = lane & 63
    row, col = idx >> log2(m), idx & (m - 1)
    col = jnp.where((code & 1) == 1, W - m + col, col)
    row = jnp.where((code >> 1) == 1, H - 1 - row, row)
    valid = idx < H * m
    return jnp.where(valid, row, -1), jnp.where(valid, col, -1)


def halo_target(H, m, code, row):
    w = iota((LANES, LANES), 1)
    picked = jnp.where((code & 1) == 1, H - m + row, row)
    flip = (code >> 1) == 1
    k = w - (LANES - m)
    left = jnp.where(flip, 64 + m * picked + (m - 1 - k), m * picked + k)
    right = jnp.where(flip, m * picked + (m - 1 - w), 64 + m * picked + w)
    return jnp.where(w >= LANES - m, left, jnp.where(w < m, right, -1))


def shift_matrix(W, d):
    source = iota((2 * LANES, 2 * LANES), 0)
    out = iota((2 * LANES, 2 * LANES), 1)
    j = out & (LANES - 1)
    minus = jnp.where(j >= d, j - d, 2 * LANES + j - d)
    plus = jnp.where(j + d < W, j + d, LANES + j + d - W)
    return onehot((source == jnp.where(out < LANES, minus, plus)) & (j < W))


def reversal(W, code, shape=(LANES, LANES)):
    u, w = iota(shape, 0), iota(shape, 1)
    flip = (code >> 1) == 1
    return (u == jnp.where(flip, W - 1 - w, w)) & (w < W)


def pick_rows_matrix(W, code):
    u = iota((2 * LANES, LANES), 0)
    w = iota((2 * LANES, LANES), 1)
    flip = (code >> 1) == 1
    hit = (u & (LANES - 1)) == jnp.where(flip, W - 1 - w, w)
    return onehot(hit & ((u >> 7) == (code & 1)) & (w < W))


def return_rows_matrix(W, code_upper, code_lower, last):
    u = iota((2 * LANES, LANES), 0)
    w = iota((2 * LANES, LANES), 1)
    code = jnp.where(u < LANES, code_upper, code_lower)
    flip = (code >> 1) == 1
    hit = (u & (LANES - 1)) == jnp.where(flip, W - 1 - w, w)
    return onehot(hit & ((code & 1) == last) & (w < W))


def rim_matrix(H, m, code_above, code_below, collapse):
    shape = (2 * LANES, LANES)
    u, lane = iota(shape, 0), iota(shape, 1)
    src = u & (LANES - 1)
    if collapse:
        src = ((src >> 3) << 1) + ((src & 3) >> 1)
    src = src + (u >> 7) * 1024
    idx = lane & 63
    row, k = idx >> log2(m), idx & (m - 1)
    leftward = lane < 64
    valid = idx < H * m
    parts = [onehot((src == (row + m) * m + k + jnp.where(leftward, 1024, 0)) & valid)]
    for code, base in ((code_above, 0), (code_below, H + m)):
        picked = jnp.where((code & 1) == 1, row - (H - m), row)
        flip = jnp.where((code >> 1) == 1, 1, 0)
        kk = jnp.where(flip == 1, m - 1 - k, k)
        left_side = jnp.where(leftward, 1 - flip, flip)
        hit = src == (picked + base) * m + kk + left_side * 1024
        parts.append(onehot(hit & valid & (picked >= 0) & (picked < m)))
    return jnp.concatenate(parts, axis=1)


def edge_matrix(H, d):
    u, v = iota((LANES, LANES), 0), iota((LANES, LANES), 1)
    row, k = v >> 2, v & 3
    parts = []
    for a in range(3):
        h = row - RIM - (a - 1) * d
        inside = (h >= 0) & (h < H)
        parts.append(onehot((u == 4 * h + (4 - d + k)) & inside & (k < d)))
        parts.append(onehot((u == 64 + 4 * h + (k - 4 + d)) & inside & (k >= 4 - d)))
    return jnp.concatenate(parts, axis=1)


def gelu_and_slope(x):
    cdf = 0.5 + 0.5 * lax.erf(x * math.sqrt(0.5))
    pdf = jnp.exp(-0.5 * x * x) * (1.0 / math.sqrt(2.0 * math.pi))
    return x * cdf, cdf + x * pdf


def stacked(values):
    return values.reshape(values.shape[0] * values.shape[1], values.shape[2])


class Refs:
    def __init__(self, **parts):
        self.__dict__.update(parts)


def flatten(part):
    for value in part.__dict__.values():
        yield from value if type(value) is list else [value]


def fill_in(parts, refs):
    named = {}
    for part in parts:
        for key, value in part.__dict__.items():
            named[key] = [next(refs) for _ in value] if type(value) is list else next(refs)
    return named


def pack(y, width, left):
    groups = LANES // width
    n = y.shape[0] // groups
    group = iota((1, LANES), 1) >> log2(width)
    out = jnp.zeros((n, LANES), F32)
    for g in range(groups):
        by = (g * width - (64 if left else 0)) % LANES
        part = y[g * n : (g + 1) * n]
        out = jnp.where(group == g, pltpu.roll(part, by, 1) if by else part, out)
    return out.astype(BF)


def unpack(p, width, left):
    p = p.astype(F32)
    parts = []
    for g in range(LANES // width):
        by = ((64 if left else 0) - g * width) % LANES
        parts.append(pltpu.roll(p, by, 1) if by else p)
    return jnp.concatenate(parts, axis=0)


def pack_rows(rows, W):
    if W == LANES:
        return rows.astype(BF)
    n, C, _ = rows.shape
    second = pltpu.roll(stacked(rows[n // 2 :]), 64, 1)
    return (stacked(rows[: n // 2]) + second).astype(BF).reshape(n // 2, C, LANES)


def unpack_rows(x, W):
    x = stacked(x)
    if W == LANES:
        return x
    return jnp.concatenate([x, pltpu.roll(x.astype(F32), 64, 1).astype(BF)], axis=0)


def net_kernel(tiles, members, scale, tree, *refs):
    R = Refs(**fill_in(tree, iter(refs)))
    tile = lax.axis_index("tile")
    ens = lax.axis_index("ens")

    def device(offset):
        return (ens, lax.rem(tile + (offset + tiles), tiles))

    copies = []
    for x, (C, m, H, sent) in enumerate(EXCHANGES):
        listed = []
        for slot, offset in enumerate(OFFSETS):
            if slot < 6:
                which = slot % sent
                src = R.cs[x].at[which]
                dst = R.cr[x].at[slot]
            else:
                src = R.rs[x].at[slot - 6]
                dst = R.rr[x].at[slot - 6]
            listed.append(
                pltpu.make_async_remote_copy(
                    src_ref=src,
                    dst_ref=dst,
                    send_sem=R.send.at[x, slot],
                    recv_sem=R.recv.at[x, slot],
                    device_id=device(offset),
                    device_id_type=MESH,
                )
            )
        copies.append(listed)
    code_copies = [
        pltpu.make_async_remote_copy(
            src_ref=R.code_rows,
            dst_ref=R.code_near.at[k],
            send_sem=R.send_code.at[k],
            recv_sem=R.recv_code.at[k],
            device_id=device(offset),
            device_id_type=MESH,
        )
        for k, offset in enumerate((8, -8))
    ]

    def start(name):
        for copy in copies[name]:
            copy.start()

    def arrive(name):
        for copy in copies[name]:
            copy.wait_recv()

    n_ens, n_low = members, 4
    n_xy, n_z = tiles // (2 * n_low), n_ens * n_low
    xy = lax.div(tile, 2 * n_low)
    low = lax.div(lax.rem(tile, 2 * n_low), 2)
    core = lax.rem(tile, 2)
    z = ens * n_low + low

    def at(z_, xy_, core_):
        return (lax.div(z_, n_low), (xy_ * n_low + lax.rem(z_, n_low)) * 2 + core_)

    def xy_peer(k):
        return lax.rem(xy + k, n_xy)

    def z_peer(k):
        return lax.rem(z + k, n_z)

    def remote(src, dst, send, recv, device_id):
        return pltpu.make_async_remote_copy(
            src_ref=src, dst_ref=dst, send_sem=send, recv_sem=recv, device_id=device_id, device_id_type=MESH
        )

    def each(n, act):
        def body(k, carry):
            act(k)
            return carry

        lax.fori_loop(1, n, body, 0)

    class Sum:
        def __init__(self, tag):
            self.pay, self.from_core = R.pay[tag], R.others[tag]
            self.half, self.buf_xy, self.buf_z = R.half[tag], R.bxy[tag], R.bz[tag]
            self.res = R.res[tag]
            self.pair_sem, self.xy_sem = R.psem[tag], R.xysem[tag]
            self.z_sem = R.zsem[tag]
            partner = at(z, xy, 1 - core)
            self.pair = remote(
                self.pay.at[1 - core], self.from_core, self.pair_sem.at[0], self.pair_sem.at[1], partner
            )
            self.other = remote(
                self.res.at[core], self.res.at[core], self.pair_sem.at[2], self.pair_sem.at[3], partner
            )
            self.theirs = remote(
                self.res.at[1 - core], self.res.at[1 - core], self.pair_sem.at[2], self.pair_sem.at[3], partner
            )

        def xy_copy(self, k):
            p = xy_peer(k)
            return remote(
                self.half.at[p], self.buf_xy.at[xy], self.xy_sem.at[0, k], self.xy_sem.at[1, xy], at(z, p, core)
            )

        def xy_arrival(self, k):
            p = xy_peer(k)
            return remote(
                self.half.at[p], self.buf_xy.at[p], self.xy_sem.at[0, k], self.xy_sem.at[1, p], at(z, p, core)
            )

        def z_copy(self, k):
            here = self.buf_z.at[z]
            return remote(here, here, self.z_sem.at[0, k], self.z_sem.at[1, z], at(z_peer(k), xy, core))

        def z_arrival(self, k):
            p = z_peer(k)
            there = self.buf_z.at[p]
            return remote(there, there, self.z_sem.at[0, k], self.z_sem.at[1, p], at(p, xy, core))

        def back_copy(self, k):
            here = self.res.at[core, xy]
            return remote(here, here, self.xy_sem.at[2, k], self.xy_sem.at[3, xy], at(z, xy_peer(k), core))

        def back_arrival(self, k):
            p = xy_peer(k)
            there = self.res.at[core, p]
            return remote(there, there, self.xy_sem.at[2, k], self.xy_sem.at[3, p], at(z, p, core))

        def first(self):
            self.pair.start()

        def second(self):
            self.pair.wait()

            def add(p, carry):
                mine = self.pay[core, p].astype(F32)
                self.half[p] = (mine + self.from_core[p].astype(F32)).astype(BF)
                return carry

            lax.fori_loop(0, n_xy, add, 0)
            each(n_xy, lambda k: self.xy_copy(k).start())
            self.buf_xy[xy] = self.half[xy]

        def third(self):
            each(n_xy, lambda k: self.xy_arrival(k).wait_recv())
            total = self.buf_xy[0].astype(F32)
            for p in range(1, n_xy):
                total = total + self.buf_xy[p].astype(F32)
            self.buf_z[z] = total.astype(BF)
            each(n_z, lambda k: self.z_copy(k).start())

        def fourth(self):
            each(n_z, lambda k: self.z_arrival(k).wait_recv())
            total = self.buf_z[0].astype(F32)
            for p in range(1, n_z):
                total = total + self.buf_z[p].astype(F32)
            self.res[core, xy] = (total * scale).astype(BF)
            each(n_xy, lambda k: self.back_copy(k).start())

        def fifth(self):
            each(n_xy, lambda k: self.back_arrival(k).wait_recv())
            self.other.start()

        def sixth(self):
            self.theirs.wait_recv()

        def finish(self):
            self.other.wait_send()
            each(n_xy, lambda k: self.xy_copy(k).wait_send())
            each(n_xy, lambda k: self.back_copy(k).wait_send())
            each(n_z, lambda k: self.z_copy(k).wait_send())

    sum_a, sum_b = Sum(0), Sum(1)

    barrier = pltpu.get_barrier_semaphore()

    def greet(device_id):
        pl.semaphore_signal(barrier, inc=1, device_id=device_id, device_id_type=MESH)

    for offset in OFFSETS[:6]:
        greet(device(offset))
    each(n_xy, lambda k: greet(at(z, xy_peer(k), core)))
    each(n_z, lambda k: greet(at(z_peer(k), xy, core)))

    codes = [R.codes[0, s] for s in range(4)]
    tile_rows = iota((8, LANES), 0) & 3
    R.code_rows[...] = jnp.where(
        tile_rows == 0, codes[0], jnp.where(tile_rows == 1, codes[1], jnp.where(tile_rows == 2, codes[2], codes[3]))
    )
    dil = [R.dil[i] for i in range(4)]

    shifts = R.shifts
    for i, (_, _, _, W) in enumerate(LAYERS):
        shifts[i] = shift_matrix(W, dil[i])
    picks = R.picks
    PICK = {(16, 4): 0, (8, 4): 1, (8, 2): 2}
    for (H, m), where in PICK.items():
        _, col = column_pick(H, 128 if H == 16 else 64, m, codes[3], codes[2])
        picks[where] = onehot(iota((LANES, LANES), 0) == col)

    def pick_rows(H, m):
        row, _ = column_pick(H, 128 if H == 16 else 64, m, codes[3], codes[2], (1, LANES))
        return row

    for X3, D3, (C, O, H, _) in zip(R.x, R.d, LAYERS):
        D3[0 : 2 * RIM] = jnp.zeros((2 * RIM, 3 * O, LANES), BF)
        D3[2 * RIM + H : 4 * RIM + H] = jnp.zeros((2 * RIM, 3 * O, LANES), BF)
        X3[:, 3 * C : 3 * C + ONES, :] = jnp.ones((H + 2 * RIM, ONES, LANES), BF)

    def columns_of(x_ref, H, m, C):
        row = pick_rows(H, m)
        total = jnp.zeros((C, LANES), F32)
        for g in range(H // 4):
            y = mm(stacked(x_ref[4 * g : 4 * g + 4]), picks[PICK[(H, m)]])
            for q in range(4):
                total = total + jnp.where(row == 4 * g + q, y[q * C : (q + 1) * C], 0.0)
        return total

    def send_forward(name, x_ref, H, W, m, C):
        y = columns_of(x_ref, H, m, C)
        for side in range(2):
            R.cs[name][side] = pack(y, m * H, side == 1)
        both = jnp.concatenate([stacked(x_ref[0:m]), stacked(x_ref[H - m : H])], axis=1)
        for k, side in enumerate((1, 0)):
            rows = mm(both, pick_rows_matrix(W, codes[side]))
            R.rs[name][k] = pack_rows(rows.reshape(m, C, LANES), W)

    def halo_arrays(name, width):
        near = R.cr[name]
        low = iota((1, LANES), 1) < 64
        listed = []
        for i in range(3):
            right, left = unpack(near[2 * i], width, False), unpack(near[2 * i + 1], width, True)
            listed.append(jnp.where(low, right, left).astype(BF))
        return listed

    def halo_rows(Z, H, m, code, rows):
        lane = iota((LANES, LANES), 0)
        mats = cat([onehot(lane == halo_target(H, m, code, r)) for r in rows], 1)
        y = mm(Z, mats).astype(BF)
        return cat([y[:, LANES * q : LANES * (q + 1)] for q in range(len(rows))], 0)

    def fill(X3, r0, core, halo, C, S, offs, repeat):
        y = mm(jnp.concatenate([core, halo], axis=1), S).astype(BF)
        for q in range(core.shape[0] // C):
            part = slice(q * C, (q + 1) * C)
            for z in range(repeat):
                r = r0 + q * repeat + z
                X3[r, offs[0] : offs[0] + C, :] = y[part, :LANES]
                X3[r, offs[1] : offs[1] + C, :] = core[part]
                X3[r, offs[2] : offs[2] + C, :] = y[part, LANES:]

    def pad_and_shift(name, x_ref, H, m, C, layer, X3, offs, refine):
        Z, Zu, Zl = halo_arrays(name, H * m)
        W = LANES * H // 16
        S = shifts[layer]
        rr = R.rr[name]
        code_u = R.code_near[0, 1:2, :]
        code_l = R.code_near[1, 0:1, :]
        rep = 2 if refine else 1

        def prepare(core, halo):
            if not refine:
                return core, halo
            u, w = iota((LANES, LANES), 0), iota((LANES, LANES), 1)
            core = mm(core, onehot(u == (w >> 1))).astype(BF)
            near = jnp.where(w < 4, w >> 1, jnp.where(w >= LANES - 4, 64 + (w >> 1), -1))
            return core, mm(halo, onehot(u == near)).astype(BF)

        def body(g, carry):
            rows = [m * g + q for q in range(m)]
            core, halo = prepare(stacked(x_ref[pl.ds(m * g, m)]), halo_rows(Z, H, m, 0, rows))
            fill(X3, RIM + m * rep * g, core, halo, C, S, offs, rep)
            return carry

        lax.fori_loop(0, H // m, body, 0, unroll=True)
        core, halo = prepare(unpack_rows(rr[0], W), halo_rows(Zu, H, m, code_u, range(m)))
        fill(X3, 0, core, halo, C, S, offs, rep)
        core, halo = prepare(unpack_rows(rr[1], W), halo_rows(Zl, H, m, code_l, range(m)))
        fill(X3, RIM + H * rep, core, halo, C, S, offs, rep)

    def conv(Z3, width, K, d, rows, write, from_row=0):
        def body(i, carry):
            r = from_row + 2 * i
            taps = []
            for b in range(3):
                base = r + RIM + (b - 1) * d
                taps.append(
                    jnp.concatenate(
                        [Z3[base, 0:width, :], Z3[base + 1, 0:width, :]], axis=1
                    )
                )
            y = mm(K[...], jnp.concatenate(taps, axis=0))
            write(r, y[:, :LANES])
            write(r + 1, y[:, LANES:])
            return carry

        lax.fori_loop(0, rows // 2, body, 0, unroll=True)

    def weight_terms(X3, C, D3, O, d, rows, acc):
        n = 3 * C + ONES

        def body(i, carry):
            r = 4 * i
            lhs = jnp.concatenate([X3[r + q] for q in range(4)], axis=1)
            taps = []
            for a in range(3):
                base = r + RIM - (a - 1) * d
                taps.append(
                    jnp.concatenate([D3[base + q, O : 2 * O, :] for q in range(4)], axis=1)
                )
            if O == 64:
                taps.append(jnp.zeros((O, 4 * LANES), BF))
            y = mm_nt(lhs, jnp.concatenate(taps, axis=0))
            acc[0:n] = acc[0:n] + y
            return carry

        acc[0:n] = jnp.zeros((n, acc.shape[1]), F32)
        lax.fori_loop(0, rows // 4, body, 0, unroll=True)

    def spread_delta(x_ref, H, O, layer, D3):
        def body(g, carry):
            core = stacked(x_ref[pl.ds(4 * g, 4)])
            y = mm(core, shifts[layer, 0:LANES, :]).astype(BF)
            for q in range(4):
                part = slice(q * O, (q + 1) * O)
                D3[2 * RIM + 4 * g + q, 0:O, :] = y[part, :LANES]
                D3[2 * RIM + 4 * g + q, O : 2 * O, :] = core[part]
                D3[2 * RIM + 4 * g + q, 2 * O : 3 * O, :] = y[part, LANES:]
            return carry

        lax.fori_loop(0, H // 4, body, 0, unroll=True)

    def rims_of(x_ref, H, W, O, layer, K):
        row, col = column_pick(H, W, RIM, 1, 0, (1, LANES))
        _, col_full = column_pick(H, W, RIM, 1, 0)
        pick = onehot(iota((LANES, LANES), 0) == col_full)
        edges = jnp.zeros((O, LANES), F32)
        for g in range(H // 4):
            y = mm(stacked(x_ref[4 * g : 4 * g + 4]), pick)
            for q in range(4):
                edges = edges + jnp.where(row == 4 * g + q, y[q * O : (q + 1) * O], 0.0)
        e = mm(edges.astype(BF), edge_matrix(H, dil[layer])).astype(BF)
        none = jnp.zeros((O, LANES), BF)
        blocks = []
        for b in range(3):
            a = 2 - b
            right = e[:, 2 * a * LANES : (2 * a + 1) * LANES]
            left = e[:, (2 * a + 1) * LANES : (2 * a + 2) * LANES]
            blocks.append(jnp.concatenate([right, none], axis=1))
            blocks.append(jnp.zeros((O, 2 * LANES), BF))
            blocks.append(jnp.concatenate([none, left], axis=1))
        return mm(K[...], jnp.concatenate(blocks, axis=0)).astype(BF)

    def send_backward(name, rims, G, c0, C, H, m, collapse=False):
        code_u = R.code_near[0, 1:2, :]
        code_l = R.code_near[1, 0:1, :]
        y = mm(rims, rim_matrix(H, m, code_u, code_l, collapse))
        for slot, k in enumerate((0, 0, 2, 2, 1, 1)):
            R.cs[name][slot] = pack(y[:, k * LANES : (k + 1) * LANES], H * m, slot % 2 == 0)
        W = LANES * H // 16
        R.rs[name][0] = pack_rows(G[H + m : H + 2 * m, c0 : c0 + C, :], W)
        R.rs[name][1] = pack_rows(G[0:m, c0 : c0 + C, :], W)

    def fold(name, G, c0, C, H, W, m, write):
        near = R.cr[name]
        rr = R.rr[name]
        low = iota((1, LANES), 1) < 64
        to_right, to_left = (
            near[i].astype(F32) + near[i + 2].astype(F32) + near[i + 4].astype(F32) for i in (1, 0)
        )
        back = jnp.where(low, unpack(to_right, H * m, False), unpack(to_left, H * m, True))
        row = pick_rows(H, m)
        both = jnp.concatenate([unpack_rows(rr[0], W), unpack_rows(rr[1], W)], axis=1)
        first = mm(both, return_rows_matrix(W, codes[0], codes[1], 0))
        last = mm(both, return_rows_matrix(W, codes[0], codes[1], 1))
        pick = picks[PICK[(H, m)]]
        for g in range(H // m):
            masked = [jnp.where(row == m * g + q, back, 0.0).astype(BF) for q in range(m)]
            y = mm_nt(cat(masked, 0), pick)
            if g == 0:
                y = y + first
            if g == H // m - 1:
                y = y + last
            for q in range(m):
                h = m * g + q
                write(h, G[h + m, c0 : c0 + C, :] + y[q * C : (q + 1) * C])

    def eye(n):
        return onehot(iota((n, n), 0) == iota((n, n), 1))

    def forward_weights(i):
        k, kf = R.k[i], R.kf[i]
        if i == 1:
            for t in range(0, 9, 2):
                block = k[8] if t == 8 else jnp.concatenate([k[t], k[t + 1]], axis=0)
                kf[:, t * 64 : t * 64 + block.shape[0]] = mm_nt(eye(LANES), block).astype(BF)
            return
        C = k.shape[2]
        for t in range(0, 9, 2):
            block = k[t] if t == 8 else jnp.concatenate([k[t], k[t + 1]], axis=1)
            kf[:, t * C : t * C + block.shape[1]] = block

    def backward_weights(i):
        k, kt = R.k[i], R.kt[i]
        if i == 1:
            for t in range(9):
                kt[:, t * LANES : (t + 1) * LANES] = k[8 - t]
            return
        O, C = k.shape[1], k.shape[2]
        for t in range(0, 9, 2):
            block = k[0] if t == 8 else jnp.concatenate([k[8 - t], k[7 - t]], axis=0)
            kt[:, t * O : t * O + block.shape[0]] = mm_nt(eye(C), block).astype(BF)

    def column(i):
        row = R.off[i][...]
        n = row.shape[1]
        return jnp.sum(jnp.where(iota((n, n), 0) == iota((n, n), 1), row, 0.0), axis=1, keepdims=True)

    pu, pw = iota((256, 256), 0), iota((256, 256), 1)
    to_rows = onehot(pw == ((pu & 15) << 4) + (pu >> 4))

    def rows_first(x_ref, out):
        for g in range(4):
            y = mm(to_rows, stacked(x_ref[16 * g : 16 * g + 16])).astype(BF)
            for h in range(16):
                out[h, 16 * g : 16 * g + 16, :] = y[16 * h : 16 * h + 16]

    def channels_first(x_ref, out, parts):
        for g in range(4):
            block = cat([x_ref[h, 16 * g : 16 * g + 16, :] for h in range(16)], 0)
            y = mm(to_rows, block) if parts == 1 else mm(to_rows, split(block))
            if parts == 2:
                y = y[:, :LANES] + y[:, LANES:]
            out[16 * g : 16 * g + 16] = y.astype(out.dtype).reshape(16, 16, LANES)

    def put(ref, start_row, value):
        q = ref.shape[2]
        done = 0
        while done < value.shape[0]:
            piece, inner = divmod(start_row + done, q)
            n = min(q - inner, value.shape[0] - done)
            ref[piece // n_xy, piece % n_xy, inner : inner + n, :] = value[done : done + n].astype(BF)
            done += n

    def get(ref, start_row, count):
        q = ref.shape[2]
        parts, done = [], 0
        while done < count:
            piece, inner = divmod(start_row + done, q)
            n = min(q - inner, count - done)
            parts.append(ref[piece // n_xy, piece % n_xy, inner : inner + n, :])
            done += n
        return cat(parts, 0)

    def put_terms(ref, listed):
        where = 0
        for acc, C, O in listed:
            chunks = 2 if O == 64 else 3
            for k in range(chunks):
                put(ref, where, acc[0 : 3 * C, k * LANES : (k + 1) * LANES])
                where += 3 * C
        for acc, C, O in listed:
            k = 0 if O == 64 else 1
            put(ref, where, acc[3 * C : 3 * C + ONES, k * LANES : (k + 1) * LANES])
            where += ONES
        pieces = ref.shape[0] * ref.shape[1] * ref.shape[2]
        put(ref, where, jnp.zeros((pieces - where, LANES), BF))

    def take_terms(ref, listed):
        sel = [onehot(iota((64, LANES), 1) == iota((64, LANES), 0) + 64 * k) for k in range(2)]
        where = 0
        for w_out, b_out, C, O in listed:
            for a in range(3):
                chunk, side = (a // 2, sel[a % 2]) if O == 64 else (a, eye(LANES))
                for e in range(3):
                    block = get(ref, where + chunk * 3 * C + e * C, C)
                    w_out[3 * a + e] = block.astype(F32) if O > C else mm_nt(side, block)
            where += (2 if O == 64 else 3) * 3 * C
        for w_out, b_out, C, O in listed:
            block = get(ref, where, ONES)
            b_out[...] = mm_nt(block, sel[1])[0:1] if O == 64 else block.astype(F32)[0:1]
            where += ONES

    rows_first(R.fields_in, R.fields)
    send_forward(FIELDS, R.fields, 16, 128, 4, 64)
    pl.semaphore_wait(barrier, 6 + (n_xy - 1) + (n_z - 1))
    for copy in code_copies:
        copy.start()
    start(FIELDS)

    forward_weights(0)
    cot = R.cot
    rows_first(R.cot_in, cot)
    backward_weights(3)
    spread_delta(cot, 16, 64, 3, R.d[3])
    G4 = R.g[3]

    def write_g4(r, v):
        G4[r] = v

    conv(R.d[3], 192, R.kt[3], dil[3], 24, write_g4)
    for i in (1, 2, 3):
        forward_weights(i)
    for i in (2, 1, 0):
        backward_weights(i)
    columns = [column(i) for i in range(4)]

    for copy in code_copies:
        copy.wait_recv()
    arrive(FIELDS)
    pad_and_shift(FIELDS, R.fields, 16, 4, 64, 0, R.x[0], (0, 64, 128), False)
    first_act, slope1 = R.first_act, R.slope1

    def write_first(r, v):
        act, slope = gelu_and_slope(v + columns[0])
        first_act[r] = act.astype(BF)
        slope1[r] = slope

    conv(R.x[0], 192, R.kf[0], dil[0], 16, write_first)
    pooled = R.pooled
    u, w = iota((2 * LANES, LANES), 0), iota((2 * LANES, LANES), 1)
    quarter = jnp.where(((u & (LANES - 1)) >> 1) == w, 0.25, 0.0).astype(BF)
    for g in range(2):
        lhs = cat(
            [
                jnp.concatenate([first_act[8 * g + 2 * q], first_act[8 * g + 2 * q + 1]], axis=1)
                for q in range(4)
            ],
            0,
        )
        pooled[4 * g : 4 * g + 4] = mm(lhs, quarter).astype(BF).reshape(4, 64, LANES)
    send_forward(POOLED, pooled, 8, 64, 4, 64)
    start(POOLED)
    send_forward(FIRST, first_act, 16, 128, 4, 64)
    rims4 = rims_of(cot, 16, 128, 64, 3, R.kt[3])
    G4c = R.g4c
    pool = onehot(((u & (LANES - 1)) >> 1) == w)
    for g in range(3):
        pairs = [G4[8 * g + 2 * q, 0:128, :] + G4[8 * g + 2 * q + 1, 0:128, :] for q in range(4)]
        y = mm(split(cat(pairs, 0)), pool)
        G4c[4 * g : 4 * g + 4] = y.reshape(4, 128, LANES)
    send_backward(BACK4C, rims4[0:128], G4c, 0, 128, 8, 2, True)
    send_backward(BACK4F, rims4[128:192], G4, 128, 64, 16, 4)


    arrive(POOLED)
    start(FIRST)
    start(BACK4C)
    pad_and_shift(POOLED, pooled, 8, 4, 64, 1, R.x[1], (0, 64, 128), False)
    second_act, slope2 = R.second_act, R.slope2
    inside = iota((1, LANES), 1) < 64

    def write_second(r, v):
        act, slope = gelu_and_slope(v + columns[1])
        second_act[r] = jnp.where(inside, act, 0.0).astype(BF)
        slope2[r] = jnp.where(inside, slope, 0.0)

    conv(R.x[1], 192, R.kf[1], dil[1], 8, write_second)
    send_forward(SECOND, second_act, 8, 64, 4, 128)
    start(SECOND)

    arrive(BACK4C)
    coarse, skip = R.coarse, R.skip

    def write_coarse(r, v):
        coarse[r] = v

    def write_skip(r, v):
        skip[r] = v

    fold(BACK4C, G4c, 0, 128, 8, 64, 2, write_coarse)


    arrive(FIRST)
    pad_and_shift(FIRST, first_act, 16, 4, 64, 3, R.x[3], (128, 320, 512), False)

    arrive(SECOND)
    start(BACK4F)
    pad_and_shift(SECOND, second_act, 8, 4, 128, 2, R.x[2], (0, 128, 256), False)
    third_act, delta3 = R.third_act, R.delta3

    def write_third(r, v):
        act, slope = gelu_and_slope(v + columns[2])
        third_act[r] = jnp.where(inside, act, 0.0).astype(BF)
        delta3[r] = jnp.where(inside, coarse[r] * slope, 0.0).astype(BF)

    conv(R.x[2], 384, R.kf[2], dil[2], 8, write_third)
    send_forward(THIRD, third_act, 8, 64, 2, 128)
    start(THIRD)
    spread_delta(delta3, 8, 128, 2, R.d[2])
    G3 = R.g[2]

    def write_g3(r, v):
        G3[r] = v

    conv(R.d[2], 384, R.kt[2], dil[2], 16, write_g3)
    send_backward(BACK3, rims_of(delta3, 8, 64, 128, 2, R.kt[2]), G3, 0, 128, 8, 4)
    start(BACK3)


    weight_terms(R.x[2], 128, R.d[2], 128, dil[2], 16, R.w[2])
    arrive(BACK4F)
    fold(BACK4F, G4, 128, 64, 16, 128, 4, write_skip)
    arrive(THIRD)
    pad_and_shift(THIRD, third_act, 8, 2, 128, 3, R.x[3], (0, 192, 384), True)

    weight_terms(R.x[3], 192, R.d[3], 64, dil[3], 24, R.w[3])
    put_terms(R.pay[0], ((R.w[3], 192, 64), (R.w[2], 128, 128)))
    sum_a.first()
    arrive(BACK3)
    delta2 = R.delta2

    def write_delta2(r, v):
        delta2[r] = (v * slope2[r]).astype(BF)

    fold(BACK3, G3, 0, 128, 8, 64, 4, write_delta2)
    spread_delta(delta2, 8, 128, 1, R.d[1])
    G2 = R.g[1]

    def write_g2(r, v):
        G2[r] = v

    conv(R.d[1], 384, R.kt[1], dil[1], 16, write_g2)
    send_backward(BACK2, rims_of(delta2, 8, 64, 128, 1, R.kt[1]), G2, 0, 64, 8, 4)
    start(BACK2)

    state = R.state

    def write_state(r, v):
        state[r] = (v + columns[3]).astype(BF)


    weight_terms(R.x[1], 64, R.d[1], 128, dil[1], 16, R.w[1])
    sum_a.second()
    conv(R.x[3], 576, R.kf[3], dil[3], 8, write_state)
    arrive(BACK2)
    delta1 = R.delta1
    repeat = jnp.where((u & (LANES - 1)) == (w >> 1), 0.25, 0.0).astype(BF)

    def write_delta1(r, v):
        wide = mm(split(v), repeat)
        for z in range(2):
            delta1[2 * r + z] = ((skip[2 * r + z] + wide) * slope1[2 * r + z]).astype(BF)

    fold(BACK2, G2, 0, 64, 8, 64, 4, write_delta1)
    spread_delta(delta1, 16, 64, 0, R.d[0])
    weight_terms(R.x[0], 64, R.d[0], 64, dil[0], 24, R.w[0])
    put_terms(R.pay[1], ((R.w[1], 64, 128), (R.w[0], 64, 64)))
    sum_b.first()
    G1 = R.g[0]

    def write_g1(r, v):
        G1[r] = v

    conv(R.d[0], 192, R.kt[0], dil[0], 24, write_g1)
    sum_a.third()
    sum_b.second()
    send_backward(BACK1, rims_of(delta1, 16, 128, 64, 0, R.kt[0]), G1, 0, 64, 16, 4)
    start(BACK1)

    sum_a.fourth()
    conv(R.x[3], 576, R.kf[3], dil[3], 8, write_state, 8)
    sum_b.third()
    channels_first(state, R.state_out, 1)
    sum_a.fifth()
    arrive(BACK1)
    grad = R.grad

    def write_grad(r, v):
        grad[r] = v

    fold(BACK1, G1, 0, 64, 16, 128, 4, write_grad)
    sum_b.fourth()
    channels_first(grad, R.grad_out, 2)
    sum_a.sixth()
    take_terms(R.res[0], ((R.wo[3], R.bo[3], 192, 64), (R.wo[2], R.bo[2], 128, 128)))
    sum_b.fifth()
    sum_b.sixth()
    take_terms(R.res[1], ((R.wo[1], R.bo[1], 64, 128), (R.wo[0], R.bo[0], 64, 64)))

    sum_a.finish()
    sum_b.finish()
    for listed in (*copies, code_copies):
        for copy in listed:
            copy.wait_send()


PIECE = (80, 32)


def run_net(tiles, members, scale, operands):
    V, D = pltpu.VMEM, pltpu.SemaphoreType.DMA
    n_xy, n_z = tiles // 8, members * 4
    sizes = [(C, O, H + 2 * RIM) for C, O, H, _ in LAYERS]
    scratch = Refs(
        shifts=V((4, 256, 256), BF),
        picks=V((3, LANES, LANES), BF),
        x=[V((P_, 3 * C + ONES, LANES), BF) for C, O, P_ in sizes],
        d=[V((P_ + 2 * RIM, 3 * O, LANES), BF) for C, O, P_ in sizes],
        g=[V((P_, C, LANES), F32) for C, O, P_ in sizes],
        g4c=V((12, 128, LANES), F32),
        kf=[V((O, 9 * C), BF) for C, O, _ in sizes],
        kt=[V((C, 9 * O), BF) for C, O, _ in sizes],
        w=[V((3 * C + ONES, 256 if O == 64 else 384), F32) for C, O, _ in sizes],
        fields=V((16, 64, LANES), BF),
        cot=V((16, 64, LANES), BF),
        state=V((16, 64, LANES), BF),
        grad=V((16, 64, LANES), F32),
        first_act=V((16, 64, LANES), BF),
        slope1=V((16, 64, LANES), F32),
        pooled=V((8, 64, LANES), BF),
        second_act=V((8, 128, LANES), BF),
        slope2=V((8, 128, LANES), F32),
        third_act=V((8, 128, LANES), BF),
        coarse=V((8, 128, LANES), F32),
        skip=V((16, 64, LANES), F32),
        delta1=V((16, 64, LANES), BF),
        delta2=V((8, 128, LANES), BF),
        delta3=V((8, 128, LANES), BF),
        code_rows=V((8, LANES), jnp.int32),
        code_near=V((2, 8, LANES), jnp.int32),
        send=D((len(EXCHANGES), 8)),
        recv=D((len(EXCHANGES), 8)),
        send_code=D((2,)),
        recv_code=D((2,)),
        pay=[V((2, n_xy, q, LANES), BF) for q in PIECE],
        others=[V((n_xy, q, LANES), BF) for q in PIECE],
        half=[V((n_xy, q, LANES), BF) for q in PIECE],
        bxy=[V((n_xy, q, LANES), BF) for q in PIECE],
        bz=[V((n_z, q, LANES), BF) for q in PIECE],
        res=[V((2, n_xy, q, LANES), BF) for q in PIECE],
        psem=[D((4,)) for q in PIECE],
        xysem=[D((4, n_xy)) for q in PIECE],
        zsem=[D((2, n_z)) for q in PIECE],
        cs=[V((sent, C * m * H // LANES, LANES), BF) for C, m, H, sent in EXCHANGES],
        rs=[V((2, m * H // 16, C, LANES), BF) for C, m, H, sent in EXCHANGES],
        cr=[V((6, C * m * H // LANES, LANES), BF) for C, m, H, sent in EXCHANGES],
        rr=[V((2, m * H // 16, C, LANES), BF) for C, m, H, sent in EXCHANGES],
    )
    smem = pl.BlockSpec(memory_space=pltpu.SMEM)
    vmem = pl.BlockSpec(memory_space=pltpu.VMEM)
    shape = jax.ShapeDtypeStruct
    outputs = Refs(
        state_out=shape((64, 16, LANES), BF),
        grad_out=shape((64, 16, LANES), F32),
        wo=[shape((9, C, O) if O > C else (9, O, C), F32) for C, O, _, _ in LAYERS],
        bo=[shape((1, O), F32) for C, O, _, _ in LAYERS],
    )
    inputs = Refs(**operands)
    flat_in, flat_out, flat_scratch = (list(flatten(part)) for part in (inputs, outputs, scratch))
    return pl.pallas_call(
        functools.partial(net_kernel, tiles, members, scale, (inputs, outputs, scratch)),
        out_shape=tuple(flat_out),
        in_specs=[smem if v.dtype == jnp.int32 else vmem for v in flat_in],
        out_specs=(vmem,) * len(flat_out),
        scratch_shapes=flat_scratch,
        compiler_params=pltpu.CompilerParams(
            collective_id=0, has_side_effects=True, vmem_limit_bytes=56 * 2**20
        ),
    )(*flat_in)


def shards(tiles, members, fields, cotangent, k1, k2, k3, k4, off1, off2, off3, off4, codes, dilations):
    operands = dict(
        codes=codes,
        dil=dilations,
        fields_in=fields[0, 0],
        cot_in=cotangent[0, 0],
        k=[k1, jnp.swapaxes(k2, 1, 2), k3, k4],
        off=[off1[None, :], off2[None, :], off3[None, :], off4[None, :]],
    )
    scale = 1.0 / math.sqrt(members * tiles * fields.shape[3] * fields.shape[4])
    state, grad, *rest = run_net(tiles, members, scale, operands)
    rest[1] = jnp.swapaxes(rest[1], 1, 2)
    return (state[None, None], grad[None, None], *rest[:4], *[b[0] for b in rest[4:]])


def solution(mesh):
    big = P("ens", "tile", None, None, None)
    in_specs = (big, big) + (P(),) * 8 + (P("tile", None), P())
    out_specs = (big, big) + (P(),) * 8
    body = functools.partial(shards, mesh.shape["tile"], mesh.shape["ens"])
    return jax.shard_map(body, mesh=mesh, in_specs=in_specs, out_specs=out_specs, check_vma=False)
```

```python
import functools
import math

import jax
import jax.numpy as jnp
from jax import lax
from jax.experimental import pallas as pl
from jax.experimental.pallas import tpu as pltpu
from jax.sharding import PartitionSpec as P

MESH = pl.DeviceIdType.MESH
BF = jnp.bfloat16
F32 = jnp.float32

RIM = 4
TILE_ROW = 8
LANES = 128
ONES = 16

FIELDS, POOLED, FIRST, SECOND, THIRD, BACK4C, BACK4F, BACK3, BACK2, BACK1 = range(10)
EXCHANGES = (
    (64, 4, 16, 2),
    (64, 4, 8, 2),
    (64, 4, 16, 2),
    (128, 4, 8, 2),
    (128, 2, 8, 2),
    (128, 2, 8, 6),
    (64, 4, 16, 6),
    (128, 4, 8, 6),
    (64, 4, 8, 6),
    (64, 4, 16, 6),
)
OFFSETS = (1, -1, 9, 7, -7, -9, 8, -8)
LAYERS = ((64, 64, 16, 128), (64, 128, 8, 64), (128, 128, 8, 64), (192, 64, 16, 128))


def iota(shape, dim):
    return lax.broadcasted_iota(jnp.int32, shape, dim)


def onehot(cond):
    return jnp.where(cond, 1.0, 0.0).astype(BF)


def mm(a, b):
    return jnp.dot(a, b, preferred_element_type=F32)


def mm_nt(a, b):
    return lax.dot_general(a, b, (((1,), (1,)), ((), ())), preferred_element_type=F32)


def split(values):
    high = values.astype(BF)
    low = (values - high.astype(F32)).astype(BF)
    return jnp.concatenate([high, low], axis=-1)


def cat(parts, axis):
    return parts[0] if len(parts) == 1 else jnp.concatenate(parts, axis=axis)


def log2(m):
    return m.bit_length() - 1


def column_pick(H, W, m, code_right, code_left):
    lane = iota((1, LANES), 1)
    code = jnp.where(lane < 64, code_right, code_left)
    idx = lane & 63
    row, col = idx >> log2(m), idx & (m - 1)
    col = jnp.where((code & 1) == 1, W - m + col, col)
    row = jnp.where((code >> 1) == 1, H - 1 - row, row)
    valid = idx < H * m
    return jnp.where(valid, row, -1), jnp.where(valid, col, -1)


def halo_target(H, m, code, row):
    w = iota((1, LANES), 1)
    picked = jnp.where((code & 1) == 1, H - m + row, row)
    flip = (code >> 1) == 1
    k = w - (LANES - m)
    left = jnp.where(flip, 64 + m * picked + (m - 1 - k), m * picked + k)
    right = jnp.where(flip, m * picked + (m - 1 - w), 64 + m * picked + w)
    return jnp.where(w >= LANES - m, left, jnp.where(w < m, right, -1))


def take(rows, target):
    return onehot(iota((rows, target.shape[1]), 0) == target)


def shift_matrix(W, d):
    out = iota((1, 2 * LANES), 1)
    j = out & (LANES - 1)
    minus = jnp.where(j >= d, j - d, 2 * LANES + j - d)
    plus = jnp.where(j + d < W, j + d, LANES + j + d - W)
    target = jnp.where(out < LANES, minus, plus)
    return take(2 * LANES, jnp.where(j < W, target, -1))


def turned(W, code):
    w = iota((1, LANES), 1)
    return jnp.where(w < W, jnp.where((code >> 1) == 1, W - 1 - w, w), -1024)


def pick_rows_matrix(W, code):
    return take(2 * LANES, turned(W, code) + LANES * (code & 1))


def return_rows_matrix(W, code_upper, code_lower, last):
    parts = []
    for code in (code_upper, code_lower):
        parts.append(take(LANES, jnp.where((code & 1) == last, turned(W, code), -1)))
    return jnp.concatenate(parts, axis=0)


def rim_matrix(H, m, code_above, code_below, collapse):
    shape = (2 * LANES, LANES)
    u, lane = iota(shape, 0), iota((1, LANES), 1)
    src = u
    if collapse:
        src = (((u & (LANES - 1)) >> 3) << 1) + ((u & 3) >> 1) + ((u >> 7) << 7)
    idx = lane & 63
    row, k = idx >> log2(m), idx & (m - 1)
    leftward = lane < 64
    valid = idx < H * m
    targets = [jnp.where(valid, (row + m) * m + k + jnp.where(leftward, LANES, 0), -1)]
    for code, base in ((code_above, 0), (code_below, H + m)):
        picked = jnp.where((code & 1) == 1, row - (H - m), row)
        flip = (code >> 1) & 1
        kk = jnp.where(flip == 1, m - 1 - k, k)
        left_side = jnp.where(leftward, 1 - flip, flip)
        inside = valid & (picked >= 0) & (picked < m)
        targets.append(jnp.where(inside, (picked + base) * m + kk + left_side * LANES, -1))
    return jnp.concatenate([onehot(src == target) for target in targets], axis=1)


def edge_matrix(H, d):
    v = iota((1, LANES), 1)
    row, k = v >> 2, v & 3
    parts = []
    for a in range(3):
        h = row - RIM - (a - 1) * d
        inside = (h >= 0) & (h < H)
        parts.append(take(LANES, jnp.where(inside & (k < d), 4 * h + (4 - d + k), -1)))
        parts.append(take(LANES, jnp.where(inside & (k >= 4 - d), 64 + 4 * h + (k - 4 + d), -1)))
    return jnp.concatenate(parts, axis=1)


def gelu_and_slope(x):
    cdf = 0.5 + 0.5 * lax.erf(x * math.sqrt(0.5))
    pdf = jnp.exp(-0.5 * x * x) * (1.0 / math.sqrt(2.0 * math.pi))
    return x * cdf, cdf + x * pdf


def stacked(values):
    return values.reshape(values.shape[0] * values.shape[1], values.shape[2])


def eye(n):
    return onehot(iota((n, n), 0) == iota((n, n), 1))


def to_rows():
    u, w = iota((256, 256), 0), iota((256, 256), 1)
    return onehot(w == ((u & 15) << 4) + (u >> 4))


def channels_first(x_ref, out, parts):
    turn = to_rows()
    for g in range(4):
        block = cat([x_ref[h, 16 * g : 16 * g + 16, :] for h in range(16)], 0)
        y = mm(turn, block) if parts == 1 else mm(turn, split(block))
        if parts == 2:
            y = y[:, :LANES] + y[:, LANES:]
        out[16 * g : 16 * g + 16] = y.astype(out.dtype).reshape(16, 16, LANES)


def get(ref, start_row, count):
    n_xy, q = ref.shape[1], ref.shape[2]
    parts, done = [], 0
    while done < count:
        piece, inner = divmod(start_row + done, q)
        n = min(q - inner, count - done)
        parts.append(ref[piece // n_xy, piece % n_xy, inner : inner + n, :])
        done += n
    return cat(parts, 0)


def take_terms(ref, listed):
    sel = [onehot(iota((64, LANES), 1) == iota((64, LANES), 0) + 64 * k) for k in range(2)]
    where = 0
    for w_out, b_out, C, O in listed:
        for a in range(3):
            chunk, side = (a // 2, sel[a % 2]) if O == 64 else (a, eye(LANES))
            for e in range(3):
                block = get(ref, where + chunk * 3 * C + e * C, C)
                w_out[3 * a + e] = block.astype(F32) if O > C else mm_nt(side, block)
        where += (2 if O == 64 else 3) * 3 * C
    for w_out, b_out, C, O in listed:
        block = get(ref, where, ONES)
        b_out[...] = mm_nt(block, sel[1])[0:1] if O == 64 else block.astype(F32)[0:1]
        where += ONES


class Refs:
    def __init__(self, **parts):
        self.__dict__.update(parts)


def flatten(part):
    for value in part.__dict__.values():
        yield from value if type(value) is list else [value]


def fill_in(parts, refs):
    named = {}
    for part in parts:
        for key, value in part.__dict__.items():
            named[key] = [next(refs) for _ in value] if type(value) is list else next(refs)
    return named


def pack(y, width, left):
    groups = LANES // width
    n = y.shape[0] // groups
    group = iota((1, LANES), 1) >> log2(width)
    out = jnp.zeros((n, LANES), F32)
    for g in range(groups):
        by = (g * width - (64 if left else 0)) % LANES
        part = y[g * n : (g + 1) * n]
        out = jnp.where(group == g, pltpu.roll(part, by, 1) if by else part, out)
    return out.astype(BF)


def unpack(p, width, left):
    p = p.astype(F32)
    parts = []
    for g in range(LANES // width):
        by = ((64 if left else 0) - g * width) % LANES
        parts.append(pltpu.roll(p, by, 1) if by else p)
    return jnp.concatenate(parts, axis=0)


def pack_rows(rows, W):
    if W == LANES:
        return rows.astype(BF)
    n, C, _ = rows.shape
    second = pltpu.roll(stacked(rows[n // 2 :]), 64, 1)
    return (stacked(rows[: n // 2]) + second).astype(BF).reshape(n // 2, C, LANES)


def unpack_rows(x, W):
    x = stacked(x)
    if W == LANES:
        return x
    return jnp.concatenate([x, pltpu.roll(x.astype(F32), 64, 1).astype(BF)], axis=0)


def net_kernel(tiles, members, scale, tree, *refs):
    R = Refs(**fill_in(tree, iter(refs)))
    tile = lax.axis_index("tile")
    ens = lax.axis_index("ens")

    def device(offset):
        return (ens, lax.rem(tile + (offset + tiles), tiles))

    copies = []
    for x, (C, m, H, sent) in enumerate(EXCHANGES):
        listed = []
        for slot, offset in enumerate(OFFSETS):
            if slot < 6:
                which = slot % sent
                src = R.cs[x].at[which]
                dst = R.cr[x].at[slot]
            else:
                src = R.rs[x].at[slot - 6]
                dst = R.rr[x].at[slot - 6]
            listed.append(
                pltpu.make_async_remote_copy(
                    src_ref=src,
                    dst_ref=dst,
                    send_sem=R.send.at[x, slot],
                    recv_sem=R.recv.at[x, slot],
                    device_id=device(offset),
                    device_id_type=MESH,
                )
            )
        copies.append(listed)
    code_copies = [
        pltpu.make_async_remote_copy(
            src_ref=R.code_rows,
            dst_ref=R.code_near.at[k],
            send_sem=R.send_code.at[k],
            recv_sem=R.recv_code.at[k],
            device_id=device(offset),
            device_id_type=MESH,
        )
        for k, offset in enumerate((8, -8))
    ]

    def start(name):
        for copy in copies[name]:
            copy.start()

    def arrive(name):
        for copy in copies[name]:
            copy.wait_recv()

    n_ens, n_low = members, 4
    n_xy, n_z = tiles // (2 * n_low), n_ens * n_low
    xy = lax.div(tile, 2 * n_low)
    low = lax.div(lax.rem(tile, 2 * n_low), 2)
    core = lax.rem(tile, 2)
    z = ens * n_low + low

    def at(z_, xy_, core_):
        return (lax.div(z_, n_low), (xy_ * n_low + lax.rem(z_, n_low)) * 2 + core_)

    def xy_peer(k):
        return lax.rem(xy + k, n_xy)

    def z_peer(k):
        return lax.rem(z + k, n_z)

    def remote(src, dst, send, recv, device_id):
        return pltpu.make_async_remote_copy(
            src_ref=src, dst_ref=dst, send_sem=send, recv_sem=recv, device_id=device_id, device_id_type=MESH
        )

    def each(n, act):
        def body(k, carry):
            act(k)
            return carry

        lax.fori_loop(1, n, body, 0)

    class Sum:
        def __init__(self, tag):
            self.pay, self.from_core = R.pay[tag], R.others[tag]
            self.half, self.buf_xy, self.buf_z = R.half[tag], R.bxy[tag], R.bz[tag]
            self.res = R.res[tag]
            self.pair_sem, self.xy_sem = R.psem[tag], R.xysem[tag]
            self.z_sem = R.zsem[tag]
            partner = at(z, xy, 1 - core)
            self.pair = remote(
                self.pay.at[1 - core], self.from_core, self.pair_sem.at[0], self.pair_sem.at[1], partner
            )
            self.other = remote(
                self.res.at[core], self.res.at[core], self.pair_sem.at[2], self.pair_sem.at[3], partner
            )
            self.theirs = remote(
                self.res.at[1 - core], self.res.at[1 - core], self.pair_sem.at[2], self.pair_sem.at[3], partner
            )

        def xy_copy(self, k):
            p = xy_peer(k)
            return remote(
                self.half.at[p], self.buf_xy.at[xy], self.xy_sem.at[0, k], self.xy_sem.at[1, xy], at(z, p, core)
            )

        def xy_arrival(self, k):
            p = xy_peer(k)
            return remote(
                self.half.at[p], self.buf_xy.at[p], self.xy_sem.at[0, k], self.xy_sem.at[1, p], at(z, p, core)
            )

        def z_copy(self, k):
            here = self.buf_z.at[z]
            return remote(here, here, self.z_sem.at[0, k], self.z_sem.at[1, z], at(z_peer(k), xy, core))

        def z_arrival(self, k):
            p = z_peer(k)
            there = self.buf_z.at[p]
            return remote(there, there, self.z_sem.at[0, k], self.z_sem.at[1, p], at(p, xy, core))

        def back_copy(self, k):
            here = self.res.at[core, xy]
            return remote(here, here, self.xy_sem.at[2, k], self.xy_sem.at[3, xy], at(z, xy_peer(k), core))

        def back_arrival(self, k):
            p = xy_peer(k)
            there = self.res.at[core, p]
            return remote(there, there, self.xy_sem.at[2, k], self.xy_sem.at[3, p], at(z, p, core))

        def first(self):
            self.pair.start()

        def second(self):
            self.pair.wait()

            def add(p, carry):
                mine = self.pay[core, p].astype(F32)
                self.half[p] = (mine + self.from_core[p].astype(F32)).astype(BF)
                return carry

            lax.fori_loop(0, n_xy, add, 0)
            each(n_xy, lambda k: self.xy_copy(k).start())
            self.buf_xy[xy] = self.half[xy]

        def third(self):
            each(n_xy, lambda k: self.xy_arrival(k).wait_recv())
            total = self.buf_xy[0].astype(F32)
            for p in range(1, n_xy):
                total = total + self.buf_xy[p].astype(F32)
            self.buf_z[z] = total.astype(BF)
            each(n_z, lambda k: self.z_copy(k).start())

        def fourth(self):
            each(n_z, lambda k: self.z_arrival(k).wait_recv())
            total = self.buf_z[0].astype(F32)
            for p in range(1, n_z):
                total = total + self.buf_z[p].astype(F32)
            self.res[core, xy] = (total * scale).astype(BF)
            each(n_xy, lambda k: self.back_copy(k).start())

        def fifth(self):
            each(n_xy, lambda k: self.back_arrival(k).wait_recv())
            self.other.start()

        def sixth(self):
            self.theirs.wait_recv()

        def finish(self):
            self.other.wait_send()
            each(n_xy, lambda k: self.xy_copy(k).wait_send())
            each(n_xy, lambda k: self.back_copy(k).wait_send())
            each(n_z, lambda k: self.z_copy(k).wait_send())

    sum_a, sum_b = Sum(0), Sum(1)

    barrier = pltpu.get_barrier_semaphore()

    def greet(device_id):
        pl.semaphore_signal(barrier, inc=1, device_id=device_id, device_id_type=MESH)

    for offset in OFFSETS[:6]:
        greet(device(offset))
    each(n_xy, lambda k: greet(at(z, xy_peer(k), core)))
    each(n_z, lambda k: greet(at(z_peer(k), xy, core)))

    codes = [R.codes[0, s] for s in range(4)]
    tile_rows = iota((8, LANES), 0) & 3
    R.code_rows[...] = jnp.where(
        tile_rows == 0, codes[0], jnp.where(tile_rows == 1, codes[1], jnp.where(tile_rows == 2, codes[2], codes[3]))
    )
    dil = [R.dil[i] for i in range(4)]

    shifts = R.shifts
    for i, (_, _, _, W) in enumerate(LAYERS):
        shifts[i] = shift_matrix(W, dil[i])
    picks = R.picks
    PICK = {(16, 4): 0, (8, 4): 1, (8, 2): 2}
    for (H, m), where in PICK.items():
        _, col = column_pick(H, 128 if H == 16 else 64, m, codes[3], codes[2])
        picks[where] = take(LANES, col)

    def pick_rows(H, m):
        row, _ = column_pick(H, 128 if H == 16 else 64, m, codes[3], codes[2])
        return row

    for X3, D3, (C, O, H, _) in zip(R.x, R.d, LAYERS):
        D3[0 : 2 * RIM] = jnp.zeros((2 * RIM, 3 * O, LANES), BF)
        D3[2 * RIM + H : 4 * RIM + H] = jnp.zeros((2 * RIM, 3 * O, LANES), BF)
        X3[:, 3 * C : 3 * C + ONES, :] = jnp.ones((H + 2 * RIM, ONES, LANES), BF)

    def columns_of(x_ref, H, m, C):
        row = pick_rows(H, m)
        total = jnp.zeros((C, LANES), F32)
        for g in range(H // 4):
            y = mm(stacked(x_ref[4 * g : 4 * g + 4]), picks[PICK[(H, m)]])
            for q in range(4):
                total = total + jnp.where(row == 4 * g + q, y[q * C : (q + 1) * C], 0.0)
        return total

    def send_forward(name, x_ref, H, W, m, C):
        y = columns_of(x_ref, H, m, C)
        for side in range(2):
            R.cs[name][side] = pack(y, m * H, side == 1)
        both = jnp.concatenate([stacked(x_ref[0:m]), stacked(x_ref[H - m : H])], axis=1)
        for k, side in enumerate((1, 0)):
            rows = mm(both, pick_rows_matrix(W, codes[side]))
            R.rs[name][k] = pack_rows(rows.reshape(m, C, LANES), W)

    def halo_arrays(name, width):
        near = R.cr[name]
        low = iota((1, LANES), 1) < 64
        listed = []
        for i in range(3):
            right, left = unpack(near[2 * i], width, False), unpack(near[2 * i + 1], width, True)
            listed.append(jnp.where(low, right, left).astype(BF))
        return listed

    def halo_rows(Z, H, m, code, rows):
        mats = cat([take(LANES, halo_target(H, m, code, r)) for r in rows], 1)
        y = mm(Z, mats).astype(BF)
        return cat([y[:, LANES * q : LANES * (q + 1)] for q in range(len(rows))], 0)

    def fill(X3, r0, core, halo, C, S, offs, repeat):
        y = mm(jnp.concatenate([core, halo], axis=1), S).astype(BF)
        for q in range(core.shape[0] // C):
            part = slice(q * C, (q + 1) * C)
            for z in range(repeat):
                r = r0 + q * repeat + z
                X3[r, offs[0] : offs[0] + C, :] = y[part, :LANES]
                X3[r, offs[1] : offs[1] + C, :] = core[part]
                X3[r, offs[2] : offs[2] + C, :] = y[part, LANES:]

    def pad_and_shift(name, x_ref, H, m, C, layer, X3, offs, refine):
        Z, Zu, Zl = halo_arrays(name, H * m)
        W = LANES * H // 16
        S = shifts[layer]
        rr = R.rr[name]
        code_u = R.code_near[0, 1:2, :]
        code_l = R.code_near[1, 0:1, :]
        rep = 2 if refine else 1

        def prepare(core, halo):
            if not refine:
                return core, halo
            w = iota((1, LANES), 1)
            core = mm(core, take(LANES, w >> 1)).astype(BF)
            near = jnp.where(w < 4, w >> 1, jnp.where(w >= LANES - 4, 64 + (w >> 1), -1))
            return core, mm(halo, take(LANES, near)).astype(BF)

        def body(g, carry):
            rows = [m * g + q for q in range(m)]
            core, halo = prepare(stacked(x_ref[pl.ds(m * g, m)]), halo_rows(Z, H, m, 0, rows))
            fill(X3, RIM + m * rep * g, core, halo, C, S, offs, rep)
            return carry

        lax.fori_loop(0, H // m, body, 0, unroll=True)
        core, halo = prepare(unpack_rows(rr[0], W), halo_rows(Zu, H, m, code_u, range(m)))
        fill(X3, 0, core, halo, C, S, offs, rep)
        core, halo = prepare(unpack_rows(rr[1], W), halo_rows(Zl, H, m, code_l, range(m)))
        fill(X3, RIM + H * rep, core, halo, C, S, offs, rep)

    def conv(Z3, width, K, d, rows, write, from_row=0):
        def body(i, carry):
            r = from_row + 2 * i
            taps = []
            for b in range(3):
                base = r + RIM + (b - 1) * d
                taps.append(
                    jnp.concatenate(
                        [Z3[base, 0:width, :], Z3[base + 1, 0:width, :]], axis=1
                    )
                )
            y = mm(K[...], jnp.concatenate(taps, axis=0))
            write(r, y[:, :LANES])
            write(r + 1, y[:, LANES:])
            return carry

        lax.fori_loop(0, rows // 2, body, 0, unroll=True)

    def weight_terms(X3, C, D3, O, d, rows, acc):
        n = 3 * C + ONES

        def body(i, carry):
            r = 4 * i
            lhs = jnp.concatenate([X3[r + q] for q in range(4)], axis=1)
            taps = []
            for a in range(3):
                base = r + RIM - (a - 1) * d
                taps.append(
                    jnp.concatenate([D3[base + q, O : 2 * O, :] for q in range(4)], axis=1)
                )
            if O == 64:
                taps.append(jnp.zeros((O, 4 * LANES), BF))
            y = mm_nt(lhs, jnp.concatenate(taps, axis=0))
            acc[0:n] = acc[0:n] + y
            return carry

        acc[0:n] = jnp.zeros((n, acc.shape[1]), F32)
        lax.fori_loop(0, rows // 4, body, 0, unroll=True)

    def spread_delta(x_ref, H, O, layer, D3):
        def body(g, carry):
            core = stacked(x_ref[pl.ds(4 * g, 4)])
            y = mm(core, shifts[layer, 0:LANES, :]).astype(BF)
            for q in range(4):
                part = slice(q * O, (q + 1) * O)
                D3[2 * RIM + 4 * g + q, 0:O, :] = y[part, :LANES]
                D3[2 * RIM + 4 * g + q, O : 2 * O, :] = core[part]
                D3[2 * RIM + 4 * g + q, 2 * O : 3 * O, :] = y[part, LANES:]
            return carry

        lax.fori_loop(0, H // 4, body, 0, unroll=True)

    def rims_of(x_ref, H, W, O, layer, K):
        row, col = column_pick(H, W, RIM, 1, 0)
        pick = take(LANES, col)
        edges = jnp.zeros((O, LANES), F32)
        for g in range(H // 4):
            y = mm(stacked(x_ref[4 * g : 4 * g + 4]), pick)
            for q in range(4):
                edges = edges + jnp.where(row == 4 * g + q, y[q * O : (q + 1) * O], 0.0)
        e = mm(edges.astype(BF), edge_matrix(H, dil[layer])).astype(BF)
        none = jnp.zeros((O, LANES), BF)
        blocks = []
        for b in range(3):
            a = 2 - b
            right = e[:, 2 * a * LANES : (2 * a + 1) * LANES]
            left = e[:, (2 * a + 1) * LANES : (2 * a + 2) * LANES]
            blocks.append(jnp.concatenate([right, none], axis=1))
            blocks.append(jnp.zeros((O, 2 * LANES), BF))
            blocks.append(jnp.concatenate([none, left], axis=1))
        return mm(K[...], jnp.concatenate(blocks, axis=0)).astype(BF)

    def send_backward(name, rims, G, c0, C, H, m, collapse=False):
        code_u = R.code_near[0, 1:2, :]
        code_l = R.code_near[1, 0:1, :]
        y = mm(rims, rim_matrix(H, m, code_u, code_l, collapse))
        for slot, k in enumerate((0, 0, 2, 2, 1, 1)):
            R.cs[name][slot] = pack(y[:, k * LANES : (k + 1) * LANES], H * m, slot % 2 == 0)
        W = LANES * H // 16
        R.rs[name][0] = pack_rows(G[H + m : H + 2 * m, c0 : c0 + C, :], W)
        R.rs[name][1] = pack_rows(G[0:m, c0 : c0 + C, :], W)

    def fold(name, G, c0, C, H, W, m, write):
        near = R.cr[name]
        rr = R.rr[name]
        low = iota((1, LANES), 1) < 64
        to_right, to_left = (
            near[i].astype(F32) + near[i + 2].astype(F32) + near[i + 4].astype(F32) for i in (1, 0)
        )
        back = jnp.where(low, unpack(to_right, H * m, False), unpack(to_left, H * m, True))
        row = pick_rows(H, m)
        both = jnp.concatenate([unpack_rows(rr[0], W), unpack_rows(rr[1], W)], axis=1)
        first = mm(both, return_rows_matrix(W, codes[0], codes[1], 0))
        last = mm(both, return_rows_matrix(W, codes[0], codes[1], 1))
        pick = picks[PICK[(H, m)]]
        for g in range(H // m):
            masked = [jnp.where(row == m * g + q, back, 0.0).astype(BF) for q in range(m)]
            y = mm_nt(cat(masked, 0), pick)
            if g == 0:
                y = y + first
            if g == H // m - 1:
                y = y + last
            for q in range(m):
                h = m * g + q
                write(h, G[h + m, c0 : c0 + C, :] + y[q * C : (q + 1) * C])

    def forward_weights(i):
        k, kf = R.k[i], R.kf[i]
        if i == 1:
            for t in range(0, 9, 2):
                block = k[8] if t == 8 else jnp.concatenate([k[t], k[t + 1]], axis=0)
                kf[:, t * 64 : t * 64 + block.shape[0]] = mm_nt(eye(LANES), block).astype(BF)
            return
        C = k.shape[2]
        for t in range(0, 9, 2):
            block = k[t] if t == 8 else jnp.concatenate([k[t], k[t + 1]], axis=1)
            kf[:, t * C : t * C + block.shape[1]] = block

    def backward_weights(i):
        k, kt = R.k[i], R.kt[i]
        if i == 1:
            for t in range(9):
                kt[:, t * LANES : (t + 1) * LANES] = k[8 - t]
            return
        O, C = k.shape[1], k.shape[2]
        for t in range(0, 9, 2):
            block = k[0] if t == 8 else jnp.concatenate([k[8 - t], k[7 - t]], axis=0)
            kt[:, t * O : t * O + block.shape[0]] = mm_nt(eye(C), block).astype(BF)

    def column(i):
        row = R.off[i][...]
        n = row.shape[1]
        return jnp.sum(jnp.where(iota((n, n), 0) == iota((n, n), 1), row, 0.0), axis=1, keepdims=True)

    def rows_first(x_ref, out):
        turn = to_rows()
        for g in range(4):
            y = mm(turn, stacked(x_ref[16 * g : 16 * g + 16])).astype(BF)
            for h in range(16):
                out[h, 16 * g : 16 * g + 16, :] = y[16 * h : 16 * h + 16]

    def put(ref, start_row, value):
        q = ref.shape[2]
        done = 0
        while done < value.shape[0]:
            piece, inner = divmod(start_row + done, q)
            n = min(q - inner, value.shape[0] - done)
            ref[piece // n_xy, piece % n_xy, inner : inner + n, :] = value[done : done + n].astype(BF)
            done += n

    def put_terms(ref, listed):
        where = 0
        for acc, C, O in listed:
            chunks = 2 if O == 64 else 3
            for k in range(chunks):
                put(ref, where, acc[0 : 3 * C, k * LANES : (k + 1) * LANES])
                where += 3 * C
        for acc, C, O in listed:
            k = 0 if O == 64 else 1
            put(ref, where, acc[3 * C : 3 * C + ONES, k * LANES : (k + 1) * LANES])
            where += ONES
        pieces = ref.shape[0] * ref.shape[1] * ref.shape[2]
        put(ref, where, jnp.zeros((pieces - where, LANES), BF))

    rows_first(R.fields_in, R.fields)
    send_forward(FIELDS, R.fields, 16, 128, 4, 64)
    pl.semaphore_wait(barrier, 6 + (n_xy - 1) + (n_z - 1))
    for copy in code_copies:
        copy.start()
    start(FIELDS)

    forward_weights(0)
    cot = R.cot
    rows_first(R.cot_in, cot)
    backward_weights(3)
    spread_delta(cot, 16, 64, 3, R.d[3])
    G4 = R.g[3]

    def write_g4(r, v):
        G4[r] = v

    conv(R.d[3], 192, R.kt[3], dil[3], 24, write_g4)
    for i in (1, 2, 3):
        forward_weights(i)
    for i in (2, 1, 0):
        backward_weights(i)
    columns = [column(i) for i in range(4)]

    for copy in code_copies:
        copy.wait_recv()
    arrive(FIELDS)
    pad_and_shift(FIELDS, R.fields, 16, 4, 64, 0, R.x[0], (0, 64, 128), False)
    first_act, slope1 = R.first_act, R.slope1

    def write_first(r, v):
        act, slope = gelu_and_slope(v + columns[0])
        first_act[r] = act.astype(BF)
        slope1[r] = slope

    conv(R.x[0], 192, R.kf[0], dil[0], 16, write_first)
    pooled = R.pooled
    u, w = iota((2 * LANES, LANES), 0), iota((2 * LANES, LANES), 1)
    quarter = jnp.where(((u & (LANES - 1)) >> 1) == w, 0.25, 0.0).astype(BF)
    for g in range(2):
        lhs = cat(
            [
                jnp.concatenate([first_act[8 * g + 2 * q], first_act[8 * g + 2 * q + 1]], axis=1)
                for q in range(4)
            ],
            0,
        )
        pooled[4 * g : 4 * g + 4] = mm(lhs, quarter).astype(BF).reshape(4, 64, LANES)
    send_forward(POOLED, pooled, 8, 64, 4, 64)
    start(POOLED)
    send_forward(FIRST, first_act, 16, 128, 4, 64)
    rims4 = rims_of(cot, 16, 128, 64, 3, R.kt[3])
    G4c = R.g4c
    pool = onehot(((u & (LANES - 1)) >> 1) == w)
    for g in range(3):
        pairs = [G4[8 * g + 2 * q, 0:128, :] + G4[8 * g + 2 * q + 1, 0:128, :] for q in range(4)]
        y = mm(split(cat(pairs, 0)), pool)
        G4c[4 * g : 4 * g + 4] = y.reshape(4, 128, LANES)
    send_backward(BACK4C, rims4[0:128], G4c, 0, 128, 8, 2, True)
    send_backward(BACK4F, rims4[128:192], G4, 128, 64, 16, 4)


    arrive(POOLED)
    start(FIRST)
    start(BACK4C)
    pad_and_shift(POOLED, pooled, 8, 4, 64, 1, R.x[1], (0, 64, 128), False)
    second_act, slope2 = R.second_act, R.slope2
    inside = iota((1, LANES), 1) < 64

    def write_second(r, v):
        act, slope = gelu_and_slope(v + columns[1])
        second_act[r] = jnp.where(inside, act, 0.0).astype(BF)
        slope2[r] = jnp.where(inside, slope, 0.0)

    conv(R.x[1], 192, R.kf[1], dil[1], 8, write_second)
    send_forward(SECOND, second_act, 8, 64, 4, 128)
    start(SECOND)

    arrive(BACK4C)
    coarse, skip = R.coarse, R.skip

    def write_coarse(r, v):
        coarse[r] = v

    def write_skip(r, v):
        skip[r] = v

    fold(BACK4C, G4c, 0, 128, 8, 64, 2, write_coarse)


    arrive(FIRST)
    pad_and_shift(FIRST, first_act, 16, 4, 64, 3, R.x[3], (128, 320, 512), False)

    arrive(SECOND)
    start(BACK4F)
    pad_and_shift(SECOND, second_act, 8, 4, 128, 2, R.x[2], (0, 128, 256), False)
    third_act, delta3 = R.third_act, R.delta3

    def write_third(r, v):
        act, slope = gelu_and_slope(v + columns[2])
        third_act[r] = jnp.where(inside, act, 0.0).astype(BF)
        delta3[r] = jnp.where(inside, coarse[r] * slope, 0.0).astype(BF)

    conv(R.x[2], 384, R.kf[2], dil[2], 8, write_third)
    send_forward(THIRD, third_act, 8, 64, 2, 128)
    start(THIRD)
    spread_delta(delta3, 8, 128, 2, R.d[2])
    G3 = R.g[2]

    def write_g3(r, v):
        G3[r] = v

    conv(R.d[2], 384, R.kt[2], dil[2], 16, write_g3)
    send_backward(BACK3, rims_of(delta3, 8, 64, 128, 2, R.kt[2]), G3, 0, 128, 8, 4)
    start(BACK3)


    weight_terms(R.x[2], 128, R.d[2], 128, dil[2], 16, R.w[2])
    arrive(BACK4F)
    fold(BACK4F, G4, 128, 64, 16, 128, 4, write_skip)
    arrive(THIRD)
    pad_and_shift(THIRD, third_act, 8, 2, 128, 3, R.x[3], (0, 192, 384), True)

    weight_terms(R.x[3], 192, R.d[3], 64, dil[3], 24, R.w[3])
    put_terms(R.pay[0], ((R.w[3], 192, 64), (R.w[2], 128, 128)))
    sum_a.first()
    arrive(BACK3)
    delta2 = R.delta2

    def write_delta2(r, v):
        delta2[r] = (v * slope2[r]).astype(BF)

    fold(BACK3, G3, 0, 128, 8, 64, 4, write_delta2)
    spread_delta(delta2, 8, 128, 1, R.d[1])
    G2 = R.g[1]

    def write_g2(r, v):
        G2[r] = v

    conv(R.d[1], 384, R.kt[1], dil[1], 16, write_g2)
    send_backward(BACK2, rims_of(delta2, 8, 64, 128, 1, R.kt[1]), G2, 0, 64, 8, 4)
    start(BACK2)

    state = R.state

    def write_state(r, v):
        state[r] = (v + columns[3]).astype(BF)


    weight_terms(R.x[1], 64, R.d[1], 128, dil[1], 16, R.w[1])
    sum_a.second()
    conv(R.x[3], 576, R.kf[3], dil[3], 8, write_state)
    arrive(BACK2)
    delta1 = R.delta1
    repeat = jnp.where((u & (LANES - 1)) == (w >> 1), 0.25, 0.0).astype(BF)

    def write_delta1(r, v):
        wide = mm(split(v), repeat)
        for z in range(2):
            delta1[2 * r + z] = ((skip[2 * r + z] + wide) * slope1[2 * r + z]).astype(BF)

    fold(BACK2, G2, 0, 64, 8, 64, 4, write_delta1)
    spread_delta(delta1, 16, 64, 0, R.d[0])
    weight_terms(R.x[0], 64, R.d[0], 64, dil[0], 24, R.w[0])
    put_terms(R.pay[1], ((R.w[1], 64, 128), (R.w[0], 64, 64)))
    sum_b.first()
    G1 = R.g[0]

    def write_g1(r, v):
        G1[r] = v

    conv(R.d[0], 192, R.kt[0], dil[0], 24, write_g1)
    sum_a.third()
    sum_b.second()
    send_backward(BACK1, rims_of(delta1, 16, 128, 64, 0, R.kt[0]), G1, 0, 64, 16, 4)
    start(BACK1)

    sum_a.fourth()
    conv(R.x[3], 576, R.kf[3], dil[3], 8, write_state, 8)
    sum_b.third()
    sum_a.fifth()
    arrive(BACK1)
    grad = R.grad

    def write_grad(r, v):
        grad[r] = v

    fold(BACK1, G1, 0, 64, 16, 128, 4, write_grad)
    sum_b.fourth()
    sum_a.sixth()
    sum_b.fifth()
    sum_b.sixth()

    sum_a.finish()
    sum_b.finish()
    for listed in (*copies, code_copies):
        for copy in listed:
            copy.wait_send()


PIECE = (80, 32)


def run_net(tiles, members, scale, operands):
    V, D = pltpu.VMEM, pltpu.SemaphoreType.DMA
    n_xy, n_z = tiles // 8, members * 4
    sizes = [(C, O, H + 2 * RIM) for C, O, H, _ in LAYERS]
    scratch = Refs(
        shifts=V((4, 256, 256), BF),
        picks=V((3, LANES, LANES), BF),
        x=[V((P_, 3 * C + ONES, LANES), BF) for C, O, P_ in sizes],
        d=[V((P_ + 2 * RIM, 3 * O, LANES), BF) for C, O, P_ in sizes],
        g=[V((P_, C, LANES), F32) for C, O, P_ in sizes],
        g4c=V((12, 128, LANES), F32),
        kf=[V((O, 9 * C), BF) for C, O, _ in sizes],
        kt=[V((C, 9 * O), BF) for C, O, _ in sizes],
        w=[V((3 * C + ONES, 256 if O == 64 else 384), F32) for C, O, _ in sizes],
        fields=V((16, 64, LANES), BF),
        cot=V((16, 64, LANES), BF),
        first_act=V((16, 64, LANES), BF),
        slope1=V((16, 64, LANES), F32),
        pooled=V((8, 64, LANES), BF),
        second_act=V((8, 128, LANES), BF),
        slope2=V((8, 128, LANES), F32),
        third_act=V((8, 128, LANES), BF),
        coarse=V((8, 128, LANES), F32),
        skip=V((16, 64, LANES), F32),
        delta1=V((16, 64, LANES), BF),
        delta2=V((8, 128, LANES), BF),
        delta3=V((8, 128, LANES), BF),
        code_rows=V((8, LANES), jnp.int32),
        code_near=V((2, 8, LANES), jnp.int32),
        send=D((len(EXCHANGES), 8)),
        recv=D((len(EXCHANGES), 8)),
        send_code=D((2,)),
        recv_code=D((2,)),
        pay=[V((2, n_xy, q, LANES), BF) for q in PIECE],
        others=[V((n_xy, q, LANES), BF) for q in PIECE],
        half=[V((n_xy, q, LANES), BF) for q in PIECE],
        bxy=[V((n_xy, q, LANES), BF) for q in PIECE],
        bz=[V((n_z, q, LANES), BF) for q in PIECE],
        psem=[D((4,)) for q in PIECE],
        xysem=[D((4, n_xy)) for q in PIECE],
        zsem=[D((2, n_z)) for q in PIECE],
        cs=[V((sent, C * m * H // LANES, LANES), BF) for C, m, H, sent in EXCHANGES],
        rs=[V((2, m * H // 16, C, LANES), BF) for C, m, H, sent in EXCHANGES],
        cr=[V((6, C * m * H // LANES, LANES), BF) for C, m, H, sent in EXCHANGES],
        rr=[V((2, m * H // 16, C, LANES), BF) for C, m, H, sent in EXCHANGES],
    )
    smem = pl.BlockSpec(memory_space=pltpu.SMEM)
    vmem = pl.BlockSpec(memory_space=pltpu.VMEM)
    shape = jax.ShapeDtypeStruct
    outputs = Refs(
        state=shape((16, 64, LANES), BF),
        grad=shape((16, 64, LANES), F32),
        res=[shape((2, n_xy, q, LANES), BF) for q in PIECE],
    )
    inputs = Refs(**operands)
    flat_in, flat_out, flat_scratch = (list(flatten(part)) for part in (inputs, outputs, scratch))
    return pl.pallas_call(
        functools.partial(net_kernel, tiles, members, scale, (inputs, outputs, scratch)),
        out_shape=tuple(flat_out),
        in_specs=[smem if v.dtype == jnp.int32 else vmem for v in flat_in],
        out_specs=(vmem,) * len(flat_out),
        scratch_shapes=flat_scratch,
        compiler_params=pltpu.CompilerParams(
            collective_id=0, has_side_effects=True, vmem_limit_bytes=56 * 2**20
        ),
    )(*flat_in)

def finish_kernel(state, grad, early, late, state_out, grad_out, w1, w2, w3, w4, b1, b2, b3, b4):
    channels_first(state, state_out, 1)
    channels_first(grad, grad_out, 2)
    take_terms(early, ((w4, b4, 192, 64), (w3, b3, 128, 128)))
    take_terms(late, ((w2, b2, 64, 128), (w1, b1, 64, 64)))


def run_finish(raw):
    vmem = pl.BlockSpec(memory_space=pltpu.VMEM)
    shape = jax.ShapeDtypeStruct
    outputs = [shape((64, 16, LANES), BF), shape((64, 16, LANES), F32)]
    outputs += [shape((9, C, O) if O > C else (9, O, C), F32) for C, O, _, _ in LAYERS]
    outputs += [shape((1, O), F32) for C, O, _, _ in LAYERS]
    return pl.pallas_call(
        finish_kernel,
        out_shape=tuple(outputs),
        in_specs=[vmem] * len(raw),
        out_specs=(vmem,) * len(outputs),
        compiler_params=pltpu.CompilerParams(vmem_limit_bytes=32 * 2**20),
    )(*raw)


def shards(tiles, members, fields, cotangent, k1, k2, k3, k4, off1, off2, off3, off4, codes, dilations):
    operands = dict(
        codes=codes,
        dil=dilations,
        fields_in=fields[0, 0],
        cot_in=cotangent[0, 0],
        k=[k1, jnp.swapaxes(k2, 1, 2), k3, k4],
        off=[off1[None, :], off2[None, :], off3[None, :], off4[None, :]],
    )
    scale = 1.0 / math.sqrt(members * tiles * fields.shape[3] * fields.shape[4])
    state, grad, *rest = run_finish(run_net(tiles, members, scale, operands))
    rest[1] = jnp.swapaxes(rest[1], 1, 2)
    return (state[None, None], grad[None, None], *rest[:4], *[b[0] for b in rest[4:]])


def solution(mesh):
    big = P("ens", "tile", None, None, None)
    in_specs = (big, big) + (P(),) * 8 + (P("tile", None), P())
    out_specs = (big, big) + (P(),) * 8
    body = functools.partial(shards, mesh.shape["tile"], mesh.shape["ens"])
    return jax.shard_map(body, mesh=mesh, in_specs=in_specs, out_specs=out_specs, check_vma=False)
```

```python
import functools
import math

import jax
import jax.numpy as jnp
from jax import lax
from jax.experimental import pallas as pl
from jax.experimental.pallas import tpu as pltpu
from jax.sharding import PartitionSpec as P

MESH = pl.DeviceIdType.MESH
BF = jnp.bfloat16
F32 = jnp.float32

RIM = 4
TILE_ROW = 8
LANES = 128
ONES = 16

FIELDS, POOLED, FIRST, SECOND, THIRD, BACK4C, BACK4F, BACK3, BACK2, BACK1 = range(10)
EXCHANGES = (
    (64, 4, 16, 2),
    (64, 4, 8, 2),
    (64, 4, 16, 2),
    (128, 4, 8, 2),
    (128, 2, 8, 2),
    (128, 2, 8, 6),
    (64, 4, 16, 6),
    (128, 4, 8, 6),
    (64, 4, 8, 6),
    (64, 4, 16, 6),
)
OFFSETS = (1, -1, 9, 7, -7, -9, 8, -8)
LAYERS = ((64, 64, 16, 128), (64, 128, 8, 64), (128, 128, 8, 64), (192, 64, 16, 128))


def iota(shape, dim):
    return lax.broadcasted_iota(jnp.int32, shape, dim)


def onehot(cond):
    return jnp.where(cond, 1.0, 0.0).astype(BF)


def mm(a, b):
    return jnp.dot(a, b, preferred_element_type=F32)


def mm_nt(a, b):
    return lax.dot_general(a, b, (((1,), (1,)), ((), ())), preferred_element_type=F32)


def split(values):
    high = values.astype(BF)
    low = (values - high.astype(F32)).astype(BF)
    return jnp.concatenate([high, low], axis=-1)


def cat(parts, axis):
    return parts[0] if len(parts) == 1 else jnp.concatenate(parts, axis=axis)


def log2(m):
    return m.bit_length() - 1


def column_pick(H, W, m, code_right, code_left):
    lane = iota((1, LANES), 1)
    code = jnp.where(lane < 64, code_right, code_left)
    idx = lane & 63
    row, col = idx >> log2(m), idx & (m - 1)
    col = jnp.where((code & 1) == 1, W - m + col, col)
    row = jnp.where((code >> 1) == 1, H - 1 - row, row)
    valid = idx < H * m
    return jnp.where(valid, row, -1), jnp.where(valid, col, -1)


def halo_target(H, m, code, row):
    w = iota((1, LANES), 1)
    picked = jnp.where((code & 1) == 1, H - m + row, row)
    flip = (code >> 1) == 1
    k = w - (LANES - m)
    left = jnp.where(flip, 64 + m * picked + (m - 1 - k), m * picked + k)
    right = jnp.where(flip, m * picked + (m - 1 - w), 64 + m * picked + w)
    return jnp.where(w >= LANES - m, left, jnp.where(w < m, right, -1))


def take(rows, target):
    return onehot(iota((rows, target.shape[1]), 0) == target)


def shift_matrix(W, d):
    out = iota((1, 2 * LANES), 1)
    j = out & (LANES - 1)
    minus = jnp.where(j >= d, j - d, 2 * LANES + j - d)
    plus = jnp.where(j + d < W, j + d, LANES + j + d - W)
    target = jnp.where(out < LANES, minus, plus)
    return take(2 * LANES, jnp.where(j < W, target, -1))


def turned(W, code):
    w = iota((1, LANES), 1)
    return jnp.where(w < W, jnp.where((code >> 1) == 1, W - 1 - w, w), -1024)


def pick_rows_matrix(W, code):
    return take(2 * LANES, turned(W, code) + LANES * (code & 1))


def return_rows_matrix(W, code_upper, code_lower, last):
    parts = []
    for code in (code_upper, code_lower):
        parts.append(take(LANES, jnp.where((code & 1) == last, turned(W, code), -1)))
    return jnp.concatenate(parts, axis=0)


def rim_matrix(H, m, code_above, code_below, collapse):
    shape = (2 * LANES, LANES)
    u, lane = iota(shape, 0), iota((1, LANES), 1)
    src = u
    if collapse:
        src = (((u & (LANES - 1)) >> 3) << 1) + ((u & 3) >> 1) + ((u >> 7) << 7)
    idx = lane & 63
    row, k = idx >> log2(m), idx & (m - 1)
    leftward = lane < 64
    valid = idx < H * m
    targets = [jnp.where(valid, (row + m) * m + k + jnp.where(leftward, LANES, 0), -1)]
    for code, base in ((code_above, 0), (code_below, H + m)):
        picked = jnp.where((code & 1) == 1, row - (H - m), row)
        flip = (code >> 1) & 1
        kk = jnp.where(flip == 1, m - 1 - k, k)
        left_side = jnp.where(leftward, 1 - flip, flip)
        inside = valid & (picked >= 0) & (picked < m)
        targets.append(jnp.where(inside, (picked + base) * m + kk + left_side * LANES, -1))
    return jnp.concatenate([onehot(src == target) for target in targets], axis=1)


def edge_matrix(H, d):
    v = iota((1, LANES), 1)
    row, k = v >> 2, v & 3
    parts = []
    for a in range(3):
        h = row - RIM - (a - 1) * d
        inside = (h >= 0) & (h < H)
        parts.append(take(LANES, jnp.where(inside & (k < d), 4 * h + (4 - d + k), -1)))
        parts.append(take(LANES, jnp.where(inside & (k >= 4 - d), 64 + 4 * h + (k - 4 + d), -1)))
    return jnp.concatenate(parts, axis=1)


def gelu_and_slope(x):
    cdf = 0.5 + 0.5 * lax.erf(x * math.sqrt(0.5))
    pdf = jnp.exp(-0.5 * x * x) * (1.0 / math.sqrt(2.0 * math.pi))
    return x * cdf, cdf + x * pdf


def stacked(values):
    return values.reshape(values.shape[0] * values.shape[1], values.shape[2])


def eye(n):
    return onehot(iota((n, n), 0) == iota((n, n), 1))


def to_rows():
    u, w = iota((256, 256), 0), iota((256, 256), 1)
    return onehot(w == ((u & 15) << 4) + (u >> 4))


def channels_first(x_ref, out, parts):
    turn = to_rows()
    for g in range(4):
        block = cat([x_ref[h, 16 * g : 16 * g + 16, :] for h in range(16)], 0)
        y = mm(turn, block) if parts == 1 else mm(turn, split(block))
        if parts == 2:
            y = y[:, :LANES] + y[:, LANES:]
        out[16 * g : 16 * g + 16] = y.astype(out.dtype).reshape(16, 16, LANES)


def get(ref, start_row, count):
    n_xy, q = ref.shape[1], ref.shape[2]
    parts, done = [], 0
    while done < count:
        piece, inner = divmod(start_row + done, q)
        n = min(q - inner, count - done)
        parts.append(ref[piece // n_xy, piece % n_xy, inner : inner + n, :])
        done += n
    return cat(parts, 0)


def take_terms(ref, listed):
    sel = [onehot(iota((64, LANES), 1) == iota((64, LANES), 0) + 64 * k) for k in range(2)]
    where = 0
    for w_out, b_out, C, O in listed:
        for a in range(3):
            chunk, side = (a // 2, sel[a % 2]) if O == 64 else (a, eye(LANES))
            for e in range(3):
                block = get(ref, where + chunk * 3 * C + e * C, C)
                w_out[3 * a + e] = block.astype(F32) if O > C else mm_nt(side, block)
        where += (2 if O == 64 else 3) * 3 * C
    for w_out, b_out, C, O in listed:
        block = get(ref, where, ONES)
        b_out[...] = mm_nt(block, sel[1])[0:1] if O == 64 else block.astype(F32)[0:1]
        where += ONES


class Refs:
    def __init__(self, **parts):
        self.__dict__.update(parts)


def flatten(part):
    for value in part.__dict__.values():
        yield from value if type(value) is list else [value]


def fill_in(parts, refs):
    named = {}
    for part in parts:
        for key, value in part.__dict__.items():
            named[key] = [next(refs) for _ in value] if type(value) is list else next(refs)
    return named


def pack(y, width, left):
    groups = LANES // width
    n = y.shape[0] // groups
    group = iota((1, LANES), 1) >> log2(width)
    out = jnp.zeros((n, LANES), F32)
    for g in range(groups):
        by = (g * width - (64 if left else 0)) % LANES
        part = y[g * n : (g + 1) * n]
        out = jnp.where(group == g, pltpu.roll(part, by, 1) if by else part, out)
    return out.astype(BF)


def unpack(p, width, left):
    p = p.astype(F32)
    parts = []
    for g in range(LANES // width):
        by = ((64 if left else 0) - g * width) % LANES
        parts.append(pltpu.roll(p, by, 1) if by else p)
    return jnp.concatenate(parts, axis=0)


def pack_rows(rows, W):
    if W == LANES:
        return rows.astype(BF)
    n, C, _ = rows.shape
    second = pltpu.roll(stacked(rows[n // 2 :]), 64, 1)
    return (stacked(rows[: n // 2]) + second).astype(BF).reshape(n // 2, C, LANES)


def unpack_rows(x, W):
    x = stacked(x)
    if W == LANES:
        return x
    return jnp.concatenate([x, pltpu.roll(x.astype(F32), 64, 1).astype(BF)], axis=0)


def net_kernel(tiles, members, scale, tree, *refs):
    R = Refs(**fill_in(tree, iter(refs)))
    tile = lax.axis_index("tile")
    ens = lax.axis_index("ens")

    def device(offset):
        return (ens, lax.rem(tile + (offset + tiles), tiles))

    copies = []
    for x, (C, m, H, sent) in enumerate(EXCHANGES):
        listed = []
        for slot, offset in enumerate(OFFSETS):
            if slot < 6:
                which = slot % sent
                src = R.cs[x].at[which]
                dst = R.cr[x].at[slot]
            else:
                src = R.rs[x].at[slot - 6]
                dst = R.rr[x].at[slot - 6]
            listed.append(
                pltpu.make_async_remote_copy(
                    src_ref=src,
                    dst_ref=dst,
                    send_sem=R.send.at[x, slot],
                    recv_sem=R.recv.at[x, slot],
                    device_id=device(offset),
                    device_id_type=MESH,
                )
            )
        copies.append(listed)
    code_copies = [
        pltpu.make_async_remote_copy(
            src_ref=R.code_rows,
            dst_ref=R.code_near.at[k],
            send_sem=R.send_code.at[k],
            recv_sem=R.recv_code.at[k],
            device_id=device(offset),
            device_id_type=MESH,
        )
        for k, offset in enumerate((8, -8))
    ]

    def start(name):
        for copy in copies[name]:
            copy.start()

    def arrive(name, slots=slice(0, 8)):
        for copy in copies[name][slots]:
            copy.wait_recv()

    n_ens, n_low = members, 4
    n_xy, n_z = tiles // (2 * n_low), n_ens * n_low
    xy = lax.div(tile, 2 * n_low)
    low = lax.div(lax.rem(tile, 2 * n_low), 2)
    core = lax.rem(tile, 2)
    z = ens * n_low + low

    def at(z_, xy_, core_):
        return (lax.div(z_, n_low), (xy_ * n_low + lax.rem(z_, n_low)) * 2 + core_)

    def xy_peer(k):
        return lax.rem(xy + k, n_xy)

    def z_peer(k):
        return lax.rem(z + k, n_z)

    def remote(src, dst, send, recv, device_id):
        return pltpu.make_async_remote_copy(
            src_ref=src, dst_ref=dst, send_sem=send, recv_sem=recv, device_id=device_id, device_id_type=MESH
        )

    def each(n, act):
        def body(k, carry):
            act(k)
            return carry

        lax.fori_loop(1, n, body, 0)

    class Sum:
        def __init__(self, tag):
            self.pay, self.from_core = R.pay[tag], R.others[tag]
            self.half, self.buf_xy, self.buf_z = R.half[tag], R.bxy[tag], R.bz[tag]
            self.res = R.res[tag]
            self.pair_sem, self.xy_sem = R.psem[tag], R.xysem[tag]
            self.z_sem = R.zsem[tag]
            partner = at(z, xy, 1 - core)
            self.pair = remote(
                self.pay.at[1 - core], self.from_core, self.pair_sem.at[0], self.pair_sem.at[1], partner
            )
            self.other = remote(
                self.res.at[core], self.res.at[core], self.pair_sem.at[2], self.pair_sem.at[3], partner
            )
            self.theirs = remote(
                self.res.at[1 - core], self.res.at[1 - core], self.pair_sem.at[2], self.pair_sem.at[3], partner
            )

        def xy_copy(self, k):
            p = xy_peer(k)
            return remote(
                self.half.at[p], self.buf_xy.at[xy], self.xy_sem.at[0, k], self.xy_sem.at[1, xy], at(z, p, core)
            )

        def xy_arrival(self, k):
            p = xy_peer(k)
            return remote(
                self.half.at[p], self.buf_xy.at[p], self.xy_sem.at[0, k], self.xy_sem.at[1, p], at(z, p, core)
            )

        def z_copy(self, k):
            here = self.buf_z.at[z]
            return remote(here, here, self.z_sem.at[0, k], self.z_sem.at[1, z], at(z_peer(k), xy, core))

        def z_arrival(self, k):
            p = z_peer(k)
            there = self.buf_z.at[p]
            return remote(there, there, self.z_sem.at[0, k], self.z_sem.at[1, p], at(p, xy, core))

        def back_copy(self, k):
            here = self.res.at[core, xy]
            return remote(here, here, self.xy_sem.at[2, k], self.xy_sem.at[3, xy], at(z, xy_peer(k), core))

        def back_arrival(self, k):
            p = xy_peer(k)
            there = self.res.at[core, p]
            return remote(there, there, self.xy_sem.at[2, k], self.xy_sem.at[3, p], at(z, p, core))

        def first(self):
            self.pair.start()

        def second(self):
            self.pair.wait()

            def add(p, carry):
                mine = self.pay[core, p].astype(F32)
                self.half[p] = (mine + self.from_core[p].astype(F32)).astype(BF)
                return carry

            lax.fori_loop(0, n_xy, add, 0)
            each(n_xy, lambda k: self.xy_copy(k).start())
            self.buf_xy[xy] = self.half[xy]

        def third(self):
            each(n_xy, lambda k: self.xy_arrival(k).wait_recv())
            total = self.buf_xy[0].astype(F32)
            for p in range(1, n_xy):
                total = total + self.buf_xy[p].astype(F32)
            self.buf_z[z] = total.astype(BF)
            each(n_z, lambda k: self.z_copy(k).start())

        def fourth(self):
            each(n_z, lambda k: self.z_arrival(k).wait_recv())
            total = self.buf_z[0].astype(F32)
            for p in range(1, n_z):
                total = total + self.buf_z[p].astype(F32)
            self.res[core, xy] = (total * scale).astype(BF)
            each(n_xy, lambda k: self.back_copy(k).start())

        def fifth(self):
            each(n_xy, lambda k: self.back_arrival(k).wait_recv())
            self.other.start()

        def sixth(self):
            self.theirs.wait_recv()

        def finish(self):
            self.other.wait_send()
            each(n_xy, lambda k: self.xy_copy(k).wait_send())
            each(n_xy, lambda k: self.back_copy(k).wait_send())
            each(n_z, lambda k: self.z_copy(k).wait_send())

    class LateSum:
        def __init__(self, tag):
            self.pay, self.buf_xy, self.buf_z = R.pay[tag], R.bxy[tag], R.bz[tag]
            self.res, self.xy_sem, self.z_sem = R.res[tag], R.xysem[tag], R.zsem[tag]
            self.here = z * 2 + core

        def xy_copy(self, k):
            p = xy_peer(k)
            sems = self.xy_sem.at[0, k], self.xy_sem.at[1, xy]
            return remote(self.pay.at[0, p], self.buf_xy.at[xy], *sems, at(z, p, core))

        def xy_arrival(self, k):
            p = xy_peer(k)
            sems = self.xy_sem.at[0, k], self.xy_sem.at[1, p]
            return remote(self.pay.at[0, p], self.buf_xy.at[p], *sems, at(z, p, core))

        def z_copy(self, k):
            p = lax.rem(self.here + k, 2 * n_z)
            mine = self.buf_z.at[self.here]
            sems = self.z_sem.at[0, k], self.z_sem.at[1, self.here]
            return remote(mine, mine, *sems, at(lax.div(p, 2), xy, lax.rem(p, 2)))

        def z_arrival(self, k):
            p = lax.rem(self.here + k, 2 * n_z)
            theirs = self.buf_z.at[p]
            sems = self.z_sem.at[0, k], self.z_sem.at[1, p]
            return remote(theirs, theirs, *sems, at(lax.div(p, 2), xy, lax.rem(p, 2)))

        def back_copy(self, k):
            mine = self.res.at[0, xy]
            sems = self.xy_sem.at[2, k], self.xy_sem.at[3, xy]
            return remote(mine, mine, *sems, at(z, xy_peer(k), core))

        def back_arrival(self, k):
            p = xy_peer(k)
            theirs = self.res.at[0, p]
            sems = self.xy_sem.at[2, k], self.xy_sem.at[3, p]
            return remote(theirs, theirs, *sems, at(z, p, core))

        def first(self):
            each(n_xy, lambda k: self.xy_copy(k).start())
            self.buf_xy[xy] = self.pay[0, xy]

        def second(self):
            each(n_xy, lambda k: self.xy_arrival(k).wait_recv())
            total = self.buf_xy[0].astype(F32)
            for p in range(1, n_xy):
                total = total + self.buf_xy[p].astype(F32)
            self.buf_z[self.here] = total.astype(BF)
            each(2 * n_z, lambda k: self.z_copy(k).start())

        def third(self):
            each(2 * n_z, lambda k: self.z_arrival(k).wait_recv())
            total = self.buf_z[0].astype(F32)
            for p in range(1, 2 * n_z):
                total = total + self.buf_z[p].astype(F32)
            self.res[0, xy] = (total * scale).astype(BF)
            each(n_xy, lambda k: self.back_copy(k).start())

        def fourth(self):
            each(n_xy, lambda k: self.back_arrival(k).wait_recv())

        def finish(self):
            each(n_xy, lambda k: self.xy_copy(k).wait_send())
            each(n_xy, lambda k: self.back_copy(k).wait_send())
            each(2 * n_z, lambda k: self.z_copy(k).wait_send())

    sum_a, sum_b = Sum(0), LateSum(1)

    barrier = pltpu.get_barrier_semaphore()

    def greet(device_id):
        pl.semaphore_signal(barrier, inc=1, device_id=device_id, device_id_type=MESH)

    for offset in OFFSETS[:6]:
        greet(device(offset))
    each(n_xy, lambda k: greet(at(z, xy_peer(k), core)))
    each(n_z, lambda k: greet(at(z_peer(k), xy, core)))
    each(n_z, lambda k: greet(at(z_peer(k), xy, 1 - core)))

    codes = [R.codes[0, s] for s in range(4)]
    tile_rows = iota((8, LANES), 0) & 3
    R.code_rows[...] = jnp.where(
        tile_rows == 0, codes[0], jnp.where(tile_rows == 1, codes[1], jnp.where(tile_rows == 2, codes[2], codes[3]))
    )
    dil = [R.dil[i] for i in range(4)]

    shifts = R.shifts
    for i, (_, _, _, W) in enumerate(LAYERS):
        shifts[i] = shift_matrix(W, dil[i])
    picks = R.picks
    PICK = {(16, 4): 0, (8, 4): 1, (8, 2): 2}
    for (H, m), where in PICK.items():
        _, col = column_pick(H, 128 if H == 16 else 64, m, codes[3], codes[2])
        picks[where] = take(LANES, col)

    def pick_rows(H, m):
        row, _ = column_pick(H, 128 if H == 16 else 64, m, codes[3], codes[2])
        return row

    for X3, D3, (C, O, H, _) in zip(R.x, R.d, LAYERS):
        D3[0 : 2 * RIM] = jnp.zeros((2 * RIM, 3 * O, LANES), BF)
        D3[2 * RIM + H : 4 * RIM + H] = jnp.zeros((2 * RIM, 3 * O, LANES), BF)
        X3[:, 3 * C : 3 * C + ONES, :] = jnp.ones((H + 2 * RIM, ONES, LANES), BF)

    def columns_of(x_ref, H, m, C):
        row = pick_rows(H, m)
        total = jnp.zeros((C, LANES), F32)
        for g in range(H // 4):
            y = mm(stacked(x_ref[4 * g : 4 * g + 4]), picks[PICK[(H, m)]])
            for q in range(4):
                total = total + jnp.where(row == 4 * g + q, y[q * C : (q + 1) * C], 0.0)
        return total

    def send_forward(name, x_ref, H, W, m, C):
        y = columns_of(x_ref, H, m, C)
        for side in range(2):
            R.cs[name][side] = pack(y, m * H, side == 1)
        both = jnp.concatenate([stacked(x_ref[0:m]), stacked(x_ref[H - m : H])], axis=1)
        for k, side in enumerate((1, 0)):
            rows = mm(both, pick_rows_matrix(W, codes[side]))
            R.rs[name][k] = pack_rows(rows.reshape(m, C, LANES), W)

    def halo_array(name, width, i):
        near = R.cr[name]
        low = iota((1, LANES), 1) < 64
        right, left = unpack(near[2 * i], width, False), unpack(near[2 * i + 1], width, True)
        return jnp.where(low, right, left).astype(BF)

    def halo_rows(Z, H, m, code, rows):
        mats = cat([take(LANES, halo_target(H, m, code, r)) for r in rows], 1)
        y = mm(Z, mats).astype(BF)
        return cat([y[:, LANES * q : LANES * (q + 1)] for q in range(len(rows))], 0)

    def fill(X3, r0, core, halo, C, S, offs, repeat):
        y = mm(jnp.concatenate([core, halo], axis=1), S).astype(BF)
        for q in range(core.shape[0] // C):
            part = slice(q * C, (q + 1) * C)
            for z in range(repeat):
                r = r0 + q * repeat + z
                X3[r, offs[0] : offs[0] + C, :] = y[part, :LANES]
                X3[r, offs[1] : offs[1] + C, :] = core[part]
                X3[r, offs[2] : offs[2] + C, :] = y[part, LANES:]

    def pad_and_shift(name, x_ref, H, m, C, layer, X3, offs, refine):
        arrive(name, slice(0, 2))
        Z = halo_array(name, H * m, 0)
        W = LANES * H // 16
        S = shifts[layer]
        rr = R.rr[name]
        code_u = R.code_near[0, 1:2, :]
        code_l = R.code_near[1, 0:1, :]
        rep = 2 if refine else 1

        def prepare(core, halo):
            if not refine:
                return core, halo
            w = iota((1, LANES), 1)
            core = mm(core, take(LANES, w >> 1)).astype(BF)
            near = jnp.where(w < 4, w >> 1, jnp.where(w >= LANES - 4, 64 + (w >> 1), -1))
            return core, mm(halo, take(LANES, near)).astype(BF)

        def body(g, carry):
            rows = [m * g + q for q in range(m)]
            core, halo = prepare(stacked(x_ref[pl.ds(m * g, m)]), halo_rows(Z, H, m, 0, rows))
            fill(X3, RIM + m * rep * g, core, halo, C, S, offs, rep)
            return carry

        lax.fori_loop(0, H // m, body, 0, unroll=True)
        arrive(name, slice(2, 8))
        Zu, Zl = halo_array(name, H * m, 1), halo_array(name, H * m, 2)
        core, halo = prepare(unpack_rows(rr[0], W), halo_rows(Zu, H, m, code_u, range(m)))
        fill(X3, 0, core, halo, C, S, offs, rep)
        core, halo = prepare(unpack_rows(rr[1], W), halo_rows(Zl, H, m, code_l, range(m)))
        fill(X3, RIM + H * rep, core, halo, C, S, offs, rep)

    def conv(Z3, width, K, d, rows, write, from_row=0):
        def body(i, carry):
            r = from_row + 2 * i
            taps = []
            for b in range(3):
                base = r + RIM + (b - 1) * d
                taps.append(
                    jnp.concatenate(
                        [Z3[base, 0:width, :], Z3[base + 1, 0:width, :]], axis=1
                    )
                )
            y = mm(K[...], jnp.concatenate(taps, axis=0))
            write(r, y[:, :LANES])
            write(r + 1, y[:, LANES:])
            return carry

        lax.fori_loop(0, rows // 2, body, 0, unroll=True)

    def weight_terms(X3, C, D3, O, d, rows, acc):
        n = 3 * C + ONES

        def body(i, carry):
            r = 4 * i
            lhs = jnp.concatenate([X3[r + q] for q in range(4)], axis=1)
            taps = []
            for a in range(3):
                base = r + RIM - (a - 1) * d
                taps.append(
                    jnp.concatenate([D3[base + q, O : 2 * O, :] for q in range(4)], axis=1)
                )
            if O == 64:
                taps.append(jnp.zeros((O, 4 * LANES), BF))
            y = mm_nt(lhs, jnp.concatenate(taps, axis=0))
            acc[0:n] = acc[0:n] + y
            return carry

        acc[0:n] = jnp.zeros((n, acc.shape[1]), F32)
        lax.fori_loop(0, rows // 4, body, 0, unroll=True)

    def spread_delta(x_ref, H, O, layer, D3):
        def body(g, carry):
            core = stacked(x_ref[pl.ds(4 * g, 4)])
            y = mm(core, shifts[layer, 0:LANES, :]).astype(BF)
            for q in range(4):
                part = slice(q * O, (q + 1) * O)
                D3[2 * RIM + 4 * g + q, 0:O, :] = y[part, :LANES]
                D3[2 * RIM + 4 * g + q, O : 2 * O, :] = core[part]
                D3[2 * RIM + 4 * g + q, 2 * O : 3 * O, :] = y[part, LANES:]
            return carry

        lax.fori_loop(0, H // 4, body, 0, unroll=True)

    def rims_of(x_ref, H, W, O, layer, K):
        row, col = column_pick(H, W, RIM, 1, 0)
        pick = take(LANES, col)
        edges = jnp.zeros((O, LANES), F32)
        for g in range(H // 4):
            y = mm(stacked(x_ref[4 * g : 4 * g + 4]), pick)
            for q in range(4):
                edges = edges + jnp.where(row == 4 * g + q, y[q * O : (q + 1) * O], 0.0)
        e = mm(edges.astype(BF), edge_matrix(H, dil[layer])).astype(BF)
        none = jnp.zeros((O, LANES), BF)
        blocks = []
        for b in range(3):
            a = 2 - b
            right = e[:, 2 * a * LANES : (2 * a + 1) * LANES]
            left = e[:, (2 * a + 1) * LANES : (2 * a + 2) * LANES]
            blocks.append(jnp.concatenate([right, none], axis=1))
            blocks.append(jnp.zeros((O, 2 * LANES), BF))
            blocks.append(jnp.concatenate([none, left], axis=1))
        return mm(K[...], jnp.concatenate(blocks, axis=0)).astype(BF)

    def send_backward(name, rims, G, c0, C, H, m, collapse=False):
        code_u = R.code_near[0, 1:2, :]
        code_l = R.code_near[1, 0:1, :]
        y = mm(rims, rim_matrix(H, m, code_u, code_l, collapse))
        for slot, k in enumerate((0, 0, 2, 2, 1, 1)):
            R.cs[name][slot] = pack(y[:, k * LANES : (k + 1) * LANES], H * m, slot % 2 == 0)
        W = LANES * H // 16
        R.rs[name][0] = pack_rows(G[H + m : H + 2 * m, c0 : c0 + C, :], W)
        R.rs[name][1] = pack_rows(G[0:m, c0 : c0 + C, :], W)

    def fold(name, G, c0, C, H, W, m, write):
        near = R.cr[name]
        rr = R.rr[name]
        low = iota((1, LANES), 1) < 64
        to_right, to_left = (
            near[i].astype(F32) + near[i + 2].astype(F32) + near[i + 4].astype(F32) for i in (1, 0)
        )
        back = jnp.where(low, unpack(to_right, H * m, False), unpack(to_left, H * m, True))
        row = pick_rows(H, m)
        both = jnp.concatenate([unpack_rows(rr[0], W), unpack_rows(rr[1], W)], axis=1)
        first = mm(both, return_rows_matrix(W, codes[0], codes[1], 0))
        last = mm(both, return_rows_matrix(W, codes[0], codes[1], 1))
        pick = picks[PICK[(H, m)]]
        for g in range(H // m):
            masked = [jnp.where(row == m * g + q, back, 0.0).astype(BF) for q in range(m)]
            y = mm_nt(cat(masked, 0), pick)
            if g == 0:
                y = y + first
            if g == H // m - 1:
                y = y + last
            for q in range(m):
                h = m * g + q
                write(h, G[h + m, c0 : c0 + C, :] + y[q * C : (q + 1) * C])

    def forward_weights(i):
        k, kf = R.k[i], R.kf[i]
        if i == 1:
            for t in range(0, 9, 2):
                block = k[8] if t == 8 else jnp.concatenate([k[t], k[t + 1]], axis=0)
                kf[:, t * 64 : t * 64 + block.shape[0]] = mm_nt(eye(LANES), block).astype(BF)
            return
        C = k.shape[2]
        for t in range(0, 9, 2):
            block = k[t] if t == 8 else jnp.concatenate([k[t], k[t + 1]], axis=1)
            kf[:, t * C : t * C + block.shape[1]] = block

    def backward_weights(i):
        k, kt = R.k[i], R.kt[i]
        if i == 1:
            for t in range(9):
                kt[:, t * LANES : (t + 1) * LANES] = k[8 - t]
            return
        O, C = k.shape[1], k.shape[2]
        for t in range(0, 9, 2):
            block = k[0] if t == 8 else jnp.concatenate([k[8 - t], k[7 - t]], axis=0)
            kt[:, t * O : t * O + block.shape[0]] = mm_nt(eye(C), block).astype(BF)

    def column(i):
        row = R.off[i][...]
        n = row.shape[1]
        return jnp.sum(jnp.where(iota((n, n), 0) == iota((n, n), 1), row, 0.0), axis=1, keepdims=True)

    def rows_first(x_ref, out):
        turn = to_rows()
        for g in range(4):
            y = mm(turn, stacked(x_ref[16 * g : 16 * g + 16])).astype(BF)
            for h in range(16):
                out[h, 16 * g : 16 * g + 16, :] = y[16 * h : 16 * h + 16]

    def put(ref, start_row, value):
        q = ref.shape[2]
        done = 0
        while done < value.shape[0]:
            piece, inner = divmod(start_row + done, q)
            n = min(q - inner, value.shape[0] - done)
            ref[piece // n_xy, piece % n_xy, inner : inner + n, :] = value[done : done + n].astype(BF)
            done += n

    def put_terms(ref, listed):
        where = 0
        for acc, C, O in listed:
            chunks = 2 if O == 64 else 3
            for k in range(chunks):
                put(ref, where, acc[0 : 3 * C, k * LANES : (k + 1) * LANES])
                where += 3 * C
        for acc, C, O in listed:
            k = 0 if O == 64 else 1
            put(ref, where, acc[3 * C : 3 * C + ONES, k * LANES : (k + 1) * LANES])
            where += ONES
        pieces = ref.shape[0] * ref.shape[1] * ref.shape[2]
        put(ref, where, jnp.zeros((pieces - where, LANES), BF))

    rows_first(R.fields_in, R.fields)
    send_forward(FIELDS, R.fields, 16, 128, 4, 64)
    pl.semaphore_wait(barrier, 6 + (n_xy - 1) + 2 * (n_z - 1))
    for copy in code_copies:
        copy.start()
    start(FIELDS)

    forward_weights(0)
    cot = R.cot
    rows_first(R.cot_in, cot)
    backward_weights(3)
    spread_delta(cot, 16, 64, 3, R.d[3])
    G4 = R.g[3]

    def write_g4(r, v):
        G4[r] = v

    conv(R.d[3], 192, R.kt[3], dil[3], 24, write_g4)
    for i in (1, 2, 3):
        forward_weights(i)
    for i in (2, 1, 0):
        backward_weights(i)
    columns = [column(i) for i in range(4)]

    for copy in code_copies:
        copy.wait_recv()
    pad_and_shift(FIELDS, R.fields, 16, 4, 64, 0, R.x[0], (0, 64, 128), False)
    first_act, slope1 = R.first_act, R.slope1

    def write_first(r, v):
        act, slope = gelu_and_slope(v + columns[0])
        first_act[r] = act.astype(BF)
        slope1[r] = slope

    conv(R.x[0], 192, R.kf[0], dil[0], 16, write_first)
    pooled = R.pooled
    u, w = iota((2 * LANES, LANES), 0), iota((2 * LANES, LANES), 1)
    quarter = jnp.where(((u & (LANES - 1)) >> 1) == w, 0.25, 0.0).astype(BF)
    for g in range(2):
        lhs = cat(
            [
                jnp.concatenate([first_act[8 * g + 2 * q], first_act[8 * g + 2 * q + 1]], axis=1)
                for q in range(4)
            ],
            0,
        )
        pooled[4 * g : 4 * g + 4] = mm(lhs, quarter).astype(BF).reshape(4, 64, LANES)
    send_forward(POOLED, pooled, 8, 64, 4, 64)
    start(POOLED)
    send_forward(FIRST, first_act, 16, 128, 4, 64)
    rims4 = rims_of(cot, 16, 128, 64, 3, R.kt[3])
    G4c = R.g4c
    pool = onehot(((u & (LANES - 1)) >> 1) == w)
    for g in range(3):
        pairs = [G4[8 * g + 2 * q, 0:128, :] + G4[8 * g + 2 * q + 1, 0:128, :] for q in range(4)]
        y = mm(split(cat(pairs, 0)), pool)
        G4c[4 * g : 4 * g + 4] = y.reshape(4, 128, LANES)
    send_backward(BACK4C, rims4[0:128], G4c, 0, 128, 8, 2, True)
    send_backward(BACK4F, rims4[128:192], G4, 128, 64, 16, 4)


    pad_and_shift(POOLED, pooled, 8, 4, 64, 1, R.x[1], (0, 64, 128), False)
    start(FIRST)
    start(BACK4C)
    second_act, slope2 = R.second_act, R.slope2
    inside = iota((1, LANES), 1) < 64

    def write_second(r, v):
        act, slope = gelu_and_slope(v + columns[1])
        second_act[r] = jnp.where(inside, act, 0.0).astype(BF)
        slope2[r] = jnp.where(inside, slope, 0.0)

    conv(R.x[1], 192, R.kf[1], dil[1], 8, write_second)
    send_forward(SECOND, second_act, 8, 64, 4, 128)
    start(SECOND)

    arrive(BACK4C)
    coarse, skip = R.coarse, R.skip

    def write_coarse(r, v):
        coarse[r] = v

    def write_skip(r, v):
        skip[r] = v

    fold(BACK4C, G4c, 0, 128, 8, 64, 2, write_coarse)


    pad_and_shift(FIRST, first_act, 16, 4, 64, 3, R.x[3], (128, 320, 512), False)

    pad_and_shift(SECOND, second_act, 8, 4, 128, 2, R.x[2], (0, 128, 256), False)
    start(BACK4F)
    third_act, delta3 = R.third_act, R.delta3

    def write_third(r, v):
        act, slope = gelu_and_slope(v + columns[2])
        third_act[r] = jnp.where(inside, act, 0.0).astype(BF)
        delta3[r] = jnp.where(inside, coarse[r] * slope, 0.0).astype(BF)

    conv(R.x[2], 384, R.kf[2], dil[2], 8, write_third)
    send_forward(THIRD, third_act, 8, 64, 2, 128)
    start(THIRD)
    spread_delta(delta3, 8, 128, 2, R.d[2])
    G3 = R.g[2]

    def write_g3(r, v):
        G3[r] = v

    conv(R.d[2], 384, R.kt[2], dil[2], 4, write_g3)
    conv(R.d[2], 384, R.kt[2], dil[2], 4, write_g3, 12)
    send_backward(BACK3, rims_of(delta3, 8, 64, 128, 2, R.kt[2]), G3, 0, 128, 8, 4)
    start(BACK3)
    conv(R.d[2], 384, R.kt[2], dil[2], 8, write_g3, 4)


    weight_terms(R.x[2], 128, R.d[2], 128, dil[2], 16, R.w[2])
    arrive(BACK4F)
    fold(BACK4F, G4, 128, 64, 16, 128, 4, write_skip)
    pad_and_shift(THIRD, third_act, 8, 2, 128, 3, R.x[3], (0, 192, 384), True)

    weight_terms(R.x[3], 192, R.d[3], 64, dil[3], 24, R.w[3])
    put_terms(R.pay[0], ((R.w[3], 192, 64), (R.w[2], 128, 128)))
    sum_a.first()
    arrive(BACK3)
    delta2 = R.delta2

    def write_delta2(r, v):
        delta2[r] = (v * slope2[r]).astype(BF)

    fold(BACK3, G3, 0, 128, 8, 64, 4, write_delta2)
    spread_delta(delta2, 8, 128, 1, R.d[1])
    G2 = R.g[1]

    def write_g2(r, v):
        G2[r] = v

    conv(R.d[1], 384, R.kt[1], dil[1], 4, write_g2)
    conv(R.d[1], 384, R.kt[1], dil[1], 4, write_g2, 12)
    send_backward(BACK2, rims_of(delta2, 8, 64, 128, 1, R.kt[1]), G2, 0, 64, 8, 4)
    start(BACK2)
    conv(R.d[1], 384, R.kt[1], dil[1], 8, write_g2, 4)

    state = R.state

    def write_state(r, v):
        state[r] = (v + columns[3]).astype(BF)


    weight_terms(R.x[1], 64, R.d[1], 128, dil[1], 16, R.w[1])
    sum_a.second()
    conv(R.x[3], 576, R.kf[3], dil[3], 8, write_state)
    arrive(BACK2)
    delta1 = R.delta1
    repeat = jnp.where((u & (LANES - 1)) == (w >> 1), 0.25, 0.0).astype(BF)

    def write_delta1(r, v):
        wide = mm(split(v), repeat)
        for z in range(2):
            delta1[2 * r + z] = ((skip[2 * r + z] + wide) * slope1[2 * r + z]).astype(BF)

    fold(BACK2, G2, 0, 64, 8, 64, 4, write_delta1)
    spread_delta(delta1, 16, 64, 0, R.d[0])
    weight_terms(R.x[0], 64, R.d[0], 64, dil[0], 24, R.w[0])
    put_terms(R.pay[1], ((R.w[1], 64, 128), (R.w[0], 64, 64)))
    sum_b.first()
    G1 = R.g[0]

    def write_g1(r, v):
        G1[r] = v

    conv(R.d[0], 192, R.kt[0], dil[0], 4, write_g1)
    conv(R.d[0], 192, R.kt[0], dil[0], 4, write_g1, 20)
    send_backward(BACK1, rims_of(delta1, 16, 128, 64, 0, R.kt[0]), G1, 0, 64, 16, 4)
    start(BACK1)
    sum_a.third()
    conv(R.d[0], 192, R.kt[0], dil[0], 16, write_g1, 4)
    sum_b.second()
    conv(R.x[3], 576, R.kf[3], dil[3], 8, write_state, 8)
    sum_a.fourth()
    arrive(BACK1)
    grad = R.grad

    def write_grad(r, v):
        grad[r] = v

    fold(BACK1, G1, 0, 64, 16, 128, 4, write_grad)
    sum_b.third()
    sum_a.fifth()
    sum_b.fourth()
    sum_a.sixth()

    sum_a.finish()
    sum_b.finish()
    for listed in (*copies, code_copies):
        for copy in listed:
            copy.wait_send()


PIECE = (80, 64)


def run_net(tiles, members, scale, operands):
    V, D = pltpu.VMEM, pltpu.SemaphoreType.DMA
    n_xy, n_z = tiles // 8, members * 4
    sizes = [(C, O, H + 2 * RIM) for C, O, H, _ in LAYERS]
    scratch = Refs(
        shifts=V((4, 256, 256), BF),
        picks=V((3, LANES, LANES), BF),
        x=[V((P_, 3 * C + ONES, LANES), BF) for C, O, P_ in sizes],
        d=[V((P_ + 2 * RIM, 3 * O, LANES), BF) for C, O, P_ in sizes],
        g=[V((P_, C, LANES), F32) for C, O, P_ in sizes],
        g4c=V((12, 128, LANES), F32),
        kf=[V((O, 9 * C), BF) for C, O, _ in sizes],
        kt=[V((C, 9 * O), BF) for C, O, _ in sizes],
        w=[V((3 * C + ONES, 256 if O == 64 else 384), F32) for C, O, _ in sizes],
        fields=V((16, 64, LANES), BF),
        cot=V((16, 64, LANES), BF),
        first_act=V((16, 64, LANES), BF),
        slope1=V((16, 64, LANES), F32),
        pooled=V((8, 64, LANES), BF),
        second_act=V((8, 128, LANES), BF),
        slope2=V((8, 128, LANES), F32),
        third_act=V((8, 128, LANES), BF),
        coarse=V((8, 128, LANES), F32),
        skip=V((16, 64, LANES), F32),
        delta1=V((16, 64, LANES), BF),
        delta2=V((8, 128, LANES), BF),
        delta3=V((8, 128, LANES), BF),
        code_rows=V((8, LANES), jnp.int32),
        code_near=V((2, 8, LANES), jnp.int32),
        send=D((len(EXCHANGES), 8)),
        recv=D((len(EXCHANGES), 8)),
        send_code=D((2,)),
        recv_code=D((2,)),
        pay=[V((2 - i, n_xy, q, LANES), BF) for i, q in enumerate(PIECE)],
        others=[V((n_xy, PIECE[0], LANES), BF)],
        half=[V((n_xy, PIECE[0], LANES), BF)],
        bxy=[V((n_xy, q, LANES), BF) for q in PIECE],
        bz=[V((n_z * (i + 1), q, LANES), BF) for i, q in enumerate(PIECE)],
        psem=[D((4,))],
        xysem=[D((4, n_xy)) for q in PIECE],
        zsem=[D((2, n_z * (i + 1))) for i, q in enumerate(PIECE)],
        cs=[V((sent, C * m * H // LANES, LANES), BF) for C, m, H, sent in EXCHANGES],
        rs=[V((2, m * H // 16, C, LANES), BF) for C, m, H, sent in EXCHANGES],
        cr=[V((6, C * m * H // LANES, LANES), BF) for C, m, H, sent in EXCHANGES],
        rr=[V((2, m * H // 16, C, LANES), BF) for C, m, H, sent in EXCHANGES],
    )
    smem = pl.BlockSpec(memory_space=pltpu.SMEM)
    vmem = pl.BlockSpec(memory_space=pltpu.VMEM)
    shape = jax.ShapeDtypeStruct
    outputs = Refs(
        state=shape((16, 64, LANES), BF),
        grad=shape((16, 64, LANES), F32),
        res=[shape((2 - i, n_xy, q, LANES), BF) for i, q in enumerate(PIECE)],
    )
    inputs = Refs(**operands)
    flat_in, flat_out, flat_scratch = (list(flatten(part)) for part in (inputs, outputs, scratch))
    return pl.pallas_call(
        functools.partial(net_kernel, tiles, members, scale, (inputs, outputs, scratch)),
        out_shape=tuple(flat_out),
        in_specs=[smem if v.dtype == jnp.int32 else vmem for v in flat_in],
        out_specs=(vmem,) * len(flat_out),
        scratch_shapes=flat_scratch,
        compiler_params=pltpu.CompilerParams(
            collective_id=0, has_side_effects=True, vmem_limit_bytes=56 * 2**20
        ),
    )(*flat_in)

def finish_kernel(state, grad, early, late, state_out, grad_out, w1, w2, w3, w4, b1, b2, b3, b4):
    channels_first(state, state_out, 1)
    channels_first(grad, grad_out, 2)
    take_terms(early, ((w4, b4, 192, 64), (w3, b3, 128, 128)))
    take_terms(late, ((w2, b2, 64, 128), (w1, b1, 64, 64)))


def run_finish(raw):
    vmem = pl.BlockSpec(memory_space=pltpu.VMEM)
    shape = jax.ShapeDtypeStruct
    outputs = [shape((64, 16, LANES), BF), shape((64, 16, LANES), F32)]
    outputs += [shape((9, C, O) if O > C else (9, O, C), F32) for C, O, _, _ in LAYERS]
    outputs += [shape((1, O), F32) for C, O, _, _ in LAYERS]
    return pl.pallas_call(
        finish_kernel,
        out_shape=tuple(outputs),
        in_specs=[vmem] * len(raw),
        out_specs=(vmem,) * len(outputs),
        compiler_params=pltpu.CompilerParams(vmem_limit_bytes=56 * 2**20),
    )(*raw)


def shards(tiles, members, fields, cotangent, k1, k2, k3, k4, off1, off2, off3, off4, codes, dilations):
    operands = dict(
        codes=codes,
        dil=dilations,
        fields_in=fields[0, 0],
        cot_in=cotangent[0, 0],
        k=[k1, jnp.swapaxes(k2, 1, 2), k3, k4],
        off=[off1[None, :], off2[None, :], off3[None, :], off4[None, :]],
    )
    scale = 1.0 / math.sqrt(members * tiles * fields.shape[3] * fields.shape[4])
    state, grad, *rest = run_finish(run_net(tiles, members, scale, operands))
    rest[1] = jnp.swapaxes(rest[1], 1, 2)
    return (state[None, None], grad[None, None], *rest[:4], *[b[0] for b in rest[4:]])


def solution(mesh):
    big = P("ens", "tile", None, None, None)
    in_specs = (big, big) + (P(),) * 8 + (P("tile", None), P())
    out_specs = (big, big) + (P(),) * 8
    body = functools.partial(shards, mesh.shape["tile"], mesh.shape["ens"])
    return jax.shard_map(body, mesh=mesh, in_specs=in_specs, out_specs=out_specs, check_vma=False)
```

```python
import functools
import math

import jax
import jax.numpy as jnp
from jax import lax
from jax.experimental import pallas as pl
from jax.experimental.pallas import tpu as pltpu
from jax.sharding import PartitionSpec as P

MESH = pl.DeviceIdType.MESH
BF = jnp.bfloat16
F32 = jnp.float32

RIM = 4
TILE_ROW = 8
LANES = 128
ONES = 16

FIELDS, POOLED, FIRST, SECOND, THIRD, BACK4C, BACK4F, BACK3, BACK2, BACK1 = range(10)
EXCHANGES = (
    (64, 4, 16, 2),
    (64, 4, 8, 2),
    (64, 4, 16, 2),
    (128, 4, 8, 2),
    (128, 2, 8, 2),
    (128, 2, 8, 6),
    (64, 4, 16, 6),
    (128, 4, 8, 6),
    (64, 4, 8, 6),
    (64, 4, 16, 6),
)
OFFSETS = (1, -1, 9, 7, -7, -9, 8, -8)
LAYERS = ((64, 64, 16, 128), (64, 128, 8, 64), (128, 128, 8, 64), (192, 64, 16, 128))


def iota(shape, dim):
    return lax.broadcasted_iota(jnp.int32, shape, dim)


def onehot(cond):
    return jnp.where(cond, 1.0, 0.0).astype(BF)


def mm(a, b):
    return jnp.dot(a, b, preferred_element_type=F32)


def mm_nt(a, b):
    return lax.dot_general(a, b, (((1,), (1,)), ((), ())), preferred_element_type=F32)


def split(values):
    high = values.astype(BF)
    low = (values - high.astype(F32)).astype(BF)
    return jnp.concatenate([high, low], axis=-1)


def cat(parts, axis):
    return parts[0] if len(parts) == 1 else jnp.concatenate(parts, axis=axis)


def log2(m):
    return m.bit_length() - 1


def column_pick(H, W, m, code_right, code_left):
    lane = iota((1, LANES), 1)
    code = jnp.where(lane < 64, code_right, code_left)
    idx = lane & 63
    row, col = idx >> log2(m), idx & (m - 1)
    col = jnp.where((code & 1) == 1, W - m + col, col)
    row = jnp.where((code >> 1) == 1, H - 1 - row, row)
    valid = idx < H * m
    return jnp.where(valid, row, -1), jnp.where(valid, col, -1)


def halo_target(H, m, code, row):
    w = iota((1, LANES), 1)
    picked = jnp.where((code & 1) == 1, H - m + row, row)
    flip = (code >> 1) == 1
    k = w - (LANES - m)
    left = jnp.where(flip, 64 + m * picked + (m - 1 - k), m * picked + k)
    right = jnp.where(flip, m * picked + (m - 1 - w), 64 + m * picked + w)
    return jnp.where(w >= LANES - m, left, jnp.where(w < m, right, -1))


def take(rows, target):
    return onehot(iota((rows, target.shape[1]), 0) == target)


def shift_matrix(W, d):
    out = iota((1, 2 * LANES), 1)
    j = out & (LANES - 1)
    minus = jnp.where(j >= d, j - d, 2 * LANES + j - d)
    plus = jnp.where(j + d < W, j + d, LANES + j + d - W)
    target = jnp.where(out < LANES, minus, plus)
    return take(2 * LANES, jnp.where(j < W, target, -1))


def turned(W, code):
    w = iota((1, LANES), 1)
    return jnp.where(w < W, jnp.where((code >> 1) == 1, W - 1 - w, w), -1024)


def pick_rows_matrix(W, code):
    return take(2 * LANES, turned(W, code) + LANES * (code & 1))


def return_rows_matrix(W, code_upper, code_lower, last):
    parts = []
    for code in (code_upper, code_lower):
        parts.append(take(LANES, jnp.where((code & 1) == last, turned(W, code), -1)))
    return jnp.concatenate(parts, axis=0)


def rim_matrix(H, m, code_above, code_below, collapse):
    shape = (2 * LANES, LANES)
    u, lane = iota(shape, 0), iota((1, LANES), 1)
    src = u
    if collapse:
        src = (((u & (LANES - 1)) >> 3) << 1) + ((u & 3) >> 1) + ((u >> 7) << 7)
    idx = lane & 63
    row, k = idx >> log2(m), idx & (m - 1)
    leftward = lane < 64
    valid = idx < H * m
    targets = [jnp.where(valid, (row + m) * m + k + jnp.where(leftward, LANES, 0), -1)]
    for code, base in ((code_above, 0), (code_below, H + m)):
        picked = jnp.where((code & 1) == 1, row - (H - m), row)
        flip = (code >> 1) & 1
        kk = jnp.where(flip == 1, m - 1 - k, k)
        left_side = jnp.where(leftward, 1 - flip, flip)
        inside = valid & (picked >= 0) & (picked < m)
        targets.append(jnp.where(inside, (picked + base) * m + kk + left_side * LANES, -1))
    return jnp.concatenate([onehot(src == target) for target in targets], axis=1)


def edge_matrix(H, d):
    v = iota((1, LANES), 1)
    row, k = v >> 2, v & 3
    parts = []
    for a in range(3):
        h = row - RIM - (a - 1) * d
        inside = (h >= 0) & (h < H)
        parts.append(take(LANES, jnp.where(inside & (k < d), 4 * h + (4 - d + k), -1)))
        parts.append(take(LANES, jnp.where(inside & (k >= 4 - d), 64 + 4 * h + (k - 4 + d), -1)))
    return jnp.concatenate(parts, axis=1)


def gelu_and_slope(x):
    cdf = 0.5 + 0.5 * lax.erf(x * math.sqrt(0.5))
    pdf = jnp.exp(-0.5 * x * x) * (1.0 / math.sqrt(2.0 * math.pi))
    return x * cdf, cdf + x * pdf


def stacked(values):
    return values.reshape(values.shape[0] * values.shape[1], values.shape[2])


def eye(n):
    return onehot(iota((n, n), 0) == iota((n, n), 1))


def to_rows():
    u, w = iota((256, 256), 0), iota((256, 256), 1)
    return onehot(w == ((u & 15) << 4) + (u >> 4))


def channels_first(x_ref, out, parts):
    turn = to_rows()
    for g in range(4):
        block = cat([x_ref[h, 16 * g : 16 * g + 16, :] for h in range(16)], 0)
        y = mm(turn, block) if parts == 1 else mm(turn, split(block))
        if parts == 2:
            y = y[:, :LANES] + y[:, LANES:]
        out[16 * g : 16 * g + 16] = y.astype(out.dtype).reshape(16, 16, LANES)


def get(ref, start_row, count):
    n_xy, q = ref.shape[1], ref.shape[2]
    parts, done = [], 0
    while done < count:
        piece, inner = divmod(start_row + done, q)
        n = min(q - inner, count - done)
        parts.append(ref[piece // n_xy, piece % n_xy, inner : inner + n, :])
        done += n
    return cat(parts, 0)


def take_terms(ref, listed):
    sel = [onehot(iota((64, LANES), 1) == iota((64, LANES), 0) + 64 * k) for k in range(2)]
    where = 0
    for w_out, b_out, C, O in listed:
        for a in range(3):
            chunk, side = (a // 2, sel[a % 2]) if O == 64 else (a, eye(LANES))
            for e in range(3):
                block = get(ref, where + chunk * 3 * C + e * C, C)
                w_out[3 * a + e] = block.astype(F32) if O > C else mm_nt(side, block)
        where += (2 if O == 64 else 3) * 3 * C
    for w_out, b_out, C, O in listed:
        block = get(ref, where, ONES)
        b_out[...] = mm_nt(block, sel[1])[0:1] if O == 64 else block.astype(F32)[0:1]
        where += ONES


class Refs:
    def __init__(self, **parts):
        self.__dict__.update(parts)


def flatten(part):
    for value in part.__dict__.values():
        yield from value if type(value) is list else [value]


def fill_in(parts, refs):
    named = {}
    for part in parts:
        for key, value in part.__dict__.items():
            named[key] = [next(refs) for _ in value] if type(value) is list else next(refs)
    return named


def pack(y, width, left):
    groups = LANES // width
    n = y.shape[0] // groups
    group = iota((1, LANES), 1) >> log2(width)
    out = jnp.zeros((n, LANES), F32)
    for g in range(groups):
        by = (g * width - (64 if left else 0)) % LANES
        part = y[g * n : (g + 1) * n]
        out = jnp.where(group == g, pltpu.roll(part, by, 1) if by else part, out)
    return out.astype(BF)


def unpack(p, width, left):
    p = p.astype(F32)
    parts = []
    for g in range(LANES // width):
        by = ((64 if left else 0) - g * width) % LANES
        parts.append(pltpu.roll(p, by, 1) if by else p)
    return jnp.concatenate(parts, axis=0)


def pack_rows(rows, W):
    if W == LANES:
        return rows.astype(BF)
    n, C, _ = rows.shape
    second = pltpu.roll(stacked(rows[n // 2 :]), 64, 1)
    return (stacked(rows[: n // 2]) + second).astype(BF).reshape(n // 2, C, LANES)


def unpack_rows(x, W):
    x = stacked(x)
    if W == LANES:
        return x
    return jnp.concatenate([x, pltpu.roll(x.astype(F32), 64, 1).astype(BF)], axis=0)


def net_kernel(tiles, members, scale, tree, *refs):
    R = Refs(**fill_in(tree, iter(refs)))
    tile = lax.axis_index("tile")
    ens = lax.axis_index("ens")

    def device(offset):
        return (ens, lax.rem(tile + (offset + tiles), tiles))

    brought = [
        pltpu.make_async_copy(there, here, R.bring.at[i])
        for i, (there, here) in enumerate(zip(R.far + R.k_far, R.near + R.k))
    ]
    for copy in brought:
        copy.start()

    copies = []
    for x, (C, m, H, sent) in enumerate(EXCHANGES):
        listed = []
        for slot, offset in enumerate(OFFSETS):
            if slot < 6:
                which = slot % sent
                src = R.cs[x].at[which]
                dst = R.cr[x].at[slot]
            else:
                src = R.rs[x].at[slot - 6]
                dst = R.rr[x].at[slot - 6]
            listed.append(
                pltpu.make_async_remote_copy(
                    src_ref=src,
                    dst_ref=dst,
                    send_sem=R.send.at[x, slot],
                    recv_sem=R.recv.at[x, slot],
                    device_id=device(offset),
                    device_id_type=MESH,
                )
            )
        copies.append(listed)
    code_copies = [
        pltpu.make_async_remote_copy(
            src_ref=R.code_rows,
            dst_ref=R.code_near.at[k],
            send_sem=R.send_code.at[k],
            recv_sem=R.recv_code.at[k],
            device_id=device(offset),
            device_id_type=MESH,
        )
        for k, offset in enumerate((8, -8))
    ]

    def start(name):
        for copy in copies[name]:
            copy.start()

    def arrive(name, slots=slice(0, 8)):
        for copy in copies[name][slots]:
            copy.wait_recv()

    n_ens, n_low = members, 4
    n_xy, n_z = tiles // (2 * n_low), n_ens * n_low
    xy = lax.div(tile, 2 * n_low)
    low = lax.div(lax.rem(tile, 2 * n_low), 2)
    core = lax.rem(tile, 2)
    z = ens * n_low + low

    def at(z_, xy_, core_):
        return (lax.div(z_, n_low), (xy_ * n_low + lax.rem(z_, n_low)) * 2 + core_)

    def xy_peer(k):
        return lax.rem(xy + k, n_xy)

    def z_peer(k):
        return lax.rem(z + k, n_z)

    def remote(src, dst, send, recv, device_id):
        return pltpu.make_async_remote_copy(
            src_ref=src, dst_ref=dst, send_sem=send, recv_sem=recv, device_id=device_id, device_id_type=MESH
        )

    def each(n, act):
        def body(k, carry):
            act(k)
            return carry

        lax.fori_loop(1, n, body, 0)

    class Sum:
        def __init__(self, tag):
            self.pay, self.from_core = R.pay[tag], R.others[tag]
            self.half, self.buf_xy, self.buf_z = R.half[tag], R.bxy[tag], R.bz[tag]
            self.res = R.res[tag]
            self.pair_sem, self.xy_sem = R.psem[tag], R.xysem[tag]
            self.z_sem = R.zsem[tag]
            partner = at(z, xy, 1 - core)
            self.pair = remote(
                self.pay.at[1 - core], self.from_core, self.pair_sem.at[0], self.pair_sem.at[1], partner
            )
            self.other = remote(
                self.res.at[core], self.res.at[core], self.pair_sem.at[2], self.pair_sem.at[3], partner
            )
            self.theirs = remote(
                self.res.at[1 - core], self.res.at[1 - core], self.pair_sem.at[2], self.pair_sem.at[3], partner
            )

        def xy_copy(self, k):
            p = xy_peer(k)
            return remote(
                self.half.at[p], self.buf_xy.at[xy], self.xy_sem.at[0, k], self.xy_sem.at[1, xy], at(z, p, core)
            )

        def xy_arrival(self, k):
            p = xy_peer(k)
            return remote(
                self.half.at[p], self.buf_xy.at[p], self.xy_sem.at[0, k], self.xy_sem.at[1, p], at(z, p, core)
            )

        def z_copy(self, k):
            here = self.buf_z.at[z]
            return remote(here, here, self.z_sem.at[0, k], self.z_sem.at[1, z], at(z_peer(k), xy, core))

        def z_arrival(self, k):
            p = z_peer(k)
            there = self.buf_z.at[p]
            return remote(there, there, self.z_sem.at[0, k], self.z_sem.at[1, p], at(p, xy, core))

        def back_copy(self, k):
            here = self.res.at[core, xy]
            return remote(here, here, self.xy_sem.at[2, k], self.xy_sem.at[3, xy], at(z, xy_peer(k), core))

        def back_arrival(self, k):
            p = xy_peer(k)
            there = self.res.at[core, p]
            return remote(there, there, self.xy_sem.at[2, k], self.xy_sem.at[3, p], at(z, p, core))

        def first(self):
            self.pair.start()

        def second(self):
            self.pair.wait()

            def add(p, carry):
                mine = self.pay[core, p].astype(F32)
                self.half[p] = (mine + self.from_core[p].astype(F32)).astype(BF)
                return carry

            lax.fori_loop(0, n_xy, add, 0)
            each(n_xy, lambda k: self.xy_copy(k).start())
            self.buf_xy[xy] = self.half[xy]

        def third(self):
            each(n_xy, lambda k: self.xy_arrival(k).wait_recv())
            total = self.buf_xy[0].astype(F32)
            for p in range(1, n_xy):
                total = total + self.buf_xy[p].astype(F32)
            self.buf_z[z] = total.astype(BF)
            each(n_z, lambda k: self.z_copy(k).start())

        def fourth(self):
            each(n_z, lambda k: self.z_arrival(k).wait_recv())
            total = self.buf_z[0].astype(F32)
            for p in range(1, n_z):
                total = total + self.buf_z[p].astype(F32)
            self.res[core, xy] = (total * scale).astype(BF)
            each(n_xy, lambda k: self.back_copy(k).start())

        def fifth(self):
            each(n_xy, lambda k: self.back_arrival(k).wait_recv())
            self.other.start()

        def sixth(self):
            self.theirs.wait_recv()

        def finish(self):
            self.other.wait_send()
            each(n_xy, lambda k: self.xy_copy(k).wait_send())
            each(n_xy, lambda k: self.back_copy(k).wait_send())
            each(n_z, lambda k: self.z_copy(k).wait_send())

    class LateSum:
        def __init__(self, tag):
            self.pay, self.buf_xy, self.buf_z = R.pay[tag], R.bxy[tag], R.bz[tag]
            self.res, self.xy_sem, self.z_sem = R.res[tag], R.xysem[tag], R.zsem[tag]
            self.here = z * 2 + core

        def xy_copy(self, k):
            p = xy_peer(k)
            sems = self.xy_sem.at[0, k], self.xy_sem.at[1, xy]
            return remote(self.pay.at[0, p], self.buf_xy.at[xy], *sems, at(z, p, core))

        def xy_arrival(self, k):
            p = xy_peer(k)
            sems = self.xy_sem.at[0, k], self.xy_sem.at[1, p]
            return remote(self.pay.at[0, p], self.buf_xy.at[p], *sems, at(z, p, core))

        def z_copy(self, k):
            p = lax.rem(self.here + k, 2 * n_z)
            mine = self.buf_z.at[self.here]
            sems = self.z_sem.at[0, k], self.z_sem.at[1, self.here]
            return remote(mine, mine, *sems, at(lax.div(p, 2), xy, lax.rem(p, 2)))

        def z_arrival(self, k):
            p = lax.rem(self.here + k, 2 * n_z)
            theirs = self.buf_z.at[p]
            sems = self.z_sem.at[0, k], self.z_sem.at[1, p]
            return remote(theirs, theirs, *sems, at(lax.div(p, 2), xy, lax.rem(p, 2)))

        def back_copy(self, k):
            mine = self.res.at[0, xy]
            sems = self.xy_sem.at[2, k], self.xy_sem.at[3, xy]
            return remote(mine, mine, *sems, at(z, xy_peer(k), core))

        def back_arrival(self, k):
            p = xy_peer(k)
            theirs = self.res.at[0, p]
            sems = self.xy_sem.at[2, k], self.xy_sem.at[3, p]
            return remote(theirs, theirs, *sems, at(z, p, core))

        def first(self):
            each(n_xy, lambda k: self.xy_copy(k).start())
            self.buf_xy[xy] = self.pay[0, xy]

        def second(self):
            each(n_xy, lambda k: self.xy_arrival(k).wait_recv())
            total = self.buf_xy[0].astype(F32)
            for p in range(1, n_xy):
                total = total + self.buf_xy[p].astype(F32)
            self.buf_z[self.here] = total.astype(BF)
            each(2 * n_z, lambda k: self.z_copy(k).start())

        def third(self):
            each(2 * n_z, lambda k: self.z_arrival(k).wait_recv())
            total = self.buf_z[0].astype(F32)
            for p in range(1, 2 * n_z):
                total = total + self.buf_z[p].astype(F32)
            self.res[0, xy] = (total * scale).astype(BF)
            each(n_xy, lambda k: self.back_copy(k).start())

        def fourth(self):
            each(n_xy, lambda k: self.back_arrival(k).wait_recv())

        def finish(self):
            each(n_xy, lambda k: self.xy_copy(k).wait_send())
            each(n_xy, lambda k: self.back_copy(k).wait_send())
            each(2 * n_z, lambda k: self.z_copy(k).wait_send())

    sum_a, sum_b = Sum(0), LateSum(1)

    barrier = pltpu.get_barrier_semaphore()

    def greet(device_id):
        pl.semaphore_signal(barrier, inc=1, device_id=device_id, device_id_type=MESH)

    for offset in OFFSETS[:6]:
        greet(device(offset))
    each(n_xy, lambda k: greet(at(z, xy_peer(k), core)))
    each(n_z, lambda k: greet(at(z_peer(k), xy, core)))
    each(n_z, lambda k: greet(at(z_peer(k), xy, 1 - core)))

    codes = [R.codes[0, s] for s in range(4)]
    tile_rows = iota((8, LANES), 0) & 3
    R.code_rows[...] = jnp.where(
        tile_rows == 0, codes[0], jnp.where(tile_rows == 1, codes[1], jnp.where(tile_rows == 2, codes[2], codes[3]))
    )
    dil = [R.dil[i] for i in range(4)]

    shifts = R.shifts
    for i, (_, _, _, W) in enumerate(LAYERS):
        shifts[i] = shift_matrix(W, dil[i])
    picks = R.picks
    PICK = {(16, 4): 0, (8, 4): 1, (8, 2): 2}
    for (H, m), where in PICK.items():
        _, col = column_pick(H, 128 if H == 16 else 64, m, codes[3], codes[2])
        picks[where] = take(LANES, col)

    def pick_rows(H, m):
        row, _ = column_pick(H, 128 if H == 16 else 64, m, codes[3], codes[2])
        return row

    for X3, D3, (C, O, H, _) in zip(R.x, R.d, LAYERS):
        D3[0 : 2 * RIM] = jnp.zeros((2 * RIM, 3 * O, LANES), BF)
        D3[2 * RIM + H : 4 * RIM + H] = jnp.zeros((2 * RIM, 3 * O, LANES), BF)
        X3[:, 3 * C : 3 * C + ONES, :] = jnp.ones((H + 2 * RIM, ONES, LANES), BF)

    def columns_of(x_ref, H, m, C):
        row = pick_rows(H, m)
        total = jnp.zeros((C, LANES), F32)
        for g in range(H // 4):
            y = mm(stacked(x_ref[4 * g : 4 * g + 4]), picks[PICK[(H, m)]])
            for q in range(4):
                total = total + jnp.where(row == 4 * g + q, y[q * C : (q + 1) * C], 0.0)
        return total

    def send_forward(name, x_ref, H, W, m, C):
        y = columns_of(x_ref, H, m, C)
        for side in range(2):
            R.cs[name][side] = pack(y, m * H, side == 1)
        both = jnp.concatenate([stacked(x_ref[0:m]), stacked(x_ref[H - m : H])], axis=1)
        for k, side in enumerate((1, 0)):
            rows = mm(both, pick_rows_matrix(W, codes[side]))
            R.rs[name][k] = pack_rows(rows.reshape(m, C, LANES), W)

    def halo_array(name, width, i):
        near = R.cr[name]
        low = iota((1, LANES), 1) < 64
        right, left = unpack(near[2 * i], width, False), unpack(near[2 * i + 1], width, True)
        return jnp.where(low, right, left).astype(BF)

    def halo_rows(Z, H, m, code, rows):
        mats = cat([take(LANES, halo_target(H, m, code, r)) for r in rows], 1)
        y = mm(Z, mats).astype(BF)
        return cat([y[:, LANES * q : LANES * (q + 1)] for q in range(len(rows))], 0)

    def fill(X3, r0, core, halo, C, S, offs, repeat):
        y = mm(jnp.concatenate([core, halo], axis=1), S).astype(BF)
        for q in range(core.shape[0] // C):
            part = slice(q * C, (q + 1) * C)
            for z in range(repeat):
                r = r0 + q * repeat + z
                X3[r, offs[0] : offs[0] + C, :] = y[part, :LANES]
                X3[r, offs[1] : offs[1] + C, :] = core[part]
                X3[r, offs[2] : offs[2] + C, :] = y[part, LANES:]

    def pad_and_shift(name, x_ref, H, m, C, layer, X3, offs, refine):
        arrive(name, slice(0, 2))
        Z = halo_array(name, H * m, 0)
        W = LANES * H // 16
        S = shifts[layer]
        rr = R.rr[name]
        code_u = R.code_near[0, 1:2, :]
        code_l = R.code_near[1, 0:1, :]
        rep = 2 if refine else 1

        def prepare(core, halo):
            if not refine:
                return core, halo
            w = iota((1, LANES), 1)
            core = mm(core, take(LANES, w >> 1)).astype(BF)
            near = jnp.where(w < 4, w >> 1, jnp.where(w >= LANES - 4, 64 + (w >> 1), -1))
            return core, mm(halo, take(LANES, near)).astype(BF)

        def body(g, carry):
            rows = [m * g + q for q in range(m)]
            core, halo = prepare(stacked(x_ref[pl.ds(m * g, m)]), halo_rows(Z, H, m, 0, rows))
            fill(X3, RIM + m * rep * g, core, halo, C, S, offs, rep)
            return carry

        lax.fori_loop(0, H // m, body, 0, unroll=True)
        arrive(name, slice(2, 8))
        Zu, Zl = halo_array(name, H * m, 1), halo_array(name, H * m, 2)
        core, halo = prepare(unpack_rows(rr[0], W), halo_rows(Zu, H, m, code_u, range(m)))
        fill(X3, 0, core, halo, C, S, offs, rep)
        core, halo = prepare(unpack_rows(rr[1], W), halo_rows(Zl, H, m, code_l, range(m)))
        fill(X3, RIM + H * rep, core, halo, C, S, offs, rep)

    def conv(Z3, width, K, d, rows, write, from_row=0):
        def body(i, carry):
            r = from_row + 2 * i
            taps = []
            for b in range(3):
                base = r + RIM + (b - 1) * d
                taps.append(
                    jnp.concatenate(
                        [Z3[base, 0:width, :], Z3[base + 1, 0:width, :]], axis=1
                    )
                )
            y = mm(K[...], jnp.concatenate(taps, axis=0))
            write(r, y[:, :LANES])
            write(r + 1, y[:, LANES:])
            return carry

        lax.fori_loop(0, rows // 2, body, 0, unroll=True)

    def weight_terms(X3, C, D3, O, d, rows, acc):
        n = 3 * C + ONES

        def body(i, carry):
            r = 4 * i
            lhs = jnp.concatenate([X3[r + q] for q in range(4)], axis=1)
            taps = []
            for a in range(3):
                base = r + RIM - (a - 1) * d
                taps.append(
                    jnp.concatenate([D3[base + q, O : 2 * O, :] for q in range(4)], axis=1)
                )
            if O == 64:
                taps.append(jnp.zeros((O, 4 * LANES), BF))
            y = mm_nt(lhs, jnp.concatenate(taps, axis=0))
            acc[0:n] = acc[0:n] + y
            return carry

        acc[0:n] = jnp.zeros((n, acc.shape[1]), F32)
        lax.fori_loop(0, rows // 4, body, 0, unroll=True)

    def spread_delta(x_ref, H, O, layer, D3):
        def body(g, carry):
            core = stacked(x_ref[pl.ds(4 * g, 4)])
            y = mm(core, shifts[layer, 0:LANES, :]).astype(BF)
            for q in range(4):
                part = slice(q * O, (q + 1) * O)
                D3[2 * RIM + 4 * g + q, 0:O, :] = y[part, :LANES]
                D3[2 * RIM + 4 * g + q, O : 2 * O, :] = core[part]
                D3[2 * RIM + 4 * g + q, 2 * O : 3 * O, :] = y[part, LANES:]
            return carry

        lax.fori_loop(0, H // 4, body, 0, unroll=True)

    def rims_of(x_ref, H, W, O, layer, K):
        row, col = column_pick(H, W, RIM, 1, 0)
        pick = take(LANES, col)
        edges = jnp.zeros((O, LANES), F32)
        for g in range(H // 4):
            y = mm(stacked(x_ref[4 * g : 4 * g + 4]), pick)
            for q in range(4):
                edges = edges + jnp.where(row == 4 * g + q, y[q * O : (q + 1) * O], 0.0)
        e = mm(edges.astype(BF), edge_matrix(H, dil[layer])).astype(BF)
        none = jnp.zeros((O, LANES), BF)
        blocks = []
        for b in range(3):
            a = 2 - b
            right = e[:, 2 * a * LANES : (2 * a + 1) * LANES]
            left = e[:, (2 * a + 1) * LANES : (2 * a + 2) * LANES]
            blocks.append(jnp.concatenate([right, none], axis=1))
            blocks.append(jnp.zeros((O, 2 * LANES), BF))
            blocks.append(jnp.concatenate([none, left], axis=1))
        return mm(K[...], jnp.concatenate(blocks, axis=0)).astype(BF)

    def send_backward(name, rims, G, c0, C, H, m, collapse=False):
        code_u = R.code_near[0, 1:2, :]
        code_l = R.code_near[1, 0:1, :]
        y = mm(rims, rim_matrix(H, m, code_u, code_l, collapse))
        for slot, k in enumerate((0, 0, 2, 2, 1, 1)):
            R.cs[name][slot] = pack(y[:, k * LANES : (k + 1) * LANES], H * m, slot % 2 == 0)
        W = LANES * H // 16
        R.rs[name][0] = pack_rows(G[H + m : H + 2 * m, c0 : c0 + C, :], W)
        R.rs[name][1] = pack_rows(G[0:m, c0 : c0 + C, :], W)

    def fold(name, G, c0, C, H, W, m, write):
        near = R.cr[name]
        rr = R.rr[name]
        low = iota((1, LANES), 1) < 64
        to_right, to_left = (
            near[i].astype(F32) + near[i + 2].astype(F32) + near[i + 4].astype(F32) for i in (1, 0)
        )
        back = jnp.where(low, unpack(to_right, H * m, False), unpack(to_left, H * m, True))
        row = pick_rows(H, m)
        both = jnp.concatenate([unpack_rows(rr[0], W), unpack_rows(rr[1], W)], axis=1)
        first = mm(both, return_rows_matrix(W, codes[0], codes[1], 0))
        last = mm(both, return_rows_matrix(W, codes[0], codes[1], 1))
        pick = picks[PICK[(H, m)]]
        for g in range(H // m):
            masked = [jnp.where(row == m * g + q, back, 0.0).astype(BF) for q in range(m)]
            y = mm_nt(cat(masked, 0), pick)
            if g == 0:
                y = y + first
            if g == H // m - 1:
                y = y + last
            for q in range(m):
                h = m * g + q
                write(h, G[h + m, c0 : c0 + C, :] + y[q * C : (q + 1) * C])

    def forward_weights(i):
        k, kf = R.k[i], R.kf[i]
        if i == 1:
            for t in range(0, 9, 2):
                block = k[8] if t == 8 else jnp.concatenate([k[t], k[t + 1]], axis=0)
                kf[:, t * 64 : t * 64 + block.shape[0]] = mm_nt(eye(LANES), block).astype(BF)
            return
        C = k.shape[2]
        for t in range(0, 9, 2):
            block = k[t] if t == 8 else jnp.concatenate([k[t], k[t + 1]], axis=1)
            kf[:, t * C : t * C + block.shape[1]] = block

    def backward_weights(i):
        k, kt = R.k[i], R.kt[i]
        if i == 1:
            for t in range(9):
                kt[:, t * LANES : (t + 1) * LANES] = k[8 - t]
            return
        O, C = k.shape[1], k.shape[2]
        for t in range(0, 9, 2):
            block = k[0] if t == 8 else jnp.concatenate([k[8 - t], k[7 - t]], axis=0)
            kt[:, t * O : t * O + block.shape[0]] = mm_nt(eye(C), block).astype(BF)

    def column(i):
        row = R.off[i][...]
        n = row.shape[1]
        return jnp.sum(jnp.where(iota((n, n), 0) == iota((n, n), 1), row, 0.0), axis=1, keepdims=True)

    def rows_first(x_ref, out):
        turn = to_rows()
        for g in range(4):
            y = mm(turn, stacked(x_ref[16 * g : 16 * g + 16])).astype(BF)
            for h in range(16):
                out[h, 16 * g : 16 * g + 16, :] = y[16 * h : 16 * h + 16]

    def put(ref, start_row, value):
        q = ref.shape[2]
        done = 0
        while done < value.shape[0]:
            piece, inner = divmod(start_row + done, q)
            n = min(q - inner, value.shape[0] - done)
            ref[piece // n_xy, piece % n_xy, inner : inner + n, :] = value[done : done + n].astype(BF)
            done += n

    def put_terms(ref, listed):
        where = 0
        for acc, C, O in listed:
            chunks = 2 if O == 64 else 3
            for k in range(chunks):
                put(ref, where, acc[0 : 3 * C, k * LANES : (k + 1) * LANES])
                where += 3 * C
        for acc, C, O in listed:
            k = 0 if O == 64 else 1
            put(ref, where, acc[3 * C : 3 * C + ONES, k * LANES : (k + 1) * LANES])
            where += ONES
        pieces = ref.shape[0] * ref.shape[1] * ref.shape[2]
        put(ref, where, jnp.zeros((pieces - where, LANES), BF))

    brought[0].wait()
    rows_first(R.near[0], R.fields)
    send_forward(FIELDS, R.fields, 16, 128, 4, 64)
    pl.semaphore_wait(barrier, 6 + (n_xy - 1) + 2 * (n_z - 1))
    for copy in code_copies:
        copy.start()
    start(FIELDS)

    for copy in brought[1:]:
        copy.wait()
    forward_weights(0)
    cot = R.cot
    rows_first(R.near[1], cot)
    backward_weights(3)
    spread_delta(cot, 16, 64, 3, R.d[3])
    G4 = R.g[3]

    def write_g4(r, v):
        G4[r] = v

    conv(R.d[3], 192, R.kt[3], dil[3], 24, write_g4)
    columns = [column(i) for i in range(4)]

    for copy in code_copies:
        copy.wait_recv()
    pad_and_shift(FIELDS, R.fields, 16, 4, 64, 0, R.x[0], (0, 64, 128), False)
    first_act, slope1 = R.first_act, R.slope1

    def write_first(r, v):
        act, slope = gelu_and_slope(v + columns[0])
        first_act[r] = act.astype(BF)
        slope1[r] = slope

    conv(R.x[0], 192, R.kf[0], dil[0], 16, write_first)
    pooled = R.pooled
    u, w = iota((2 * LANES, LANES), 0), iota((2 * LANES, LANES), 1)
    quarter = jnp.where(((u & (LANES - 1)) >> 1) == w, 0.25, 0.0).astype(BF)
    for g in range(2):
        lhs = cat(
            [
                jnp.concatenate([first_act[8 * g + 2 * q], first_act[8 * g + 2 * q + 1]], axis=1)
                for q in range(4)
            ],
            0,
        )
        pooled[4 * g : 4 * g + 4] = mm(lhs, quarter).astype(BF).reshape(4, 64, LANES)
    send_forward(POOLED, pooled, 8, 64, 4, 64)
    start(POOLED)
    send_forward(FIRST, first_act, 16, 128, 4, 64)
    rims4 = rims_of(cot, 16, 128, 64, 3, R.kt[3])
    G4c = R.g4c
    pool = onehot(((u & (LANES - 1)) >> 1) == w)
    for g in range(3):
        pairs = [G4[8 * g + 2 * q, 0:128, :] + G4[8 * g + 2 * q + 1, 0:128, :] for q in range(4)]
        y = mm(split(cat(pairs, 0)), pool)
        G4c[4 * g : 4 * g + 4] = y.reshape(4, 128, LANES)
    send_backward(BACK4C, rims4[0:128], G4c, 0, 128, 8, 2, True)
    send_backward(BACK4F, rims4[128:192], G4, 128, 64, 16, 4)
    forward_weights(1)


    pad_and_shift(POOLED, pooled, 8, 4, 64, 1, R.x[1], (0, 64, 128), False)
    start(FIRST)
    start(BACK4C)
    second_act, slope2 = R.second_act, R.slope2
    inside = iota((1, LANES), 1) < 64

    def write_second(r, v):
        act, slope = gelu_and_slope(v + columns[1])
        second_act[r] = jnp.where(inside, act, 0.0).astype(BF)
        slope2[r] = jnp.where(inside, slope, 0.0)

    conv(R.x[1], 192, R.kf[1], dil[1], 8, write_second)
    send_forward(SECOND, second_act, 8, 64, 4, 128)
    start(SECOND)
    for i in (2, 3):
        forward_weights(i)
    for i in (2, 1, 0):
        backward_weights(i)

    arrive(BACK4C)
    coarse, skip = R.coarse, R.skip

    def write_coarse(r, v):
        coarse[r] = v

    def write_skip(r, v):
        skip[r] = v

    fold(BACK4C, G4c, 0, 128, 8, 64, 2, write_coarse)


    pad_and_shift(FIRST, first_act, 16, 4, 64, 3, R.x[3], (128, 320, 512), False)

    pad_and_shift(SECOND, second_act, 8, 4, 128, 2, R.x[2], (0, 128, 256), False)
    start(BACK4F)
    third_act, delta3 = R.third_act, R.delta3

    def write_third(r, v):
        act, slope = gelu_and_slope(v + columns[2])
        third_act[r] = jnp.where(inside, act, 0.0).astype(BF)
        delta3[r] = jnp.where(inside, coarse[r] * slope, 0.0).astype(BF)

    conv(R.x[2], 384, R.kf[2], dil[2], 8, write_third)
    send_forward(THIRD, third_act, 8, 64, 2, 128)
    start(THIRD)
    spread_delta(delta3, 8, 128, 2, R.d[2])
    G3 = R.g[2]

    def write_g3(r, v):
        G3[r] = v

    conv(R.d[2], 384, R.kt[2], dil[2], 4, write_g3)
    conv(R.d[2], 384, R.kt[2], dil[2], 4, write_g3, 12)
    send_backward(BACK3, rims_of(delta3, 8, 64, 128, 2, R.kt[2]), G3, 0, 128, 8, 4)
    start(BACK3)
    conv(R.d[2], 384, R.kt[2], dil[2], 8, write_g3, 4)


    weight_terms(R.x[2], 128, R.d[2], 128, dil[2], 16, R.w[2])
    arrive(BACK4F)
    fold(BACK4F, G4, 128, 64, 16, 128, 4, write_skip)
    pad_and_shift(THIRD, third_act, 8, 2, 128, 3, R.x[3], (0, 192, 384), True)

    weight_terms(R.x[3], 192, R.d[3], 64, dil[3], 24, R.w[3])
    put_terms(R.pay[0], ((R.w[3], 192, 64), (R.w[2], 128, 128)))
    sum_a.first()
    arrive(BACK3)
    delta2 = R.delta2

    def write_delta2(r, v):
        delta2[r] = (v * slope2[r]).astype(BF)

    fold(BACK3, G3, 0, 128, 8, 64, 4, write_delta2)
    spread_delta(delta2, 8, 128, 1, R.d[1])
    G2 = R.g[1]

    def write_g2(r, v):
        G2[r] = v

    conv(R.d[1], 384, R.kt[1], dil[1], 4, write_g2)
    conv(R.d[1], 384, R.kt[1], dil[1], 4, write_g2, 12)
    send_backward(BACK2, rims_of(delta2, 8, 64, 128, 1, R.kt[1]), G2, 0, 64, 8, 4)
    start(BACK2)
    conv(R.d[1], 384, R.kt[1], dil[1], 8, write_g2, 4)

    state = R.state

    def write_state(r, v):
        state[r] = (v + columns[3]).astype(BF)


    weight_terms(R.x[1], 64, R.d[1], 128, dil[1], 16, R.w[1])
    sum_a.second()
    conv(R.x[3], 576, R.kf[3], dil[3], 8, write_state)
    arrive(BACK2)
    delta1 = R.delta1
    repeat = jnp.where((u & (LANES - 1)) == (w >> 1), 0.25, 0.0).astype(BF)

    def write_delta1(r, v):
        wide = mm(split(v), repeat)
        for z in range(2):
            delta1[2 * r + z] = ((skip[2 * r + z] + wide) * slope1[2 * r + z]).astype(BF)

    fold(BACK2, G2, 0, 64, 8, 64, 4, write_delta1)
    spread_delta(delta1, 16, 64, 0, R.d[0])
    weight_terms(R.x[0], 64, R.d[0], 64, dil[0], 24, R.w[0])
    put_terms(R.pay[1], ((R.w[1], 64, 128), (R.w[0], 64, 64)))
    sum_b.first()
    sum_a.third()
    G1 = R.g[0]

    def write_g1(r, v):
        G1[r] = v

    conv(R.d[0], 192, R.kt[0], dil[0], 4, write_g1)
    conv(R.d[0], 192, R.kt[0], dil[0], 4, write_g1, 20)
    send_backward(BACK1, rims_of(delta1, 16, 128, 64, 0, R.kt[0]), G1, 0, 64, 16, 4)
    start(BACK1)
    conv(R.d[0], 192, R.kt[0], dil[0], 16, write_g1, 4)
    sum_a.fourth()
    sum_b.second()
    conv(R.x[3], 576, R.kf[3], dil[3], 8, write_state, 8)
    arrive(BACK1)
    grad = R.grad

    def write_grad(r, v):
        grad[r] = v

    fold(BACK1, G1, 0, 64, 16, 128, 4, write_grad)
    sum_a.fifth()
    sum_b.third()
    sum_a.sixth()
    sum_b.fourth()

    sum_a.finish()
    sum_b.finish()
    for listed in (*copies, code_copies):
        for copy in listed:
            copy.wait_send()


PIECE = (80, 64)


def run_net(tiles, members, scale, operands):
    V, D = pltpu.VMEM, pltpu.SemaphoreType.DMA
    n_xy, n_z = tiles // 8, members * 4
    sizes = [(C, O, H + 2 * RIM) for C, O, H, _ in LAYERS]
    scratch = Refs(
        shifts=V((4, 256, 256), BF),
        picks=V((3, LANES, LANES), BF),
        x=[V((P_, 3 * C + ONES, LANES), BF) for C, O, P_ in sizes],
        d=[V((P_ + 2 * RIM, 3 * O, LANES), BF) for C, O, P_ in sizes],
        g=[V((P_, C, LANES), F32) for C, O, P_ in sizes],
        g4c=V((12, 128, LANES), F32),
        near=[V(v.shape, BF) for v in operands["far"]],
        k=[V(v.shape, BF) for v in operands["k_far"]],
        bring=D((6,)),
        kf=[V((O, 9 * C), BF) for C, O, _ in sizes],
        kt=[V((C, 9 * O), BF) for C, O, _ in sizes],
        w=[V((3 * C + ONES, 256 if O == 64 else 384), F32) for C, O, _ in sizes],
        fields=V((16, 64, LANES), BF),
        cot=V((16, 64, LANES), BF),
        first_act=V((16, 64, LANES), BF),
        slope1=V((16, 64, LANES), F32),
        pooled=V((8, 64, LANES), BF),
        second_act=V((8, 128, LANES), BF),
        slope2=V((8, 128, LANES), F32),
        third_act=V((8, 128, LANES), BF),
        coarse=V((8, 128, LANES), F32),
        skip=V((16, 64, LANES), F32),
        delta1=V((16, 64, LANES), BF),
        delta2=V((8, 128, LANES), BF),
        delta3=V((8, 128, LANES), BF),
        code_rows=V((8, LANES), jnp.int32),
        code_near=V((2, 8, LANES), jnp.int32),
        send=D((len(EXCHANGES), 8)),
        recv=D((len(EXCHANGES), 8)),
        send_code=D((2,)),
        recv_code=D((2,)),
        pay=[V((2 - i, n_xy, q, LANES), BF) for i, q in enumerate(PIECE)],
        others=[V((n_xy, PIECE[0], LANES), BF)],
        half=[V((n_xy, PIECE[0], LANES), BF)],
        bxy=[V((n_xy, q, LANES), BF) for q in PIECE],
        bz=[V((n_z * (i + 1), q, LANES), BF) for i, q in enumerate(PIECE)],
        psem=[D((4,))],
        xysem=[D((4, n_xy)) for q in PIECE],
        zsem=[D((2, n_z * (i + 1))) for i, q in enumerate(PIECE)],
        cs=[V((sent, C * m * H // LANES, LANES), BF) for C, m, H, sent in EXCHANGES],
        rs=[V((2, m * H // 16, C, LANES), BF) for C, m, H, sent in EXCHANGES],
        cr=[V((6, C * m * H // LANES, LANES), BF) for C, m, H, sent in EXCHANGES],
        rr=[V((2, m * H // 16, C, LANES), BF) for C, m, H, sent in EXCHANGES],
    )
    smem = pl.BlockSpec(memory_space=pltpu.SMEM)
    vmem = pl.BlockSpec(memory_space=pltpu.VMEM)
    shape = jax.ShapeDtypeStruct
    outputs = Refs(
        state=shape((16, 64, LANES), BF),
        grad=shape((16, 64, LANES), F32),
        res=[shape((2 - i, n_xy, q, LANES), BF) for i, q in enumerate(PIECE)],
    )
    inputs = Refs(**operands)
    flat_in, flat_out, flat_scratch = (list(flatten(part)) for part in (inputs, outputs, scratch))
    return pl.pallas_call(
        functools.partial(net_kernel, tiles, members, scale, (inputs, outputs, scratch)),
        out_shape=tuple(flat_out),
        in_specs=[
            smem if v.dtype == jnp.int32 else vmem if v.dtype == F32 else pl.BlockSpec(memory_space=pl.ANY)
            for v in flat_in
        ],
        out_specs=(vmem,) * len(flat_out),
        scratch_shapes=flat_scratch,
        compiler_params=pltpu.CompilerParams(
            collective_id=0, has_side_effects=True, vmem_limit_bytes=56 * 2**20
        ),
    )(*flat_in)

def finish_kernel(state, grad, early, late, state_out, grad_out, w1, w2, w3, w4, b1, b2, b3, b4):
    channels_first(state, state_out, 1)
    channels_first(grad, grad_out, 2)
    take_terms(early, ((w4, b4, 192, 64), (w3, b3, 128, 128)))
    take_terms(late, ((w2, b2, 64, 128), (w1, b1, 64, 64)))


def run_finish(raw):
    vmem = pl.BlockSpec(memory_space=pltpu.VMEM)
    shape = jax.ShapeDtypeStruct
    outputs = [shape((64, 16, LANES), BF), shape((64, 16, LANES), F32)]
    outputs += [shape((9, C, O) if O > C else (9, O, C), F32) for C, O, _, _ in LAYERS]
    outputs += [shape((1, O), F32) for C, O, _, _ in LAYERS]
    return pl.pallas_call(
        finish_kernel,
        out_shape=tuple(outputs),
        in_specs=[vmem] * len(raw),
        out_specs=(vmem,) * len(outputs),
        compiler_params=pltpu.CompilerParams(vmem_limit_bytes=56 * 2**20),
    )(*raw)


def shards(tiles, members, fields, cotangent, k1, k2, k3, k4, off1, off2, off3, off4, codes, dilations):
    operands = dict(
        codes=codes,
        dil=dilations,
        far=[fields[0, 0], cotangent[0, 0]],
        k_far=[k1, jnp.swapaxes(k2, 1, 2), k3, k4],
        off=[off1[None, :], off2[None, :], off3[None, :], off4[None, :]],
    )
    scale = 1.0 / math.sqrt(members * tiles * fields.shape[3] * fields.shape[4])
    state, grad, *rest = run_finish(run_net(tiles, members, scale, operands))
    rest[1] = jnp.swapaxes(rest[1], 1, 2)
    return (state[None, None], grad[None, None], *rest[:4], *[b[0] for b in rest[4:]])


def solution(mesh):
    big = P("ens", "tile", None, None, None)
    in_specs = (big, big) + (P(),) * 8 + (P("tile", None), P())
    out_specs = (big, big) + (P(),) * 8
    body = functools.partial(shards, mesh.shape["tile"], mesh.shape["ens"])
    return jax.shard_map(body, mesh=mesh, in_specs=in_specs, out_specs=out_specs, check_vma=False)
```

```python
import functools
import math

import jax
import jax.numpy as jnp
from jax import lax
from jax.experimental import pallas as pl
from jax.experimental.pallas import tpu as pltpu
from jax.sharding import PartitionSpec as P

MESH = pl.DeviceIdType.MESH
BF = jnp.bfloat16
F32 = jnp.float32

RIM = 4
TILE_ROW = 8
LANES = 128
ONES = 16

FIELDS, POOLED, FIRST, SECOND, THIRD, BACK4C, BACK4F, BACK3, BACK2, BACK1 = range(10)
EXCHANGES = (
    (64, 4, 16, 2),
    (64, 4, 8, 2),
    (64, 4, 16, 2),
    (128, 4, 8, 2),
    (128, 2, 8, 2),
    (128, 2, 8, 6),
    (64, 4, 16, 6),
    (128, 4, 8, 6),
    (64, 4, 8, 6),
    (64, 4, 16, 6),
)
OFFSETS = (1, -1, 9, 7, -7, -9, 8, -8)
LAYERS = ((64, 64, 16, 128), (64, 128, 8, 64), (128, 128, 8, 64), (192, 64, 16, 128))


def iota(shape, dim):
    return lax.broadcasted_iota(jnp.int32, shape, dim)


def onehot(cond):
    return jnp.where(cond, 1.0, 0.0).astype(BF)


def mm(a, b):
    return jnp.dot(a, b, preferred_element_type=F32)


def mm_nt(a, b):
    return lax.dot_general(a, b, (((1,), (1,)), ((), ())), preferred_element_type=F32)


def split(values):
    high = values.astype(BF)
    low = (values - high.astype(F32)).astype(BF)
    return jnp.concatenate([high, low], axis=-1)


def cat(parts, axis):
    return parts[0] if len(parts) == 1 else jnp.concatenate(parts, axis=axis)


def log2(m):
    return m.bit_length() - 1


def column_pick(H, W, m, code_right, code_left):
    lane = iota((1, LANES), 1)
    code = jnp.where(lane < 64, code_right, code_left)
    idx = lane & 63
    row, col = idx >> log2(m), idx & (m - 1)
    col = jnp.where((code & 1) == 1, W - m + col, col)
    row = jnp.where((code >> 1) == 1, H - 1 - row, row)
    valid = idx < H * m
    return jnp.where(valid, row, -1), jnp.where(valid, col, -1)


def halo_target(H, m, code, row):
    w = iota((1, LANES), 1)
    picked = jnp.where((code & 1) == 1, H - m + row, row)
    flip = (code >> 1) == 1
    k = w - (LANES - m)
    left = jnp.where(flip, 64 + m * picked + (m - 1 - k), m * picked + k)
    right = jnp.where(flip, m * picked + (m - 1 - w), 64 + m * picked + w)
    return jnp.where(w >= LANES - m, left, jnp.where(w < m, right, -1))


def take(rows, target):
    return onehot(iota((rows, target.shape[1]), 0) == target)


def shift_matrix(W, d):
    out = iota((1, 2 * LANES), 1)
    j = out & (LANES - 1)
    minus = jnp.where(j >= d, j - d, 2 * LANES + j - d)
    plus = jnp.where(j + d < W, j + d, LANES + j + d - W)
    target = jnp.where(out < LANES, minus, plus)
    return take(2 * LANES, jnp.where(j < W, target, -1))


def turned(W, code):
    w = iota((1, LANES), 1)
    return jnp.where(w < W, jnp.where((code >> 1) == 1, W - 1 - w, w), -1024)


def pick_rows_matrix(W, code):
    return take(2 * LANES, turned(W, code) + LANES * (code & 1))


def return_rows_matrix(W, code_upper, code_lower, last):
    parts = []
    for code in (code_upper, code_lower):
        parts.append(take(LANES, jnp.where((code & 1) == last, turned(W, code), -1)))
    return jnp.concatenate(parts, axis=0)


def rim_matrix(H, m, code_above, code_below, collapse):
    shape = (2 * LANES, LANES)
    u, lane = iota(shape, 0), iota((1, LANES), 1)
    src = u
    if collapse:
        src = (((u & (LANES - 1)) >> 3) << 1) + ((u & 3) >> 1) + ((u >> 7) << 7)
    idx = lane & 63
    row, k = idx >> log2(m), idx & (m - 1)
    leftward = lane < 64
    valid = idx < H * m
    targets = [jnp.where(valid, (row + m) * m + k + jnp.where(leftward, LANES, 0), -1)]
    for code, base in ((code_above, 0), (code_below, H + m)):
        picked = jnp.where((code & 1) == 1, row - (H - m), row)
        flip = (code >> 1) & 1
        kk = jnp.where(flip == 1, m - 1 - k, k)
        left_side = jnp.where(leftward, 1 - flip, flip)
        inside = valid & (picked >= 0) & (picked < m)
        targets.append(jnp.where(inside, (picked + base) * m + kk + left_side * LANES, -1))
    return jnp.concatenate([onehot(src == target) for target in targets], axis=1)


def edge_matrix(H, d):
    v = iota((1, LANES), 1)
    row, k = v >> 2, v & 3
    parts = []
    for a in range(3):
        h = row - RIM - (a - 1) * d
        inside = (h >= 0) & (h < H)
        parts.append(take(LANES, jnp.where(inside & (k < d), 4 * h + (4 - d + k), -1)))
        parts.append(take(LANES, jnp.where(inside & (k >= 4 - d), 64 + 4 * h + (k - 4 + d), -1)))
    return jnp.concatenate(parts, axis=1)


def gelu_and_slope(x):
    cdf = 0.5 + 0.5 * lax.erf(x * math.sqrt(0.5))
    pdf = jnp.exp(-0.5 * x * x) * (1.0 / math.sqrt(2.0 * math.pi))
    return x * cdf, cdf + x * pdf


def stacked(values):
    return values.reshape(values.shape[0] * values.shape[1], values.shape[2])


def eye(n):
    return onehot(iota((n, n), 0) == iota((n, n), 1))


def to_rows():
    u, w = iota((256, 256), 0), iota((256, 256), 1)
    return onehot(w == ((u & 15) << 4) + (u >> 4))


def channels_first(x_ref, out, parts):
    turn = to_rows()
    for g in range(4):
        block = cat([x_ref[h, 16 * g : 16 * g + 16, :] for h in range(16)], 0)
        y = mm(turn, block) if parts == 1 else mm(turn, split(block))
        if parts == 2:
            y = y[:, :LANES] + y[:, LANES:]
        out[16 * g : 16 * g + 16] = y.astype(out.dtype).reshape(16, 16, LANES)


def get(ref, start_row, count):
    n_xy, q = ref.shape[1], ref.shape[2]
    parts, done = [], 0
    while done < count:
        piece, inner = divmod(start_row + done, q)
        n = min(q - inner, count - done)
        parts.append(ref[piece // n_xy, piece % n_xy, inner : inner + n, :])
        done += n
    return cat(parts, 0)


def take_terms(ref, listed):
    sel = [onehot(iota((64, LANES), 1) == iota((64, LANES), 0) + 64 * k) for k in range(2)]
    where = 0
    for w_out, b_out, C, O in listed:
        for a in range(3):
            chunk, side = (a // 2, sel[a % 2]) if O == 64 else (a, eye(LANES))
            for e in range(3):
                block = get(ref, where + chunk * 3 * C + e * C, C)
                w_out[3 * a + e] = block.astype(F32) if O > C else mm_nt(side, block)
        where += (2 if O == 64 else 3) * 3 * C
    for w_out, b_out, C, O in listed:
        block = get(ref, where, ONES)
        b_out[...] = mm_nt(block, sel[1])[0:1] if O == 64 else block.astype(F32)[0:1]
        where += ONES


class Refs:
    def __init__(self, **parts):
        self.__dict__.update(parts)


def flatten(part):
    for value in part.__dict__.values():
        yield from value if type(value) is list else [value]


def fill_in(parts, refs):
    named = {}
    for part in parts:
        for key, value in part.__dict__.items():
            named[key] = [next(refs) for _ in value] if type(value) is list else next(refs)
    return named


def pack(y, width, left):
    groups = LANES // width
    n = y.shape[0] // groups
    group = iota((1, LANES), 1) >> log2(width)
    out = jnp.zeros((n, LANES), F32)
    for g in range(groups):
        by = (g * width - (64 if left else 0)) % LANES
        part = y[g * n : (g + 1) * n]
        out = jnp.where(group == g, pltpu.roll(part, by, 1) if by else part, out)
    return out.astype(BF)


def unpack(p, width, left):
    p = p.astype(F32)
    parts = []
    for g in range(LANES // width):
        by = ((64 if left else 0) - g * width) % LANES
        parts.append(pltpu.roll(p, by, 1) if by else p)
    return jnp.concatenate(parts, axis=0)


def pack_rows(rows, W):
    if W == LANES:
        return rows.astype(BF)
    n, C, _ = rows.shape
    second = pltpu.roll(stacked(rows[n // 2 :]), 64, 1)
    return (stacked(rows[: n // 2]) + second).astype(BF).reshape(n // 2, C, LANES)


def unpack_rows(x, W):
    x = stacked(x)
    if W == LANES:
        return x
    return jnp.concatenate([x, pltpu.roll(x.astype(F32), 64, 1).astype(BF)], axis=0)


def net_kernel(tiles, members, scale, tree, *refs):
    R = Refs(**fill_in(tree, iter(refs)))
    tile = lax.axis_index("tile")
    ens = lax.axis_index("ens")

    def device(offset):
        return (ens, lax.rem(tile + (offset + tiles), tiles))

    brought = [
        pltpu.make_async_copy(there, here, R.bring.at[i])
        for i, (there, here) in enumerate(zip(R.far + R.k_far, R.near + R.k))
    ]
    for copy in brought:
        copy.start()

    copies = []
    for x, (C, m, H, sent) in enumerate(EXCHANGES):
        listed = []
        for slot, offset in enumerate(OFFSETS):
            if slot < 6:
                which = slot % sent
                src = R.cs[x].at[which]
                dst = R.cr[x].at[slot]
            else:
                src = R.rs[x].at[slot - 6]
                dst = R.rr[x].at[slot - 6]
            listed.append(
                pltpu.make_async_remote_copy(
                    src_ref=src,
                    dst_ref=dst,
                    send_sem=R.send.at[x, slot],
                    recv_sem=R.recv.at[x, slot],
                    device_id=device(offset),
                    device_id_type=MESH,
                )
            )
        copies.append(listed)
    code_copies = [
        pltpu.make_async_remote_copy(
            src_ref=R.code_rows,
            dst_ref=R.code_near.at[k],
            send_sem=R.send_code.at[k],
            recv_sem=R.recv_code.at[k],
            device_id=device(offset),
            device_id_type=MESH,
        )
        for k, offset in enumerate((8, -8))
    ]

    def start(name):
        for copy in copies[name]:
            copy.start()

    def arrive(name, slots=slice(0, 8)):
        for copy in copies[name][slots]:
            copy.wait_recv()

    n_ens, n_low = members, 4
    n_xy, n_z = tiles // (2 * n_low), n_ens * n_low
    xy = lax.div(tile, 2 * n_low)
    low = lax.div(lax.rem(tile, 2 * n_low), 2)
    core = lax.rem(tile, 2)
    z = ens * n_low + low

    def at(z_, xy_, core_):
        return (lax.div(z_, n_low), (xy_ * n_low + lax.rem(z_, n_low)) * 2 + core_)

    def xy_peer(k):
        return lax.rem(xy + k, n_xy)

    def z_peer(k):
        return lax.rem(z + k, n_z)

    def remote(src, dst, send, recv, device_id):
        return pltpu.make_async_remote_copy(
            src_ref=src, dst_ref=dst, send_sem=send, recv_sem=recv, device_id=device_id, device_id_type=MESH
        )

    def each(n, act):
        def body(k, carry):
            act(k)
            return carry

        lax.fori_loop(1, n, body, 0)

    class Sum:
        def __init__(self, tag):
            self.pay, self.from_core = R.pay[tag], R.others[tag]
            self.half, self.buf_xy, self.buf_z = R.half[tag], R.bxy[tag], R.bz[tag]
            self.res = R.res[tag]
            self.pair_sem, self.xy_sem = R.psem[tag], R.xysem[tag]
            self.z_sem = R.zsem[tag]
            partner = at(z, xy, 1 - core)
            self.pair = remote(
                self.pay.at[1 - core], self.from_core, self.pair_sem.at[0], self.pair_sem.at[1], partner
            )
            self.other = remote(
                self.res.at[core], self.res.at[core], self.pair_sem.at[2], self.pair_sem.at[3], partner
            )
            self.theirs = remote(
                self.res.at[1 - core], self.res.at[1 - core], self.pair_sem.at[2], self.pair_sem.at[3], partner
            )

        def xy_copy(self, k):
            p = xy_peer(k)
            return remote(
                self.half.at[p], self.buf_xy.at[xy], self.xy_sem.at[0, k], self.xy_sem.at[1, xy], at(z, p, core)
            )

        def xy_arrival(self, k):
            p = xy_peer(k)
            return remote(
                self.half.at[p], self.buf_xy.at[p], self.xy_sem.at[0, k], self.xy_sem.at[1, p], at(z, p, core)
            )

        def z_copy(self, k):
            here = self.buf_z.at[z]
            return remote(here, here, self.z_sem.at[0, k], self.z_sem.at[1, z], at(z_peer(k), xy, core))

        def z_arrival(self, k):
            p = z_peer(k)
            there = self.buf_z.at[p]
            return remote(there, there, self.z_sem.at[0, k], self.z_sem.at[1, p], at(p, xy, core))

        def back_copy(self, k):
            here = self.res.at[core, xy]
            return remote(here, here, self.xy_sem.at[2, k], self.xy_sem.at[3, xy], at(z, xy_peer(k), core))

        def back_arrival(self, k):
            p = xy_peer(k)
            there = self.res.at[core, p]
            return remote(there, there, self.xy_sem.at[2, k], self.xy_sem.at[3, p], at(z, p, core))

        def first(self):
            self.pair.start()

        def second(self):
            self.pair.wait()

            def add(p, carry):
                mine = self.pay[core, p].astype(F32)
                self.half[p] = (mine + self.from_core[p].astype(F32)).astype(BF)
                return carry

            lax.fori_loop(0, n_xy, add, 0)
            each(n_xy, lambda k: self.xy_copy(k).start())
            self.buf_xy[xy] = self.half[xy]

        def third(self):
            each(n_xy, lambda k: self.xy_arrival(k).wait_recv())
            total = self.buf_xy[0].astype(F32)
            for p in range(1, n_xy):
                total = total + self.buf_xy[p].astype(F32)
            self.buf_z[z] = total.astype(BF)
            each(n_z, lambda k: self.z_copy(k).start())

        def fourth(self):
            each(n_z, lambda k: self.z_arrival(k).wait_recv())
            total = self.buf_z[0].astype(F32)
            for p in range(1, n_z):
                total = total + self.buf_z[p].astype(F32)
            self.res[core, xy] = (total * scale).astype(BF)
            each(n_xy, lambda k: self.back_copy(k).start())

        def fifth(self):
            each(n_xy, lambda k: self.back_arrival(k).wait_recv())
            self.other.start()

        def sixth(self):
            self.theirs.wait_recv()

        def finish(self):
            self.other.wait_send()
            each(n_xy, lambda k: self.xy_copy(k).wait_send())
            each(n_xy, lambda k: self.back_copy(k).wait_send())
            each(n_z, lambda k: self.z_copy(k).wait_send())

    class LateSum:
        def __init__(self, tag):
            self.pay, self.buf_xy, self.buf_z = R.pay[tag], R.bxy[tag], R.bz[tag]
            self.res, self.xy_sem, self.z_sem = R.res[tag], R.xysem[tag], R.zsem[tag]
            self.here = z * 2 + core

        def xy_copy(self, k):
            p = xy_peer(k)
            sems = self.xy_sem.at[0, k], self.xy_sem.at[1, xy]
            return remote(self.pay.at[0, p], self.buf_xy.at[xy], *sems, at(z, p, core))

        def xy_arrival(self, k):
            p = xy_peer(k)
            sems = self.xy_sem.at[0, k], self.xy_sem.at[1, p]
            return remote(self.pay.at[0, p], self.buf_xy.at[p], *sems, at(z, p, core))

        def z_copy(self, k):
            p = lax.rem(self.here + k, 2 * n_z)
            mine = self.buf_z.at[self.here]
            sems = self.z_sem.at[0, k], self.z_sem.at[1, self.here]
            return remote(mine, mine, *sems, at(lax.div(p, 2), xy, lax.rem(p, 2)))

        def z_arrival(self, k):
            p = lax.rem(self.here + k, 2 * n_z)
            theirs = self.buf_z.at[p]
            sems = self.z_sem.at[0, k], self.z_sem.at[1, p]
            return remote(theirs, theirs, *sems, at(lax.div(p, 2), xy, lax.rem(p, 2)))

        def back_copy(self, k):
            mine = self.res.at[0, xy]
            sems = self.xy_sem.at[2, k], self.xy_sem.at[3, xy]
            return remote(mine, mine, *sems, at(z, xy_peer(k), core))

        def back_arrival(self, k):
            p = xy_peer(k)
            theirs = self.res.at[0, p]
            sems = self.xy_sem.at[2, k], self.xy_sem.at[3, p]
            return remote(theirs, theirs, *sems, at(z, p, core))

        def first(self):
            each(n_xy, lambda k: self.xy_copy(k).start())
            self.buf_xy[xy] = self.pay[0, xy]

        def second(self):
            each(n_xy, lambda k: self.xy_arrival(k).wait_recv())
            total = self.buf_xy[0].astype(F32)
            for p in range(1, n_xy):
                total = total + self.buf_xy[p].astype(F32)
            self.buf_z[self.here] = total.astype(BF)
            each(2 * n_z, lambda k: self.z_copy(k).start())

        def third(self):
            each(2 * n_z, lambda k: self.z_arrival(k).wait_recv())
            total = self.buf_z[0].astype(F32)
            for p in range(1, 2 * n_z):
                total = total + self.buf_z[p].astype(F32)
            self.res[0, xy] = (total * scale).astype(BF)
            each(n_xy, lambda k: self.back_copy(k).start())

        def fourth(self):
            each(n_xy, lambda k: self.back_arrival(k).wait_recv())

        def finish(self):
            each(n_xy, lambda k: self.xy_copy(k).wait_send())
            each(n_xy, lambda k: self.back_copy(k).wait_send())
            each(2 * n_z, lambda k: self.z_copy(k).wait_send())

    sum_a, sum_b, sum_c = Sum(0), LateSum(1), LateSum(2)

    barrier = pltpu.get_barrier_semaphore()

    def greet(device_id):
        pl.semaphore_signal(barrier, inc=1, device_id=device_id, device_id_type=MESH)

    for offset in OFFSETS[:6]:
        greet(device(offset))
    each(n_xy, lambda k: greet(at(z, xy_peer(k), core)))
    each(n_z, lambda k: greet(at(z_peer(k), xy, core)))
    each(n_z, lambda k: greet(at(z_peer(k), xy, 1 - core)))

    codes = [R.codes[0, s] for s in range(4)]
    tile_rows = iota((8, LANES), 0) & 3
    R.code_rows[...] = jnp.where(
        tile_rows == 0, codes[0], jnp.where(tile_rows == 1, codes[1], jnp.where(tile_rows == 2, codes[2], codes[3]))
    )
    dil = [R.dil[i] for i in range(4)]

    shifts = R.shifts
    for i, (_, _, _, W) in enumerate(LAYERS):
        shifts[i] = shift_matrix(W, dil[i])
    picks = R.picks
    PICK = {(16, 4): 0, (8, 4): 1, (8, 2): 2}
    for (H, m), where in PICK.items():
        _, col = column_pick(H, 128 if H == 16 else 64, m, codes[3], codes[2])
        picks[where] = take(LANES, col)

    def pick_rows(H, m):
        row, _ = column_pick(H, 128 if H == 16 else 64, m, codes[3], codes[2])
        return row

    for X3, D3, (C, O, H, _) in zip(R.x, R.d, LAYERS):
        D3[0 : 2 * RIM] = jnp.zeros((2 * RIM, 3 * O, LANES), BF)
        D3[2 * RIM + H : 4 * RIM + H] = jnp.zeros((2 * RIM, 3 * O, LANES), BF)
        X3[:, 3 * C : 3 * C + ONES, :] = jnp.ones((H + 2 * RIM, ONES, LANES), BF)

    def columns_of(x_ref, H, m, C):
        row = pick_rows(H, m)
        total = jnp.zeros((C, LANES), F32)
        for g in range(H // 4):
            y = mm(stacked(x_ref[4 * g : 4 * g + 4]), picks[PICK[(H, m)]])
            for q in range(4):
                total = total + jnp.where(row == 4 * g + q, y[q * C : (q + 1) * C], 0.0)
        return total

    def send_forward(name, x_ref, H, W, m, C):
        y = columns_of(x_ref, H, m, C)
        for side in range(2):
            R.cs[name][side] = pack(y, m * H, side == 1)
        both = jnp.concatenate([stacked(x_ref[0:m]), stacked(x_ref[H - m : H])], axis=1)
        for k, side in enumerate((1, 0)):
            rows = mm(both, pick_rows_matrix(W, codes[side]))
            R.rs[name][k] = pack_rows(rows.reshape(m, C, LANES), W)

    def halo_array(name, width, i):
        near = R.cr[name]
        low = iota((1, LANES), 1) < 64
        right, left = unpack(near[2 * i], width, False), unpack(near[2 * i + 1], width, True)
        return jnp.where(low, right, left).astype(BF)

    def halo_rows(Z, H, m, code, rows):
        mats = cat([take(LANES, halo_target(H, m, code, r)) for r in rows], 1)
        y = mm(Z, mats).astype(BF)
        return cat([y[:, LANES * q : LANES * (q + 1)] for q in range(len(rows))], 0)

    def fill(X3, r0, core, halo, C, S, offs, repeat):
        y = mm(jnp.concatenate([core, halo], axis=1), S).astype(BF)
        for q in range(core.shape[0] // C):
            part = slice(q * C, (q + 1) * C)
            for z in range(repeat):
                r = r0 + q * repeat + z
                X3[r, offs[0] : offs[0] + C, :] = y[part, :LANES]
                X3[r, offs[1] : offs[1] + C, :] = core[part]
                X3[r, offs[2] : offs[2] + C, :] = y[part, LANES:]

    def pad_and_shift(name, x_ref, H, m, C, layer, X3, offs, refine):
        arrive(name, slice(0, 2))
        Z = halo_array(name, H * m, 0)
        W = LANES * H // 16
        S = shifts[layer]
        rr = R.rr[name]
        code_u = R.code_near[0, 1:2, :]
        code_l = R.code_near[1, 0:1, :]
        rep = 2 if refine else 1

        def prepare(core, halo):
            if not refine:
                return core, halo
            w = iota((1, LANES), 1)
            core = mm(core, take(LANES, w >> 1)).astype(BF)
            near = jnp.where(w < 4, w >> 1, jnp.where(w >= LANES - 4, 64 + (w >> 1), -1))
            return core, mm(halo, take(LANES, near)).astype(BF)

        def body(g, carry):
            rows = [m * g + q for q in range(m)]
            core, halo = prepare(stacked(x_ref[pl.ds(m * g, m)]), halo_rows(Z, H, m, 0, rows))
            fill(X3, RIM + m * rep * g, core, halo, C, S, offs, rep)
            return carry

        lax.fori_loop(0, H // m, body, 0, unroll=True)
        arrive(name, slice(2, 8))
        Zu, Zl = halo_array(name, H * m, 1), halo_array(name, H * m, 2)
        core, halo = prepare(unpack_rows(rr[0], W), halo_rows(Zu, H, m, code_u, range(m)))
        fill(X3, 0, core, halo, C, S, offs, rep)
        core, halo = prepare(unpack_rows(rr[1], W), halo_rows(Zl, H, m, code_l, range(m)))
        fill(X3, RIM + H * rep, core, halo, C, S, offs, rep)

    def conv(Z3, width, K, d, rows, write, from_row=0):
        def body(i, carry):
            r = from_row + 2 * i
            taps = []
            for b in range(3):
                base = r + RIM + (b - 1) * d
                taps.append(
                    jnp.concatenate(
                        [Z3[base, 0:width, :], Z3[base + 1, 0:width, :]], axis=1
                    )
                )
            y = mm(K[...], jnp.concatenate(taps, axis=0))
            write(r, y[:, :LANES])
            write(r + 1, y[:, LANES:])
            return carry

        lax.fori_loop(0, rows // 2, body, 0, unroll=True)

    def weight_terms(X3, C, D3, O, d, rows, acc):
        n = 3 * C + ONES

        def body(i, carry):
            r = 4 * i
            lhs = jnp.concatenate([X3[r + q] for q in range(4)], axis=1)
            taps = []
            for a in range(3):
                base = r + RIM - (a - 1) * d
                taps.append(
                    jnp.concatenate([D3[base + q, O : 2 * O, :] for q in range(4)], axis=1)
                )
            if O == 64:
                taps.append(jnp.zeros((O, 4 * LANES), BF))
            y = mm_nt(lhs, jnp.concatenate(taps, axis=0))
            acc[0:n] = acc[0:n] + y
            return carry

        acc[0:n] = jnp.zeros((n, acc.shape[1]), F32)
        lax.fori_loop(0, rows // 4, body, 0, unroll=True)

    def spread_delta(x_ref, H, O, layer, D3):
        def body(g, carry):
            core = stacked(x_ref[pl.ds(4 * g, 4)])
            y = mm(core, shifts[layer, 0:LANES, :]).astype(BF)
            for q in range(4):
                part = slice(q * O, (q + 1) * O)
                D3[2 * RIM + 4 * g + q, 0:O, :] = y[part, :LANES]
                D3[2 * RIM + 4 * g + q, O : 2 * O, :] = core[part]
                D3[2 * RIM + 4 * g + q, 2 * O : 3 * O, :] = y[part, LANES:]
            return carry

        lax.fori_loop(0, H // 4, body, 0, unroll=True)

    def rims_of(x_ref, H, W, O, layer, K):
        row, col = column_pick(H, W, RIM, 1, 0)
        pick = take(LANES, col)
        edges = jnp.zeros((O, LANES), F32)
        for g in range(H // 4):
            y = mm(stacked(x_ref[4 * g : 4 * g + 4]), pick)
            for q in range(4):
                edges = edges + jnp.where(row == 4 * g + q, y[q * O : (q + 1) * O], 0.0)
        e = mm(edges.astype(BF), edge_matrix(H, dil[layer])).astype(BF)
        none = jnp.zeros((O, LANES), BF)
        blocks = []
        for b in range(3):
            a = 2 - b
            right = e[:, 2 * a * LANES : (2 * a + 1) * LANES]
            left = e[:, (2 * a + 1) * LANES : (2 * a + 2) * LANES]
            blocks.append(jnp.concatenate([right, none], axis=1))
            blocks.append(jnp.zeros((O, 2 * LANES), BF))
            blocks.append(jnp.concatenate([none, left], axis=1))
        return mm(K[...], jnp.concatenate(blocks, axis=0)).astype(BF)

    def send_backward(name, rims, G, c0, C, H, m, collapse=False):
        code_u = R.code_near[0, 1:2, :]
        code_l = R.code_near[1, 0:1, :]
        y = mm(rims, rim_matrix(H, m, code_u, code_l, collapse))
        for slot, k in enumerate((0, 0, 2, 2, 1, 1)):
            R.cs[name][slot] = pack(y[:, k * LANES : (k + 1) * LANES], H * m, slot % 2 == 0)
        W = LANES * H // 16
        R.rs[name][0] = pack_rows(G[H + m : H + 2 * m, c0 : c0 + C, :], W)
        R.rs[name][1] = pack_rows(G[0:m, c0 : c0 + C, :], W)

    def fold(name, G, c0, C, H, W, m, write):
        near = R.cr[name]
        rr = R.rr[name]
        low = iota((1, LANES), 1) < 64
        to_right, to_left = (
            near[i].astype(F32) + near[i + 2].astype(F32) + near[i + 4].astype(F32) for i in (1, 0)
        )
        back = jnp.where(low, unpack(to_right, H * m, False), unpack(to_left, H * m, True))
        row = pick_rows(H, m)
        both = jnp.concatenate([unpack_rows(rr[0], W), unpack_rows(rr[1], W)], axis=1)
        first = mm(both, return_rows_matrix(W, codes[0], codes[1], 0))
        last = mm(both, return_rows_matrix(W, codes[0], codes[1], 1))
        pick = picks[PICK[(H, m)]]
        for g in range(H // m):
            masked = [jnp.where(row == m * g + q, back, 0.0).astype(BF) for q in range(m)]
            y = mm_nt(cat(masked, 0), pick)
            if g == 0:
                y = y + first
            if g == H // m - 1:
                y = y + last
            for q in range(m):
                h = m * g + q
                write(h, G[h + m, c0 : c0 + C, :] + y[q * C : (q + 1) * C])

    def forward_weights(i):
        k, kf = R.k[i], R.kf[i]
        if i == 1:
            for t in range(0, 9, 2):
                block = k[8] if t == 8 else jnp.concatenate([k[t], k[t + 1]], axis=0)
                kf[:, t * 64 : t * 64 + block.shape[0]] = mm_nt(eye(LANES), block).astype(BF)
            return
        C = k.shape[2]
        for t in range(0, 9, 2):
            block = k[t] if t == 8 else jnp.concatenate([k[t], k[t + 1]], axis=1)
            kf[:, t * C : t * C + block.shape[1]] = block

    def backward_weights(i):
        k, kt = R.k[i], R.kt[i]
        if i == 1:
            for t in range(9):
                kt[:, t * LANES : (t + 1) * LANES] = k[8 - t]
            return
        O, C = k.shape[1], k.shape[2]
        for t in range(0, 9, 2):
            block = k[0] if t == 8 else jnp.concatenate([k[8 - t], k[7 - t]], axis=0)
            kt[:, t * O : t * O + block.shape[0]] = mm_nt(eye(C), block).astype(BF)

    def column(i):
        row = R.off[i][...]
        n = row.shape[1]
        return jnp.sum(jnp.where(iota((n, n), 0) == iota((n, n), 1), row, 0.0), axis=1, keepdims=True)

    def rows_first(x_ref, out):
        turn = to_rows()
        for g in range(4):
            y = mm(turn, stacked(x_ref[16 * g : 16 * g + 16])).astype(BF)
            for h in range(16):
                out[h, 16 * g : 16 * g + 16, :] = y[16 * h : 16 * h + 16]

    def put(ref, start_row, value):
        q = ref.shape[2]
        done = 0
        while done < value.shape[0]:
            piece, inner = divmod(start_row + done, q)
            n = min(q - inner, value.shape[0] - done)
            ref[piece // n_xy, piece % n_xy, inner : inner + n, :] = value[done : done + n].astype(BF)
            done += n

    def put_terms(ref, listed):
        where = 0
        for acc, C, O in listed:
            chunks = 2 if O == 64 else 3
            for k in range(chunks):
                put(ref, where, acc[0 : 3 * C, k * LANES : (k + 1) * LANES])
                where += 3 * C
        for acc, C, O in listed:
            k = 0 if O == 64 else 1
            put(ref, where, acc[3 * C : 3 * C + ONES, k * LANES : (k + 1) * LANES])
            where += ONES
        pieces = ref.shape[0] * ref.shape[1] * ref.shape[2]
        put(ref, where, jnp.zeros((pieces - where, LANES), BF))

    brought[0].wait()
    rows_first(R.near[0], R.fields)
    send_forward(FIELDS, R.fields, 16, 128, 4, 64)
    pl.semaphore_wait(barrier, 6 + (n_xy - 1) + 2 * (n_z - 1))
    for copy in code_copies:
        copy.start()
    start(FIELDS)

    for copy in brought[1:]:
        copy.wait()
    forward_weights(0)
    cot = R.cot
    rows_first(R.near[1], cot)
    backward_weights(3)
    spread_delta(cot, 16, 64, 3, R.d[3])
    G4 = R.g[3]

    def write_g4(r, v):
        G4[r] = v

    conv(R.d[3], 192, R.kt[3], dil[3], 24, write_g4)
    columns = [column(i) for i in range(4)]

    for copy in code_copies:
        copy.wait_recv()
    pad_and_shift(FIELDS, R.fields, 16, 4, 64, 0, R.x[0], (0, 64, 128), False)
    first_act, slope1 = R.first_act, R.slope1

    def write_first(r, v):
        act, slope = gelu_and_slope(v + columns[0])
        first_act[r] = act.astype(BF)
        slope1[r] = slope

    conv(R.x[0], 192, R.kf[0], dil[0], 16, write_first)
    pooled = R.pooled
    u, w = iota((2 * LANES, LANES), 0), iota((2 * LANES, LANES), 1)
    quarter = jnp.where(((u & (LANES - 1)) >> 1) == w, 0.25, 0.0).astype(BF)
    for g in range(2):
        lhs = cat(
            [
                jnp.concatenate([first_act[8 * g + 2 * q], first_act[8 * g + 2 * q + 1]], axis=1)
                for q in range(4)
            ],
            0,
        )
        pooled[4 * g : 4 * g + 4] = mm(lhs, quarter).astype(BF).reshape(4, 64, LANES)
    send_forward(POOLED, pooled, 8, 64, 4, 64)
    start(POOLED)
    send_forward(FIRST, first_act, 16, 128, 4, 64)
    rims4 = rims_of(cot, 16, 128, 64, 3, R.kt[3])
    G4c = R.g4c
    pool = onehot(((u & (LANES - 1)) >> 1) == w)
    for g in range(3):
        pairs = [G4[8 * g + 2 * q, 0:128, :] + G4[8 * g + 2 * q + 1, 0:128, :] for q in range(4)]
        y = mm(split(cat(pairs, 0)), pool)
        G4c[4 * g : 4 * g + 4] = y.reshape(4, 128, LANES)
    send_backward(BACK4C, rims4[0:128], G4c, 0, 128, 8, 2, True)
    send_backward(BACK4F, rims4[128:192], G4, 128, 64, 16, 4)
    forward_weights(1)


    pad_and_shift(POOLED, pooled, 8, 4, 64, 1, R.x[1], (0, 64, 128), False)
    start(FIRST)
    start(BACK4C)
    second_act, slope2 = R.second_act, R.slope2
    inside = iota((1, LANES), 1) < 64

    def write_second(r, v):
        act, slope = gelu_and_slope(v + columns[1])
        second_act[r] = jnp.where(inside, act, 0.0).astype(BF)
        slope2[r] = jnp.where(inside, slope, 0.0)

    conv(R.x[1], 192, R.kf[1], dil[1], 8, write_second)
    send_forward(SECOND, second_act, 8, 64, 4, 128)
    start(SECOND)
    for i in (2, 3):
        forward_weights(i)
    for i in (2, 1, 0):
        backward_weights(i)

    arrive(BACK4C)
    coarse, skip = R.coarse, R.skip

    def write_coarse(r, v):
        coarse[r] = v

    def write_skip(r, v):
        skip[r] = v

    fold(BACK4C, G4c, 0, 128, 8, 64, 2, write_coarse)


    pad_and_shift(FIRST, first_act, 16, 4, 64, 3, R.x[3], (128, 320, 512), False)

    pad_and_shift(SECOND, second_act, 8, 4, 128, 2, R.x[2], (0, 128, 256), False)
    start(BACK4F)
    third_act, delta3 = R.third_act, R.delta3

    def write_third(r, v):
        act, slope = gelu_and_slope(v + columns[2])
        third_act[r] = jnp.where(inside, act, 0.0).astype(BF)
        delta3[r] = jnp.where(inside, coarse[r] * slope, 0.0).astype(BF)

    conv(R.x[2], 384, R.kf[2], dil[2], 8, write_third)
    send_forward(THIRD, third_act, 8, 64, 2, 128)
    start(THIRD)
    spread_delta(delta3, 8, 128, 2, R.d[2])
    G3 = R.g[2]

    def write_g3(r, v):
        G3[r] = v

    conv(R.d[2], 384, R.kt[2], dil[2], 4, write_g3)
    conv(R.d[2], 384, R.kt[2], dil[2], 4, write_g3, 12)
    send_backward(BACK3, rims_of(delta3, 8, 64, 128, 2, R.kt[2]), G3, 0, 128, 8, 4)
    start(BACK3)
    conv(R.d[2], 384, R.kt[2], dil[2], 8, write_g3, 4)


    weight_terms(R.x[2], 128, R.d[2], 128, dil[2], 16, R.w[2])
    arrive(BACK4F)
    fold(BACK4F, G4, 128, 64, 16, 128, 4, write_skip)
    pad_and_shift(THIRD, third_act, 8, 2, 128, 3, R.x[3], (0, 192, 384), True)

    weight_terms(R.x[3], 192, R.d[3], 64, dil[3], 24, R.w[3])
    put_terms(R.pay[0], ((R.w[3], 192, 64), (R.w[2], 128, 128)))
    sum_a.first()
    arrive(BACK3)
    delta2 = R.delta2

    def write_delta2(r, v):
        delta2[r] = (v * slope2[r]).astype(BF)

    fold(BACK3, G3, 0, 128, 8, 64, 4, write_delta2)
    spread_delta(delta2, 8, 128, 1, R.d[1])
    G2 = R.g[1]

    def write_g2(r, v):
        G2[r] = v

    conv(R.d[1], 384, R.kt[1], dil[1], 4, write_g2)
    conv(R.d[1], 384, R.kt[1], dil[1], 4, write_g2, 12)
    send_backward(BACK2, rims_of(delta2, 8, 64, 128, 1, R.kt[1]), G2, 0, 64, 8, 4)
    start(BACK2)
    conv(R.d[1], 384, R.kt[1], dil[1], 8, write_g2, 4)

    state = R.state

    def write_state(r, v):
        state[r] = (v + columns[3]).astype(BF)


    weight_terms(R.x[1], 64, R.d[1], 128, dil[1], 16, R.w[1])
    put_terms(R.pay[2], ((R.w[1], 64, 128),))
    sum_c.first()
    sum_a.second()
    conv(R.x[3], 576, R.kf[3], dil[3], 8, write_state)
    sum_c.second()
    arrive(BACK2)
    delta1 = R.delta1
    repeat = jnp.where((u & (LANES - 1)) == (w >> 1), 0.25, 0.0).astype(BF)

    def write_delta1(r, v):
        wide = mm(split(v), repeat)
        for z in range(2):
            delta1[2 * r + z] = ((skip[2 * r + z] + wide) * slope1[2 * r + z]).astype(BF)

    fold(BACK2, G2, 0, 64, 8, 64, 4, write_delta1)
    spread_delta(delta1, 16, 64, 0, R.d[0])
    weight_terms(R.x[0], 64, R.d[0], 64, dil[0], 24, R.w[0])
    put_terms(R.pay[1], ((R.w[0], 64, 64),))
    sum_b.first()
    G1 = R.g[0]

    def write_g1(r, v):
        G1[r] = v

    conv(R.d[0], 192, R.kt[0], dil[0], 4, write_g1)
    conv(R.d[0], 192, R.kt[0], dil[0], 4, write_g1, 20)
    send_backward(BACK1, rims_of(delta1, 16, 128, 64, 0, R.kt[0]), G1, 0, 64, 16, 4)
    start(BACK1)
    sum_a.third()
    conv(R.d[0], 192, R.kt[0], dil[0], 16, write_g1, 4)
    sum_c.third()
    sum_b.second()
    conv(R.x[3], 576, R.kf[3], dil[3], 8, write_state, 8)
    sum_a.fourth()
    arrive(BACK1)
    grad = R.grad

    def write_grad(r, v):
        grad[r] = v

    fold(BACK1, G1, 0, 64, 16, 128, 4, write_grad)
    sum_b.third()
    sum_c.fourth()
    sum_a.fifth()
    sum_b.fourth()
    sum_a.sixth()

    sum_a.finish()
    sum_b.finish()
    sum_c.finish()
    for listed in (*copies, code_copies):
        for copy in listed:
            copy.wait_send()


PIECE = (80, 32, 48)


def run_net(tiles, members, scale, operands):
    V, D = pltpu.VMEM, pltpu.SemaphoreType.DMA
    n_xy, n_z = tiles // 8, members * 4
    sizes = [(C, O, H + 2 * RIM) for C, O, H, _ in LAYERS]
    scratch = Refs(
        shifts=V((4, 256, 256), BF),
        picks=V((3, LANES, LANES), BF),
        x=[V((P_, 3 * C + ONES, LANES), BF) for C, O, P_ in sizes],
        d=[V((P_ + 2 * RIM, 3 * O, LANES), BF) for C, O, P_ in sizes],
        g=[V((P_, C, LANES), F32) for C, O, P_ in sizes],
        g4c=V((12, 128, LANES), F32),
        near=[V(v.shape, BF) for v in operands["far"]],
        k=[V(v.shape, BF) for v in operands["k_far"]],
        bring=D((6,)),
        kf=[V((O, 9 * C), BF) for C, O, _ in sizes],
        kt=[V((C, 9 * O), BF) for C, O, _ in sizes],
        w=[V((3 * C + ONES, 256 if O == 64 else 384), F32) for C, O, _ in sizes],
        fields=V((16, 64, LANES), BF),
        cot=V((16, 64, LANES), BF),
        first_act=V((16, 64, LANES), BF),
        slope1=V((16, 64, LANES), F32),
        pooled=V((8, 64, LANES), BF),
        second_act=V((8, 128, LANES), BF),
        slope2=V((8, 128, LANES), F32),
        third_act=V((8, 128, LANES), BF),
        coarse=V((8, 128, LANES), F32),
        skip=V((16, 64, LANES), F32),
        delta1=V((16, 64, LANES), BF),
        delta2=V((8, 128, LANES), BF),
        delta3=V((8, 128, LANES), BF),
        code_rows=V((8, LANES), jnp.int32),
        code_near=V((2, 8, LANES), jnp.int32),
        send=D((len(EXCHANGES), 8)),
        recv=D((len(EXCHANGES), 8)),
        send_code=D((2,)),
        recv_code=D((2,)),
        pay=[V((1 if i else 2, n_xy, q, LANES), BF) for i, q in enumerate(PIECE)],
        others=[V((n_xy, PIECE[0], LANES), BF)],
        half=[V((n_xy, PIECE[0], LANES), BF)],
        bxy=[V((n_xy, q, LANES), BF) for q in PIECE],
        bz=[V((n_z * (2 if i else 1), q, LANES), BF) for i, q in enumerate(PIECE)],
        psem=[D((4,))],
        xysem=[D((4, n_xy)) for q in PIECE],
        zsem=[D((2, n_z * (2 if i else 1))) for i, q in enumerate(PIECE)],
        cs=[V((sent, C * m * H // LANES, LANES), BF) for C, m, H, sent in EXCHANGES],
        rs=[V((2, m * H // 16, C, LANES), BF) for C, m, H, sent in EXCHANGES],
        cr=[V((6, C * m * H // LANES, LANES), BF) for C, m, H, sent in EXCHANGES],
        rr=[V((2, m * H // 16, C, LANES), BF) for C, m, H, sent in EXCHANGES],
    )
    smem = pl.BlockSpec(memory_space=pltpu.SMEM)
    vmem = pl.BlockSpec(memory_space=pltpu.VMEM)
    shape = jax.ShapeDtypeStruct
    outputs = Refs(
        state=shape((16, 64, LANES), BF),
        grad=shape((16, 64, LANES), F32),
        res=[shape((1 if i else 2, n_xy, q, LANES), BF) for i, q in enumerate(PIECE)],
    )
    inputs = Refs(**operands)
    flat_in, flat_out, flat_scratch = (list(flatten(part)) for part in (inputs, outputs, scratch))
    return pl.pallas_call(
        functools.partial(net_kernel, tiles, members, scale, (inputs, outputs, scratch)),
        out_shape=tuple(flat_out),
        in_specs=[
            smem if v.dtype == jnp.int32 else vmem if v.dtype == F32 else pl.BlockSpec(memory_space=pl.ANY)
            for v in flat_in
        ],
        out_specs=(vmem,) * len(flat_out),
        scratch_shapes=flat_scratch,
        compiler_params=pltpu.CompilerParams(
            collective_id=0, has_side_effects=True, vmem_limit_bytes=56 * 2**20
        ),
    )(*flat_in)

def finish_kernel(state, grad, early, late, middle, state_out, grad_out, w1, w2, w3, w4, b1, b2, b3, b4):
    channels_first(state, state_out, 1)
    channels_first(grad, grad_out, 2)
    take_terms(early, ((w4, b4, 192, 64), (w3, b3, 128, 128)))
    take_terms(late, ((w1, b1, 64, 64),))
    take_terms(middle, ((w2, b2, 64, 128),))


def run_finish(raw):
    vmem = pl.BlockSpec(memory_space=pltpu.VMEM)
    shape = jax.ShapeDtypeStruct
    outputs = [shape((64, 16, LANES), BF), shape((64, 16, LANES), F32)]
    outputs += [shape((9, C, O) if O > C else (9, O, C), F32) for C, O, _, _ in LAYERS]
    outputs += [shape((1, O), F32) for C, O, _, _ in LAYERS]
    return pl.pallas_call(
        finish_kernel,
        out_shape=tuple(outputs),
        in_specs=[vmem] * len(raw),
        out_specs=(vmem,) * len(outputs),
        compiler_params=pltpu.CompilerParams(vmem_limit_bytes=56 * 2**20),
    )(*raw)


def shards(tiles, members, fields, cotangent, k1, k2, k3, k4, off1, off2, off3, off4, codes, dilations):
    operands = dict(
        codes=codes,
        dil=dilations,
        far=[fields[0, 0], cotangent[0, 0]],
        k_far=[k1, jnp.swapaxes(k2, 1, 2), k3, k4],
        off=[off1[None, :], off2[None, :], off3[None, :], off4[None, :]],
    )
    scale = 1.0 / math.sqrt(members * tiles * fields.shape[3] * fields.shape[4])
    state, grad, *rest = run_finish(run_net(tiles, members, scale, operands))
    rest[1] = jnp.swapaxes(rest[1], 1, 2)
    return (state[None, None], grad[None, None], *rest[:4], *[b[0] for b in rest[4:]])


def solution(mesh):
    big = P("ens", "tile", None, None, None)
    in_specs = (big, big) + (P(),) * 8 + (P("tile", None), P())
    out_specs = (big, big) + (P(),) * 8
    body = functools.partial(shards, mesh.shape["tile"], mesh.shape["ens"])
    return jax.shard_map(body, mesh=mesh, in_specs=in_specs, out_specs=out_specs, check_vma=False)
```
